32 devices in a mesh: dp: 16 (over z, y, x), tensor: 2 (over core).
Axes of the slice: x: 2, y: 2, z: 4, core: 2. Of those that a mesh axis runs over, the one named last changes fastest.
Arguments:
- inputs: bfloat16 [12288, 2048], P(('dp', 'tensor')), may hold values from -6 to 6
- cotangent: bfloat16 [12288, 2048], P(('dp', 'tensor')), may hold values from -6 to 6
- seq_lengths: int32 [16, 5], P('dp'), may hold values from 0 to 768, as said below
- attn_gain: bfloat16 [2048], P('dp'), may hold values from 0.25 to 1.75
- w_query: bfloat16 [2048, 2048], P('dp', 'tensor'), may hold values from -0.125 to 0.125
- w_key: bfloat16 [2048, 256], P('dp', 'tensor'), may hold values from -0.125 to 0.125
- w_value: bfloat16 [2048, 256], P('dp', 'tensor'), may hold values from -0.125 to 0.125
- w_out: bfloat16 [2048, 2048], P('tensor', 'dp'), may hold values from -1 to 1
- mlp_gain: bfloat16 [2048], P('dp'), may hold values from 0.25 to 1.75
- w_gate: bfloat16 [2048, 5632], P('dp', 'tensor'), may hold values from -0.125 to 0.125
- w_up: bfloat16 [2048, 5632], P('dp', 'tensor'), may hold values from -0.125 to 0.125
- w_down: bfloat16 [5632, 2048], P('tensor', 'dp'), may hold values from -0.078125 to 0.078125
Outputs:
- output: bfloat16 [12288, 2048], P(('dp', 'tensor'))
- grad_inputs: float32 [12288, 2048], P(('dp', 'tensor'))
- grad_attn_gain: float32 [2048], P('dp')
- grad_w_query: float32 [2048, 2048], P('dp', 'tensor')
- grad_w_key: float32 [2048, 256], P('dp', 'tensor')
- grad_w_value: float32 [2048, 256], P('dp', 'tensor')
- grad_w_out: float32 [2048, 2048], P('tensor', 'dp')
- grad_mlp_gain: float32 [2048], P('dp')
- grad_w_gate: float32 [2048, 5632], P('dp', 'tensor')
- grad_w_up: float32 [2048, 5632], P('dp', 'tensor')
- grad_w_down: float32 [5632, 2048], P('tensor', 'dp')
The draws below stay inside these ranges and needn't reach their ends.
Inputs may be any that keep to these rules, and one draw needn't show every extreme that they name: `seq_lengths`: row g lists the lengths of the sequences of index g of dp in order, nonzero ones first, zeros for unused slots; their blocks, ceil(length / 128) each, number more than 3 and at most 6; in every row some sequence holds rows on both sides of row 384; one sequence in every draw has length 768.
All inputs are finite; a program needn't handle non-finite values.
Results may differ from the reference program's by a relative error of at most 0.015.
Values may be sent and summed in bfloat16 or wider, within the bound.
No kernel may reach another device: no remote copies, remote signals or barrier semaphores. Data moves between devices by JAX's collectives and lax.ppermute only.
A program may use at most 256 MiB of HBM per device.

```python
import jax
import jax.numpy as jnp
from jax import lax

D = 2048
HEADS = 32
KV_HEADS = 4
HEAD_DIM = 64
FF = 5632
BLOCK = 128
BLK_GRP = 6
SEQ_GRP = 5
ROWS = 12288
N_DP = 16


def draw_seq_lengths(key, part):
    key = jax.random.fold_in(key, 11)
    key_fill, key_cut, key_trim, key_pick = jax.random.split(key, 4)
    groups = N_DP
    blocks = BLK_GRP
    filled = jax.random.randint(key_fill, (groups,), blocks // 2 + 1, blocks + 1)
    chosen = jax.random.randint(key_pick, (), 0, groups)
    group_ids = jnp.arange(groups, dtype=jnp.int32)
    is_chosen = group_ids == chosen
    filled = jnp.where(is_chosen, blocks, filled)
    cut_bits = jax.random.randint(key_cut, (groups, blocks), 0, 2)
    block_ids = jnp.arange(blocks, dtype=jnp.int32)
    opens = (block_ids[None, :] == 0) | (cut_bits == 1) & (block_ids[None, :] != blocks // 2) & ~is_chosen[:, None]
    used = block_ids[None, :] < filled[:, None]
    opens = opens & used
    seq_index = jnp.cumsum(opens.astype(jnp.int32), axis=1) - 1
    slot_ids = jnp.arange(SEQ_GRP, dtype=jnp.int32)
    owner = (seq_index[:, :, None] == slot_ids[None, None, :]) & used[:, :, None]
    block_count = jnp.sum(owner.astype(jnp.int32), axis=1)
    trims = jax.random.randint(key_trim, (groups, SEQ_GRP), 0, BLOCK)
    trims = jnp.where(is_chosen[:, None], 0, trims)
    lengths = jnp.where(block_count > 0, block_count * BLOCK - trims, 0)
    return lengths.astype(jnp.int32)


def spiked(result, key, source, target, blocks, factor):
    owner, partner = [(jnp.arange(result.shape[dim]) // (result.shape[dim] // blocks)).reshape([-1 if axis == dim else 1 for axis in range(result.ndim)]) for dim in (source, target)]
    chosen = jax.random.permutation(key, blocks)[partner]
    strong = (owner == chosen) | (owner == (partner + blocks // 2) % blocks)
    return jnp.where(strong, factor * result, result)


def shard_levels(own_key, dims, cuts, low, top_value):
    def one(dim, parts):
        draws = jax.random.uniform(jax.random.fold_in(jax.random.fold_in(own_key, 6), dim), (parts,), jnp.float32, low / len(cuts), top_value / len(cuts))
        return jnp.repeat(jnp.exp(draws), dims[dim] // parts).reshape((-1,) + (1,) * (len(dims) - dim - 1))

    gain = one(*cuts[0])
    for cut in cuts[1:]:
        gain = gain * one(*cut)
    return gain


def centred(own_key, dims, spread, bound, pieces=(), kind=jnp.bfloat16):
    loudness = shard_levels(own_key, dims, pieces, -0.22, 0.18) if pieces else 1.0
    array = jax.random.normal(own_key, dims, jnp.float32) * spread * loudness
    return jnp.minimum(jnp.maximum(array, -bound), bound).astype(kind)


def noise_with(rng, dims, scale, most, pieces, heavy, held_as=jnp.bfloat16):
    result = scale * jax.random.normal(rng, dims, jnp.float32)
    if pieces:
        result = result * shard_levels(rng, dims, pieces, -0.22, 0.18)
    return jnp.clip(spiked(result, jax.random.fold_in(rng, 3), *heavy), -most, most).astype(held_as)


def setup_inputs(seed: int = 0) -> dict:
    splits = jax.random.split(jax.random.key(seed), 13)
    inputs = noise_with(splits[0], (ROWS, D), 1.0, 6.0, ((0, 32),), (0, 1, 32, 2.75))
    cotangent = noise_with(splits[1], (ROWS, D), 1.0, 6.0, ((0, 32),), (0, 1, 32, 2.75))
    seq_lengths = draw_seq_lengths(jax.random.fold_in(splits[12], 71), 0)
    attn_gain = jnp.clip(1.0 + 0.15 * jax.random.normal(splits[3], (D,), jnp.float32), 0.25, 1.75).astype(jnp.bfloat16)
    w_query = centred(splits[4], (D, HEADS * HEAD_DIM), D ** -0.5, 0.125, ((0, 16), (1, 2)))
    w_key = centred(splits[5], (D, KV_HEADS * HEAD_DIM), D ** -0.5, 0.125, ((0, 16), (1, 2)))
    w_value = centred(splits[6], (D, KV_HEADS * HEAD_DIM), D ** -0.5, 0.125, ((0, 16), (1, 2)))
    w_out = centred(splits[7], (HEADS * HEAD_DIM, D), (max(HEADS * HEAD_DIM // 64, 16)) ** -0.5, 1.0, ((0, 2), (1, 16)))
    mlp_gain = jnp.clip(1.0 + 0.15 * jax.random.normal(splits[8], (D,), jnp.float32), 0.25, 1.75).astype(jnp.bfloat16)
    w_gate = centred(splits[9], (D, FF), D ** -0.5, 0.125, ((0, 16), (1, 2)))
    w_up = centred(splits[10], (D, FF), D ** -0.5, 0.125, ((0, 16), (1, 2)))
    w_down = centred(splits[11], (FF, D), FF ** -0.5, 0.078125, ((0, 2), (1, 16)))
    return dict(inputs=inputs, cotangent=cotangent, seq_lengths=seq_lengths, attn_gain=attn_gain, w_query=w_query, w_key=w_key, w_value=w_value, w_out=w_out, mlp_gain=mlp_gain, w_gate=w_gate, w_up=w_up, w_down=w_down)


norm_epsilon = 1e-05
rope_base = 10000.0
masked_score = -1e+30
exact_mode = lax.Precision.HIGHEST

@jax.custom_vjp
def low(v):
    return lax.optimization_barrier(v.astype(jnp.bfloat16)).astype(jnp.float32)

@jax.custom_vjp
def low_back(v):
    return v

def low_keep(v):
    return (low(v), None)

def low_pass(kept, grad):
    return (grad,)

def back_keep(v):
    return (v, None)

def back_low(kept, grad):
    return (low(grad),)
low.defvjp(low_keep, low_pass)
low_back.defvjp(back_keep, back_low)

def build_layout(lengths, total_rows):
    block_counts = (lengths + BLOCK - 1) // BLOCK
    seq_ends = jnp.cumsum(block_counts, dtype=jnp.int32) * BLOCK
    seq_starts = seq_ends - block_counts * BLOCK
    row_ids = jnp.arange(total_rows, dtype=jnp.int32)
    membership = ((row_ids[:, None] >= seq_starts[None, :]) & (row_ids[:, None] < seq_ends[None, :])).astype(jnp.int32)
    slot_ids = jnp.arange(lengths.shape[0], dtype=jnp.int32)
    segment = lax.optimization_barrier(jnp.sum(membership * (slot_ids[None, :] + 1), axis=1, dtype=jnp.int32)) - 1
    first_row = lax.optimization_barrier(jnp.sum(membership * seq_starts[None, :], axis=1, dtype=jnp.int32))
    seq_limit = lax.optimization_barrier(jnp.sum(membership * lengths[None, :], axis=1, dtype=jnp.int32))
    position = row_ids - first_row
    is_valid = (segment >= 0) & (position < seq_limit)
    allowed = (segment[:, None] == segment[None, :]) & (segment[:, None] >= 0) & (position[None, :] <= position[:, None]) & is_valid[None, :]
    allowed = allowed | (row_ids[:, None] == row_ids[None, :])
    return (position, is_valid, allowed)

def group_layout(lengths):
    return build_layout(lengths, BLK_GRP * BLOCK)

def rotate_heads(values, position, direction):
    row_count = values.shape[0]
    head_count = values.shape[1] // HEAD_DIM
    half_dim = HEAD_DIM // 2
    frequency = rope_base ** (-2.0 * jnp.arange(half_dim, dtype=jnp.float32) / HEAD_DIM)
    angles = position.astype(jnp.float32)[:, None] * frequency[None, :]
    cosine = jnp.cos(angles)[:, None, :]
    sine_part = direction * jnp.sin(angles)[:, None, :]
    shaped = values.reshape(row_count, head_count, 2, half_dim)
    first_half = shaped[:, :, 0, :]
    second_half = shaped[:, :, 1, :]
    turned = jnp.stack([first_half * cosine - second_half * sine_part, second_half * cosine + first_half * sine_part], axis=2)
    return turned.reshape(row_count, head_count * HEAD_DIM)

def matmul(left, right):
    return jnp.dot(left, right, precision=exact_mode)

def rms_scale(values):
    return lax.rsqrt(lax.optimization_barrier(jnp.mean(values * values, axis=-1, keepdims=True)) + norm_epsilon)

def attend(queries, key_rows, values, allowed):
    row_count = queries.shape[0]
    per_group = HEADS // KV_HEADS
    query_heads = queries.reshape(row_count, KV_HEADS, per_group, HEAD_DIM)
    key_heads = key_rows.reshape(row_count, KV_HEADS, HEAD_DIM)
    value_heads = values.reshape(row_count, KV_HEADS, HEAD_DIM)
    scores = jnp.einsum('qgzd,kgd->gzqk', query_heads, key_heads, precision=exact_mode) * HEAD_DIM ** (-0.5)
    scores = low_back(scores)
    scores = jnp.where(allowed[None, None], scores, masked_score)
    row_max = lax.optimization_barrier(jnp.max(scores, axis=-1, keepdims=True))
    weights = jnp.exp(scores - row_max)
    weights = weights / lax.optimization_barrier(jnp.sum(weights, axis=-1, keepdims=True))
    mixed = jnp.einsum('gzqk,kgd->qgzd', low(weights), value_heads, precision=exact_mode)
    return mixed.reshape(row_count, HEADS * HEAD_DIM)

def group_layer(params, data):
    attn_gain, w_query, w_key, w_value, w_out, mlp_gain, w_gate, w_up, w_down = params
    inputs, position, is_valid, allowed = data
    normed = low(inputs * rms_scale(inputs) * attn_gain)
    queries = low(rotate_heads(low_back(matmul(normed, w_query)), position, 1.0))
    key_rows = low(rotate_heads(low_back(matmul(normed, w_key)), position, 1.0))
    values = low(low_back(matmul(normed, w_value)))
    mixed = low(low_back(attend(queries, key_rows, values, allowed)))
    residual = inputs + low_back(matmul(mixed, w_out))
    normed_mlp = low(residual * rms_scale(residual) * mlp_gain)
    gate_act = low_back(matmul(normed_mlp, w_gate))
    up_act = low_back(matmul(normed_mlp, w_up))
    hidden = low(jax.nn.silu(gate_act) * up_act)
    branch = low_back(matmul(hidden, w_down))
    return jnp.where(is_valid[:, None], residual + branch, 0.0)

def reference(inputs, cotangent, seq_lengths, attn_gain, w_query, w_key, w_value, w_out, mlp_gain, w_gate, w_up, w_down):
    group_rows = BLK_GRP * BLOCK
    position, is_valid, allowed = jax.vmap(group_layout)(seq_lengths)
    params = tuple((weight_arg.astype(jnp.float32) for weight_arg in (attn_gain, w_query, w_key, w_value, w_out, mlp_gain, w_gate, w_up, w_down)))
    grouped = inputs.astype(jnp.float32).reshape(N_DP, group_rows, D)

    def forward(grouped_rows, weight_set):

        def one_group(data):
            return jax.checkpoint(group_layer)(weight_set, data)
        return lax.map(one_group, (grouped_rows, position, is_valid, allowed))
    output, pullback = jax.vjp(forward, grouped, params)
    grad_rows, grad_params = pullback(cotangent.astype(jnp.float32).reshape(N_DP, group_rows, D))
    return (output.reshape(ROWS, D).astype(jnp.bfloat16), grad_rows.reshape(ROWS, D), grad_params[0], grad_params[1], grad_params[2], grad_params[3], grad_params[4], grad_params[5], grad_params[6], grad_params[7], grad_params[8])
```

```python
import functools

import jax
import jax.numpy as jnp
from jax import lax
from jax.experimental import pallas as pl
from jax.experimental.layout import Layout, with_layout_constraint
from jax.experimental.pallas import tpu as pltpu
from jax.sharding import PartitionSpec as P

HEAD_DIM = 64
BLOCK = 128
LANES = 128

norm_epsilon = 1e-05
rope_base = 10000.0
masked_score = -1e30

bf16 = jnp.bfloat16
f32 = jnp.float32

X, Y, T, Z = 0, 1, 2, 3


def nbits():
    return lax.axis_size("dp").bit_length() - 1


def block_axes():
    return [T] + list(range(nbits() - 1, Z - 1, -1)) + [Y, X]


def rest_bits():
    return list(range(Z, nbits()))


def exchange(values, bit):
    size = lax.axis_size("dp")
    return lax.ppermute(values, "dp", [(i, i ^ (1 << bit)) for i in range(size)])


def core_exchange(values):
    return lax.ppermute(values, "tensor", [(0, 1), (1, 0)])


def as_block(values):
    return values.reshape((1,) * nbits() + values.shape)


def after(values, *others):
    return lax.optimization_barrier((values,) + others)[0] if others else values


def row_major(values):
    return with_layout_constraint(values, Layout(major_to_minor=tuple(range(values.ndim))))


def gather_step(values, bit, *others):
    came = exchange(after(values, *others), bit)
    return jnp.concatenate([values, came], axis=block_axes().index(bit)), came


def gather_bits(values, bits):
    for bit in bits:
        values, _ = gather_step(values, bit)
    return values


def scatter_step(values, bit, kind, *others):
    axis = block_axes().index(bit)
    kept = lax.slice_in_dim(values, 0, 1, axis=axis)
    sent = lax.slice_in_dim(values, 1, 2, axis=axis)
    came = exchange(row_major(after(sent.astype(bf16), *others)), bit)
    total = kept.astype(f32) + came.astype(f32)
    return row_major(total.astype(kind)), came


def flat(blocks):
    return blocks.reshape(-1, blocks.shape[-1])


def as_blocks(rows):
    return rows.reshape((2,) * nbits() + (rows.shape[0] // lax.axis_size("dp"), rows.shape[1]))


def block_mask(place):
    axes = block_axes()
    mask = 0
    for level, bit in enumerate(axes):
        mask |= ((place >> (len(axes) - 1 - level)) & 1) << bit
    return mask


def block_place(mask):
    axes = block_axes()
    place = 0
    for level, bit in enumerate(axes):
        place = place + (((mask >> bit) & 1) << (len(axes) - 1 - level))
    return place


def reorder_kernel(count, offsets, *refs):
    half = len(refs) // 2
    for source, target in zip(refs[:half], refs[half:]):
        for place in range(count):
            start = pl.multiple_of(offsets[place], LANES)
            target[:, place * LANES : (place + 1) * LANES] = source[:, pl.ds(start, LANES)]


def reorder(arrays, places):
    count = len(places)
    rows, columns = arrays[0].shape
    width = columns // count
    if width % LANES:
        return [
            jnp.concatenate(
                [lax.dynamic_slice_in_dim(v, p * width, width, 1) for p in places], axis=1
            )
            for v in arrays
        ]
    spec = pl.BlockSpec((BLOCK, columns), lambda i, offsets: (i, 0))
    return pl.pallas_call(
        functools.partial(reorder_kernel, count),
        grid_spec=pltpu.PrefetchScalarGridSpec(
            num_scalar_prefetch=1,
            grid=(rows // BLOCK,),
            in_specs=[spec] * len(arrays),
            out_specs=[spec] * len(arrays),
        ),
        out_shape=[jax.ShapeDtypeStruct(v.shape, v.dtype) for v in arrays],
        compiler_params=pltpu.CompilerParams(vmem_limit_bytes=32 * 1024 * 1024),
        cost_estimate=pl.CostEstimate(
            flops=0, bytes_accessed=sum(2 * v.size * v.dtype.itemsize for v in arrays), transcendentals=0
        ),
        name="reorder",
    )(jnp.stack(places).astype(jnp.int32) * width, *arrays)


def to_relative(*arrays):
    me = lax.axis_index("dp")
    return reorder(arrays, [me ^ block_mask(place) for place in range(lax.axis_size("dp"))])


def from_relative(*arrays):
    me = lax.axis_index("dp")
    return reorder(arrays, [block_place(me ^ index) for index in range(lax.axis_size("dp"))])


def swap_halves(values):
    half = values.shape[1] // 2
    return jnp.concatenate([values[:, half:], values[:, :half]], axis=1)


def pick_first(flag, first, second, axis):
    return jnp.concatenate(
        [jnp.where(flag, first, second), jnp.where(flag, second, first)], axis=axis
    )


def build_layout(lengths, total_rows):
    block_counts = (lengths + BLOCK - 1) // BLOCK
    seq_ends = jnp.cumsum(block_counts, dtype=jnp.int32) * BLOCK
    seq_starts = seq_ends - block_counts * BLOCK
    row_ids = jnp.arange(total_rows, dtype=jnp.int32)
    membership = (
        (row_ids[:, None] >= seq_starts[None, :]) & (row_ids[:, None] < seq_ends[None, :])
    ).astype(jnp.int32)
    slot_ids = jnp.arange(lengths.shape[0], dtype=jnp.int32)
    segment = jnp.sum(membership * (slot_ids[None, :] + 1), axis=1, dtype=jnp.int32) - 1
    first_row = jnp.sum(membership * seq_starts[None, :], axis=1, dtype=jnp.int32)
    seq_limit = jnp.sum(membership * lengths[None, :], axis=1, dtype=jnp.int32)
    position = row_ids - first_row
    is_valid = (segment >= 0) & (position < seq_limit)
    allowed = (
        (segment[:, None] == segment[None, :])
        & (segment[:, None] >= 0)
        & (position[:, None] <= position[None, :])
        & is_valid[:, None]
    )
    allowed = allowed | (row_ids[:, None] == row_ids[None, :])
    bias = jnp.where(allowed, 0.0, masked_score).astype(f32)
    return position, is_valid, bias


def rotation_tables(position):
    half_dim = HEAD_DIM // 2
    lane = jnp.arange(LANES, dtype=jnp.int32)
    frequency = rope_base ** (-2.0 * (lane % half_dim).astype(f32) / HEAD_DIM)
    angles = position.astype(f32)[:, None] * frequency[None, :]
    sign = jnp.where(lane % HEAD_DIM < half_dim, -1.0, 1.0).astype(f32)
    return jnp.cos(angles), jnp.sin(angles) * sign[None, :]


def matmul(left, right):
    return jnp.dot(left, right, preferred_element_type=f32)


def contract_rows(left, right):
    return lax.dot_general(left, right, (((0,), (0,)), ((), ())), preferred_element_type=f32)


def contract_cols(left, right):
    return lax.dot_general(left, right, (((1,), (1,)), ((), ())), preferred_element_type=f32)


def rms_scale(values):
    return lax.rsqrt(jnp.mean(values * values, axis=-1, keepdims=True) + norm_epsilon)


def norm_back(grad_normed, unit_rows, row_scale, gain):
    scaled = grad_normed * gain
    grad_gain = jnp.sum(grad_normed * unit_rows, axis=0)
    grad_rows = row_scale * (
        scaled - unit_rows * jnp.mean(scaled * unit_rows, axis=-1, keepdims=True)
    )
    return grad_gain, grad_rows


def turn(values, cosine, sine):
    lane = lax.broadcasted_iota(jnp.int32, values.shape, 1)
    half_dim = HEAD_DIM // 2
    partner = jnp.where(
        lane % HEAD_DIM < half_dim,
        pltpu.roll(values, LANES - half_dim, 1),
        pltpu.roll(values, half_dim, 1),
    )
    return values * cosine + partner * sine


def doubled(values, second):
    lane = lax.broadcasted_iota(jnp.int32, values.shape, 1)
    rolled = pltpu.roll(values, HEAD_DIM, 1)
    low = lane < HEAD_DIM
    return jnp.where(second, jnp.where(low, rolled, values), jnp.where(low, values, rolled))


def split_heads(pair):
    lane = lax.broadcasted_iota(jnp.int32, pair.shape, 1)
    zero = jnp.zeros_like(pair)
    return jnp.concatenate(
        [jnp.where(lane < HEAD_DIM, pair, zero), jnp.where(lane < HEAD_DIM, zero, pair)], axis=0
    )


def join_heads(wide):
    row = lax.broadcasted_iota(jnp.int32, (LANES, BLOCK), 0)
    return jnp.where(row < HEAD_DIM, wide[:, :BLOCK], wide[:, BLOCK:]).T


def forward_kernel(
    pairs_per_kv, q_ref, k_ref, v_ref, bias_ref, cos_ref, sin_ref,
    out_ref, turned_ref, keys_ref, values_ref, total_ref, k2, v2t,
):
    pair = pl.program_id(0)
    rows = q_ref.shape[0]
    cosine, sine = cos_ref[...], sin_ref[...]

    @pl.when(pair == 0)
    def _():
        keys_ref[...] = turn(k_ref[...], cosine, sine).astype(bf16)
        values_ref[...] = v_ref[...].astype(bf16)

    @pl.when(lax.rem(pair, pairs_per_kv) == 0)
    def _():
        second = pair >= pairs_per_kv
        k2[...] = doubled(keys_ref[...].astype(f32), second).astype(bf16)
        v2t[...] = doubled(values_ref[...].astype(f32), second).T.astype(bf16)

    turned_ref[...] = (turn(q_ref[...], cosine, sine) * HEAD_DIM ** (-0.5)).astype(bf16)
    for index in range(rows // BLOCK):
        span = (index + 1) * BLOCK
        here = slice(index * BLOCK, span)
        queries = split_heads(turned_ref[here, :])
        scores = lax.dot_general(
            k2[:span, :], queries, (((1,), (1,)), ((), ())), preferred_element_type=f32
        )
        bias = bias_ref[:span, here]
        scores = scores + jnp.concatenate([bias, bias], axis=1)
        top = jnp.max(scores, axis=0, keepdims=True)
        weights = jnp.exp(scores - top)
        total = jnp.sum(weights, axis=0, keepdims=True)
        weights = (weights * (1.0 / total)).astype(bf16)
        mixed = jnp.dot(v2t[:, :span], weights, preferred_element_type=f32)
        out_ref[here, :] = join_heads(mixed).astype(bf16)
        total_ref[:, 2 * index * BLOCK : 2 * span] = top + jnp.log(total)


def backward_kernel(
    pairs_per_kv, q_ref, k_ref, v_ref, grad_ref, bias_ref, cos_ref, sin_ref, total_ref,
    dq_ref, dk_ref, dv_ref, k2, k2t, v2, dk_sum, dv_sum, dk_first, dv_first,
):
    pair = pl.program_id(0)
    rows = q_ref.shape[0]
    cosine, sine = cos_ref[...], sin_ref[...]

    @pl.when(lax.rem(pair, pairs_per_kv) == 0)
    def _():
        second = pair >= pairs_per_kv
        keys = doubled(k_ref[...].astype(f32), second)
        k2[...] = keys.astype(bf16)
        k2t[...] = keys.T.astype(bf16)
        v2[...] = doubled(v_ref[...].astype(f32), second).astype(bf16)
        dk_sum[...] = jnp.zeros_like(dk_sum)
        dv_sum[...] = jnp.zeros_like(dv_sum)

    for index in range(rows // BLOCK):
        span = (index + 1) * BLOCK
        here = slice(index * BLOCK, span)
        queries = split_heads(q_ref[here, :])
        grads = split_heads(grad_ref[here, :])
        scores = lax.dot_general(
            k2[:span, :], queries, (((1,), (1,)), ((), ())), preferred_element_type=f32
        )
        bias = bias_ref[:span, here]
        scores = scores + jnp.concatenate([bias, bias], axis=1)
        probs = jnp.exp(scores - total_ref[:, 2 * index * BLOCK : 2 * span])
        grad_prob = lax.dot_general(
            v2[:span, :], grads, (((1,), (1,)), ((), ())), preferred_element_type=f32
        )
        center = jnp.sum(probs * grad_prob, axis=0, keepdims=True)
        grad_score = (probs * (grad_prob - center)).astype(bf16)
        dv_sum[:span, :] += jnp.dot(probs.astype(bf16), grads, preferred_element_type=f32)
        dk_sum[:span, :] += jnp.dot(grad_score, queries, preferred_element_type=f32)
        wide = jnp.dot(k2t[:, :span], grad_score, preferred_element_type=f32)
        grad_query = join_heads(wide) * HEAD_DIM ** (-0.5)
        dq_ref[here, :] = turn(grad_query, cosine[here, :], -sine[here, :]).astype(bf16)

    @pl.when(pair == pairs_per_kv - 1)
    def _():
        dk_first[...] = dk_sum[...] + pltpu.roll(dk_sum[...], HEAD_DIM, 1)
        dv_first[...] = dv_sum[...] + pltpu.roll(dv_sum[...], HEAD_DIM, 1)

    @pl.when(pair == pl.num_programs(0) - 1)
    def _():
        lane = lax.broadcasted_iota(jnp.int32, dk_first.shape, 1)
        low = lane < HEAD_DIM
        keys = jnp.where(low, dk_first[...], dk_sum[...] + pltpu.roll(dk_sum[...], HEAD_DIM, 1))
        dk_ref[...] = turn(keys, cosine, -sine).astype(bf16)
        dv_ref[...] = jnp.where(
            low, dv_first[...], dv_sum[...] + pltpu.roll(dv_sum[...], HEAD_DIM, 1)
        ).astype(bf16)


def attend_forward(raw, heads_width, bias, cosine, sine):
    rows = raw.shape[0]
    pairs = heads_width // LANES
    whole = lambda shape: pl.BlockSpec(shape, lambda i: (0, 0))
    column = pl.BlockSpec((rows, LANES), lambda i: (0, i))
    return pl.pallas_call(
        functools.partial(forward_kernel, pairs // 2),
        grid=(pairs,),
        in_specs=[
            column,
            pl.BlockSpec((rows, LANES), lambda i: (0, pairs)),
            pl.BlockSpec((rows, LANES), lambda i: (0, pairs + 1)),
            whole((rows, rows)),
            whole((rows, LANES)),
            whole((rows, LANES)),
        ],
        out_specs=[
            column,
            column,
            whole((rows, LANES)),
            whole((rows, LANES)),
            pl.BlockSpec((None, 1, 2 * rows), lambda i: (i, 0, 0)),
        ],
        out_shape=[
            jax.ShapeDtypeStruct((rows, heads_width), bf16),
            jax.ShapeDtypeStruct((rows, heads_width), bf16),
            jax.ShapeDtypeStruct((rows, LANES), bf16),
            jax.ShapeDtypeStruct((rows, LANES), bf16),
            jax.ShapeDtypeStruct((pairs, 1, 2 * rows), f32),
        ],
        scratch_shapes=[pltpu.VMEM((rows, LANES), bf16), pltpu.VMEM((LANES, rows), bf16)],
        compiler_params=pltpu.CompilerParams(vmem_limit_bytes=40 * 1024 * 1024),
        cost_estimate=pl.CostEstimate(
            flops=12 * rows * rows * heads_width,
            bytes_accessed=16 * rows * heads_width,
            transcendentals=rows * rows * heads_width // HEAD_DIM,
        ),
        name="attend_forward",
    )(raw, raw, raw, bias, cosine, sine)


def attend_backward(queries, keys, values, grads, bias, cosine, sine, totals):
    rows, heads_width = queries.shape
    pairs = heads_width // LANES
    whole = lambda shape: pl.BlockSpec(shape, lambda i: (0, 0))
    column = pl.BlockSpec((rows, LANES), lambda i: (0, i))
    return pl.pallas_call(
        functools.partial(backward_kernel, pairs // 2),
        grid=(pairs,),
        in_specs=[
            column,
            whole((rows, LANES)),
            whole((rows, LANES)),
            column,
            whole((rows, rows)),
            whole((rows, LANES)),
            whole((rows, LANES)),
            pl.BlockSpec((None, 1, 2 * rows), lambda i: (i, 0, 0)),
        ],
        out_specs=[column, whole((rows, LANES)), whole((rows, LANES))],
        out_shape=[
            jax.ShapeDtypeStruct((rows, heads_width), bf16),
            jax.ShapeDtypeStruct((rows, LANES), bf16),
            jax.ShapeDtypeStruct((rows, LANES), bf16),
        ],
        scratch_shapes=[
            pltpu.VMEM((rows, LANES), bf16),
            pltpu.VMEM((LANES, rows), bf16),
            pltpu.VMEM((rows, LANES), bf16),
            pltpu.VMEM((rows, LANES), f32),
            pltpu.VMEM((rows, LANES), f32),
            pltpu.VMEM((rows, LANES), f32),
            pltpu.VMEM((rows, LANES), f32),
        ],
        compiler_params=pltpu.CompilerParams(vmem_limit_bytes=40 * 1024 * 1024),
        cost_estimate=pl.CostEstimate(
            flops=30 * rows * rows * heads_width,
            bytes_accessed=16 * rows * heads_width,
            transcendentals=rows * rows * heads_width // HEAD_DIM,
        ),
        name="attend_backward",
    )(queries, keys, values, grads, bias, cosine, sine, totals)


def own_columns(weight):
    t = (lax.axis_index("dp") >> T) & 1
    half = weight.shape[1] // 2
    own = lax.dynamic_slice_in_dim(weight, t * half, half, 1)
    other = lax.dynamic_slice_in_dim(weight, (1 - t) * half, half, 1)
    return as_block(own), as_block(other)


def finish_kernel(turned, t_ref, own_ref, came_ref, out_ref):
    half = own_ref.shape[1]
    first = t_ref[0] == 0
    own = own_ref[...]
    came = came_ref[...].astype(f32)
    low, high = jnp.where(first, own, came), jnp.where(first, came, own)
    if turned:
        out_ref[:half, :] = low.T
        out_ref[half:, :] = high.T
    else:
        out_ref[:, :half] = low
        out_ref[:, half:] = high


def finish_columns(own, came, turned):
    rows, half = own.shape
    t = (lax.axis_index("dp") >> T) & 1
    shape = (2 * half, rows) if turned else (rows, 2 * half)
    if rows % LANES:
        joined = pick_first(t == 0, own, came.astype(f32), 1)
        return joined.T if turned else joined
    return pl.pallas_call(
        functools.partial(finish_kernel, turned),
        in_specs=[
            pl.BlockSpec(memory_space=pltpu.SMEM),
            pl.BlockSpec(memory_space=pltpu.VMEM),
            pl.BlockSpec(memory_space=pltpu.VMEM),
        ],
        out_specs=pl.BlockSpec(memory_space=pltpu.VMEM),
        out_shape=jax.ShapeDtypeStruct(shape, f32),
        compiler_params=pltpu.CompilerParams(vmem_limit_bytes=32 * 1024 * 1024),
        cost_estimate=pl.CostEstimate(
            flops=0, bytes_accessed=14 * rows * half, transcendentals=0
        ),
        name="finish_columns",
    )(t.reshape(1).astype(jnp.int32), own, came)


def body(
    inputs, cotangent, seq_lengths, attn_gain, w_query, w_key, w_value, w_out,
    mlp_gain, w_gate, w_up, w_down,
):
    own_rows = inputs.shape[0]
    core = lax.axis_index("tensor")
    rest = rest_bits()
    heads_width = w_query.shape[1]
    kv_width = w_key.shape[1]
    cut = (heads_width + 2 * kv_width) // 2
    cut_out = heads_width // 2

    def along(blocks, bits, *others):
        for bit in bits:
            blocks, came = gather_step(blocks, bit, *others)
            others = ()
        return blocks, came

    deep = rest + [T]
    out_t = w_out.T
    qa, qa_z = along(as_block(w_query[:, :cut]), deep)
    qb, qb_z = along(as_block(jnp.concatenate([w_query[:, cut:], w_key, w_value], axis=1)), deep)
    gains = flat(gather_bits(as_block(jnp.stack([attn_gain, mlp_gain])), deep + [X, Y]))
    gains = gains.reshape(-1, 2, attn_gain.shape[0]).transpose(1, 0, 2).reshape(2, -1).astype(f32)
    gain_one, gain_two = gains[0], gains[1]
    oa, oa_z = along(as_block(out_t[:, :cut_out]), deep, qa_z)
    ob, ob_z = along(as_block(out_t[:, cut_out:]), deep, qb_z)
    qa, qa_x = gather_step(qa, X)
    qb, qb_y = gather_step(qb, Y)
    qa, qa_y = gather_step(qa, Y)
    qb, qb_x = gather_step(qb, X)
    query_w = jnp.concatenate([flat(qa), flat(qb)], axis=1)

    def swapped(weight, *others):
        own, other = own_columns(weight)
        return jnp.concatenate([own, exchange(after(other, *others), T)], axis=0)

    gate, gate_z = along(swapped(w_gate, qa_z), rest, oa_z)
    up, up_z = along(swapped(w_up, qb_z), rest, ob_z)
    down, down_z = along(swapped(w_down.T, oa_z, ob_z), rest, gate_z)

    oa, oa_x = gather_step(oa, X, qa_x)
    ob, ob_y = gather_step(ob, Y, qb_y)
    oa, oa_y = gather_step(oa, Y, qa_y)
    ob, ob_x = gather_step(ob, X, qb_x)
    out_w = jnp.concatenate([flat(oa), flat(ob)], axis=1)

    gate, gate_x = gather_step(gate, X, oa_x, qb_x)
    up, up_y = gather_step(up, Y, ob_y, qa_y)
    gate, gate_y = gather_step(gate, Y, oa_y)
    up, up_x = gather_step(up, X, ob_x)
    gate_w, up_w = flat(gate), flat(up)
    cut_down = down.shape[-1] // 2 // LANES * LANES
    down_a, down_ax = gather_step(down[..., :cut_down], X, gate_x, ob_x)
    down_b, down_by = gather_step(down[..., cut_down:], Y, up_y, oa_y)
    down_a, _ = gather_step(down_a, Y, gate_y)
    down_b, _ = gather_step(down_b, X, up_x)
    down_w = jnp.concatenate([flat(down_a), flat(down_b)], axis=1)

    position, is_valid, bias = build_layout(seq_lengths[0], 2 * own_rows)
    cosine, sine = rotation_tables(position)
    own_valid = lax.dynamic_slice_in_dim(is_valid, core * own_rows, own_rows, 0)[:, None]

    inputs_rel, cotangent_rel = to_relative(inputs, cotangent)
    inputs_wide = inputs_rel.astype(f32)
    scale_one = rms_scale(inputs_wide)
    unit_one = inputs_wide * scale_one
    normed_own = (unit_one * gain_one).astype(bf16)
    normed = pick_first(core == 0, normed_own, core_exchange(normed_own), 0)
    raw = matmul(normed, query_w)
    mixed, queries, keys, values, totals = attend_forward(raw, heads_width, bias, cosine, sine)
    mixed_own = lax.dynamic_slice_in_dim(mixed, core * own_rows, own_rows, 0)
    mixed_other = lax.dynamic_slice_in_dim(mixed, (1 - core) * own_rows, own_rows, 0)
    came = core_exchange(contract_cols(mixed_other, out_w).astype(bf16))
    residual = inputs_wide + (contract_cols(mixed_own, out_w) + came.astype(f32))

    scale_two = rms_scale(residual)
    unit_two = residual * scale_two
    normed_mlp_own = (unit_two * gain_two).astype(bf16)
    far_own = exchange(swap_halves(normed_mlp_own), T)
    near = jnp.concatenate([normed_mlp_own, core_exchange(normed_mlp_own)], axis=0)
    far = jnp.concatenate([far_own, core_exchange(far_own)], axis=0)
    grad_branch_own = jnp.where(own_valid, cotangent_rel, jnp.zeros_like(cotangent_rel))
    grad_far_own = exchange(after(swap_halves(grad_branch_own), far_own), T)
    grad_near = jnp.concatenate([grad_branch_own, core_exchange(grad_branch_own)], axis=0)
    grad_far = jnp.concatenate([grad_far_own, core_exchange(grad_far_own)], axis=0)
    parts = []
    for rows, grads in ((near, grad_near), (far, grad_far)):
        gate_act = matmul(rows, gate_w)
        up_act = matmul(rows, up_w)
        sigmoid_gate = jax.nn.sigmoid(gate_act)
        hidden = (gate_act * sigmoid_gate * up_act).astype(bf16)
        parts.append((rows, grads, gate_act, up_act, sigmoid_gate, hidden))
    grad_branch = jnp.concatenate([grad_near, grad_far], axis=0)
    grad_down = contract_rows(
        grad_branch, jnp.concatenate([parts[0][5], parts[1][5]], axis=0)
    ).astype(bf16)
    grads_gate, grads_up = [], []
    for rows, grads, gate_act, up_act, sigmoid_gate, hidden in parts:
        grad_hidden = matmul(grads, down_w)
        grads_gate.append(
            (
                grad_hidden * up_act * sigmoid_gate * (1.0 + gate_act * (1.0 - sigmoid_gate))
            ).astype(bf16)
        )
        grads_up.append((grad_hidden * gate_act * sigmoid_gate).astype(bf16))

    def to_owners(near_part, far_part, *others):
        far_sum = far_part[:own_rows] + core_exchange(far_part[own_rows:].astype(bf16)).astype(f32)
        came = exchange(after(swap_halves(far_sum).astype(bf16), *others), T)
        other = core_exchange(near_part[own_rows:].astype(bf16))
        return near_part[:own_rows] + other.astype(f32) + came.astype(f32), came

    far_part = contract_cols(grads_gate[1], gate_w) + contract_cols(grads_up[1], up_w)
    near_part = contract_cols(grads_gate[0], gate_w) + contract_cols(grads_up[0], up_w)
    grad_normed_mlp, grad_z = to_owners(near_part, far_part)
    normed_mlp = jnp.concatenate([near, far], axis=0)
    grad_gate_w = contract_rows(normed_mlp, jnp.concatenate(grads_gate, axis=0)).astype(bf16)
    grad_up_w = contract_rows(normed_mlp, jnp.concatenate(grads_up, axis=0)).astype(bf16)
    branch, _ = to_owners(
        contract_cols(parts[0][5], down_w), contract_cols(parts[1][5], down_w), grad_z
    )
    output = jnp.where(own_valid, residual + branch, 0.0).astype(bf16)

    def back_along(blocks, bits, last_type, *others):
        for step, bit in enumerate(bits):
            kind = last_type if step == len(bits) - 1 else bf16
            blocks, came = scatter_step(blocks, bit, kind, *others)
            others = ()
        return blocks, came

    shallow = rest[::-1]
    down_blocks = as_blocks(grad_down)
    down_a, down_ay = scatter_step(down_blocks[..., :cut_down], Y, bf16)
    down_b, down_bx = scatter_step(down_blocks[..., cut_down:], X, bf16)
    down_a, down_ax = scatter_step(down_a, X, bf16)
    down_b, down_by = scatter_step(down_b, Y, bf16)
    down_sum, _ = back_along(jnp.concatenate([down_a, down_b], axis=-1), shallow, f32)
    gate_sum, gate_y = scatter_step(as_blocks(grad_gate_w), Y, bf16, down_ay)
    up_sum, up_x = scatter_step(as_blocks(grad_up_w), X, bf16, down_bx)
    gate_sum, gate_x = scatter_step(gate_sum, X, bf16, down_ax)
    up_sum, up_y = scatter_step(up_sum, Y, bf16, down_by)
    gate_sum, _ = back_along(gate_sum, shallow, f32, grad_z)
    up_sum, _ = back_along(up_sum, shallow, f32, grad_z)

    def finish(total, turned):
        own = flat(lax.slice_in_dim(total, 0, 1, axis=0))
        sent = lax.slice_in_dim(total, 1, 2, axis=0).astype(bf16)
        return finish_columns(own, flat(exchange(sent, T)), turned)

    sum_down, sum_gate, sum_up = finish(down_sum, True), finish(gate_sum, False), finish(up_sum, False)

    grad_gain_two, grad_norm_two = norm_back(grad_normed_mlp, unit_two, scale_two, gain_two)
    grad_residual = grad_branch_own.astype(f32) + grad_norm_two
    grad_att_own = grad_residual.astype(bf16)
    grad_attended = pick_first(core == 0, grad_att_own, core_exchange(grad_att_own), 0)
    grad_mixed = matmul(grad_attended, out_w).astype(bf16)
    grad_out_w = contract_rows(grad_attended, mixed).astype(bf16)
    out_blocks = as_blocks(grad_out_w)
    out_a, out_ay = scatter_step(out_blocks[..., :cut_out], Y, bf16, gate_y)
    out_b, out_bx = scatter_step(out_blocks[..., cut_out:], X, bf16, up_x)
    out_a, out_ax = scatter_step(out_a, X, bf16, gate_x)
    out_b, out_by = scatter_step(out_b, Y, bf16, up_y)
    deep_back = [T] + shallow
    out_a, _ = back_along(out_a, deep_back, f32)
    out_b, _ = back_along(out_b, deep_back, f32)
    sum_out = jnp.concatenate([flat(out_a), flat(out_b)], axis=1).T
    d_query, d_key, d_value = attend_backward(
        queries, keys, values, grad_mixed, bias, cosine, sine, totals
    )
    d_qkv = jnp.concatenate([d_query, d_key, d_value], axis=1)
    grad_qkv_w = as_blocks(contract_rows(normed, d_qkv).astype(bf16))
    sums = []
    for blocks, bits in ((grad_qkv_w[..., :cut], [Y, X]), (grad_qkv_w[..., cut:], [X, Y])):
        blocks, _ = back_along(blocks, bits + deep_back, f32)
        sums.append(flat(blocks))
    d_own = lax.dynamic_slice_in_dim(d_qkv, core * own_rows, own_rows, 0)
    d_other = lax.dynamic_slice_in_dim(d_qkv, (1 - core) * own_rows, own_rows, 0)
    came = core_exchange(contract_cols(d_other, query_w).astype(bf16))
    grad_normed = contract_cols(d_own, query_w) + came.astype(f32)
    grad_gain_one, grad_norm_one = norm_back(grad_normed, unit_one, scale_one, gain_one)
    grad_rows = grad_residual + grad_norm_one

    def sum_gain(grad):
        grad = grad + core_exchange(grad)
        blocks = as_blocks(grad.reshape(lax.axis_size("dp"), -1))
        for bit in [Y, X] + deep_back:
            axis = block_axes().index(bit)
            kept = lax.slice_in_dim(blocks, 0, 1, axis=axis)
            blocks = kept + exchange(lax.slice_in_dim(blocks, 1, 2, axis=axis), bit)
        return blocks.reshape(-1)

    return (
        from_relative(output)[0],
        from_relative(grad_rows)[0],
        sum_gain(grad_gain_one),
        jnp.concatenate([sums[0], sums[1][:, : heads_width - cut]], axis=1),
        sums[1][:, heads_width - cut : heads_width + kv_width - cut],
        sums[1][:, heads_width + kv_width - cut :],
        sum_out,
        sum_gain(grad_gain_two),
        sum_gate,
        sum_up,
        sum_down,
    )


def solution(mesh):
    placed = (
        P(("dp", "tensor"), None),
        P(("dp", "tensor"), None),
        P("dp", None),
        P("dp"),
        P("dp", "tensor"),
        P("dp", "tensor"),
        P("dp", "tensor"),
        P("tensor", "dp"),
        P("dp"),
        P("dp", "tensor"),
        P("dp", "tensor"),
        P("tensor", "dp"),
    )
    return jax.shard_map(
        body,
        mesh=mesh,
        in_specs=placed,
        out_specs=(
            P(("dp", "tensor"), None),
            P(("dp", "tensor"), None),
            P("dp"),
            P("dp", "tensor"),
            P("dp", "tensor"),
            P("dp", "tensor"),
            P("tensor", "dp"),
            P("dp"),
            P("dp", "tensor"),
            P("dp", "tensor"),
            P("tensor", "dp"),
        ),
        check_vma=False,
    )
```

```python
import functools

import jax
import jax.numpy as jnp
from jax import lax
from jax.experimental import pallas as pl
from jax.experimental.layout import Layout, with_layout_constraint
from jax.experimental.pallas import tpu as pltpu
from jax.sharding import PartitionSpec as P

HEAD_DIM = 64
BLOCK = 128
LANES = 128

norm_epsilon = 1e-05
rope_base = 10000.0
masked_score = -1e30

bf16 = jnp.bfloat16
f32 = jnp.float32

X, Y, T, Z = 0, 1, 2, 3


def nbits():
    return lax.axis_size("dp").bit_length() - 1


def block_axes():
    return [T] + list(range(nbits() - 1, Z - 1, -1)) + [Y, X]


def rest_bits():
    return list(range(Z, nbits()))


def exchange(values, bit):
    size = lax.axis_size("dp")
    return lax.ppermute(values, "dp", [(i, i ^ (1 << bit)) for i in range(size)])


def core_exchange(values):
    return lax.ppermute(values, "tensor", [(0, 1), (1, 0)])


def as_block(values):
    return values.reshape((1,) * nbits() + values.shape)


def after(values, *others):
    return lax.optimization_barrier((values,) + others)[0] if others else values


def row_major(values):
    return with_layout_constraint(values, Layout(major_to_minor=tuple(range(values.ndim))))


def join(values, came, bit):
    return jnp.concatenate([values, came], axis=block_axes().index(bit))


def part(values, bit, index):
    return lax.slice_in_dim(values, index, index + 1, axis=block_axes().index(bit))


def columns(values, low, high):
    return lax.slice_in_dim(values, low, high, axis=values.ndim - 1)


def add(kept, came, kind=bf16):
    return row_major((kept.astype(f32) + came.astype(f32)).astype(kind))


def flat(blocks):
    return blocks.reshape(-1, blocks.shape[-1])


def as_blocks(rows):
    return rows.reshape((2,) * nbits() + (rows.shape[0] // lax.axis_size("dp"), rows.shape[1]))


def block_mask(place):
    axes = block_axes()
    mask = 0
    for level, bit in enumerate(axes):
        mask |= ((place >> (len(axes) - 1 - level)) & 1) << bit
    return mask


def block_place(mask):
    axes = block_axes()
    place = 0
    for level, bit in enumerate(axes):
        place = place + (((mask >> bit) & 1) << (len(axes) - 1 - level))
    return place


def reorder_kernel(count, offsets, *refs):
    half = len(refs) // 2
    for source, target in zip(refs[:half], refs[half:]):
        for place in range(count):
            start = pl.multiple_of(offsets[place], LANES)
            target[:, place * LANES : (place + 1) * LANES] = source[:, pl.ds(start, LANES)]


def reorder(arrays, places):
    count = len(places)
    rows, columns = arrays[0].shape
    width = columns // count
    if width % LANES:
        return [
            jnp.concatenate(
                [lax.dynamic_slice_in_dim(v, p * width, width, 1) for p in places], axis=1
            )
            for v in arrays
        ]
    spec = pl.BlockSpec((BLOCK, columns), lambda i, offsets: (i, 0))
    return pl.pallas_call(
        functools.partial(reorder_kernel, count),
        grid_spec=pltpu.PrefetchScalarGridSpec(
            num_scalar_prefetch=1,
            grid=(rows // BLOCK,),
            in_specs=[spec] * len(arrays),
            out_specs=[spec] * len(arrays),
        ),
        out_shape=[jax.ShapeDtypeStruct(v.shape, v.dtype) for v in arrays],
        compiler_params=pltpu.CompilerParams(vmem_limit_bytes=32 * 1024 * 1024),
        cost_estimate=no_cost(),
        name="reorder",
    )(jnp.stack(places).astype(jnp.int32) * width, *arrays)


def to_relative(*arrays):
    me = lax.axis_index("dp")
    return reorder(arrays, [me ^ block_mask(place) for place in range(lax.axis_size("dp"))])


def from_relative(*arrays):
    me = lax.axis_index("dp")
    return reorder(arrays, [block_place(me ^ index) for index in range(lax.axis_size("dp"))])


def swap_halves(values):
    half = values.shape[1] // 2
    return jnp.concatenate([values[:, half:], values[:, :half]], axis=1)


def pick_first(flag, first, second, axis):
    return jnp.concatenate(
        [jnp.where(flag, first, second), jnp.where(flag, second, first)], axis=axis
    )


def build_layout(lengths, total_rows):
    block_counts = (lengths + BLOCK - 1) // BLOCK
    seq_ends = jnp.cumsum(block_counts, dtype=jnp.int32) * BLOCK
    seq_starts = seq_ends - block_counts * BLOCK
    row_ids = jnp.arange(total_rows, dtype=jnp.int32)
    membership = (
        (row_ids[:, None] >= seq_starts[None, :]) & (row_ids[:, None] < seq_ends[None, :])
    ).astype(jnp.int32)
    slot_ids = jnp.arange(lengths.shape[0], dtype=jnp.int32)
    segment = jnp.sum(membership * (slot_ids[None, :] + 1), axis=1, dtype=jnp.int32) - 1
    first_row = jnp.sum(membership * seq_starts[None, :], axis=1, dtype=jnp.int32)
    seq_limit = jnp.sum(membership * lengths[None, :], axis=1, dtype=jnp.int32)
    position = row_ids - first_row
    is_valid = (segment >= 0) & (position < seq_limit)
    allowed = (
        (segment[:, None] == segment[None, :])
        & (segment[:, None] >= 0)
        & (position[:, None] <= position[None, :])
        & is_valid[:, None]
    )
    allowed = allowed | (row_ids[:, None] == row_ids[None, :])
    bias = jnp.where(allowed, 0.0, masked_score).astype(f32)
    return position, is_valid, bias


def rotation_tables(position):
    half_dim = HEAD_DIM // 2
    lane = jnp.arange(LANES, dtype=jnp.int32)
    frequency = rope_base ** (-2.0 * (lane % half_dim).astype(f32) / HEAD_DIM)
    angles = position.astype(f32)[:, None] * frequency[None, :]
    sign = jnp.where(lane % HEAD_DIM < half_dim, -1.0, 1.0).astype(f32)
    return jnp.cos(angles), jnp.sin(angles) * sign[None, :]


def matmul(left, right):
    return jnp.dot(left, right, preferred_element_type=f32)


def contract_rows(left, right):
    return lax.dot_general(left, right, (((0,), (0,)), ((), ())), preferred_element_type=f32)


def contract_cols(left, right):
    return lax.dot_general(left, right, (((1,), (1,)), ((), ())), preferred_element_type=f32)


def rms_scale(values):
    return lax.rsqrt(jnp.mean(values * values, axis=-1, keepdims=True) + norm_epsilon)


def norm_back(grad_normed, unit_rows, row_scale, gain):
    scaled = grad_normed * gain
    grad_gain = jnp.sum(grad_normed * unit_rows, axis=0)
    grad_rows = row_scale * (
        scaled - unit_rows * jnp.mean(scaled * unit_rows, axis=-1, keepdims=True)
    )
    return grad_gain, grad_rows


def turn(values, cosine, sine):
    lane = lax.broadcasted_iota(jnp.int32, values.shape, 1)
    half_dim = HEAD_DIM // 2
    partner = jnp.where(
        lane % HEAD_DIM < half_dim,
        pltpu.roll(values, LANES - half_dim, 1),
        pltpu.roll(values, half_dim, 1),
    )
    return values * cosine + partner * sine


def doubled(values, second):
    lane = lax.broadcasted_iota(jnp.int32, values.shape, 1)
    rolled = pltpu.roll(values, HEAD_DIM, 1)
    low = lane < HEAD_DIM
    return jnp.where(second, jnp.where(low, rolled, values), jnp.where(low, values, rolled))


def split_heads(pair):
    lane = lax.broadcasted_iota(jnp.int32, pair.shape, 1)
    zero = jnp.zeros_like(pair)
    return jnp.concatenate(
        [jnp.where(lane < HEAD_DIM, pair, zero), jnp.where(lane < HEAD_DIM, zero, pair)], axis=0
    )


def join_heads(wide):
    row = lax.broadcasted_iota(jnp.int32, (LANES, BLOCK), 0)
    return jnp.where(row < HEAD_DIM, wide[:, :BLOCK], wide[:, BLOCK:]).T


def forward_kernel(
    second, q_ref, k_ref, v_ref, bias_ref, cos_ref, sin_ref,
    out_ref, turned_ref, keys_ref, values_ref, total_ref, v2t,
):
    rows = q_ref.shape[0]
    cosine, sine = cos_ref[...], sin_ref[...]

    @pl.when(pl.program_id(0) == 0)
    def _():
        keys = turn(k_ref[...], cosine, sine).astype(bf16).astype(f32)
        keys_ref[...] = doubled(keys, second).astype(bf16)
        values = doubled(v_ref[...], second)
        values_ref[...] = values.astype(bf16)
        v2t[...] = values.T.astype(bf16)

    turned_ref[...] = (turn(q_ref[...], cosine, sine) * HEAD_DIM ** (-0.5)).astype(bf16)
    for index in range(rows // BLOCK):
        span = (index + 1) * BLOCK
        here = slice(index * BLOCK, span)
        queries = split_heads(turned_ref[here, :])
        scores = lax.dot_general(
            keys_ref[:span, :], queries, (((1,), (1,)), ((), ())), preferred_element_type=f32
        )
        bias = bias_ref[:span, here]
        scores = scores + jnp.concatenate([bias, bias], axis=1)
        top = jnp.max(scores, axis=0, keepdims=True)
        weights = jnp.exp(scores - top)
        total = jnp.sum(weights, axis=0, keepdims=True)
        weights = (weights * (1.0 / total)).astype(bf16)
        mixed = jnp.dot(v2t[:, :span], weights, preferred_element_type=f32)
        out_ref[here, :] = join_heads(mixed).astype(bf16)
        total_ref[:, 2 * index * BLOCK : 2 * span] = top + jnp.log(total)


def backward_kernel(
    q_ref, k_ref, v_ref, grad_ref, bias_ref, cos_ref, sin_ref, total_ref,
    dq_ref, dk_ref, dv_ref, k2t, dk_sum, dv_sum,
):
    pair = pl.program_id(0)
    rows = q_ref.shape[0]
    cosine, sine = cos_ref[...], sin_ref[...]

    @pl.when(pair == 0)
    def _():
        k2t[...] = k_ref[...].astype(f32).T.astype(bf16)
        dk_sum[...] = jnp.zeros_like(dk_sum)
        dv_sum[...] = jnp.zeros_like(dv_sum)

    for index in range(rows // BLOCK):
        span = (index + 1) * BLOCK
        here = slice(index * BLOCK, span)
        queries = split_heads(q_ref[here, :])
        grads = split_heads(grad_ref[here, :])
        scores = lax.dot_general(
            k_ref[:span, :], queries, (((1,), (1,)), ((), ())), preferred_element_type=f32
        )
        bias = bias_ref[:span, here]
        scores = scores + jnp.concatenate([bias, bias], axis=1)
        probs = jnp.exp(scores - total_ref[:, 2 * index * BLOCK : 2 * span])
        grad_prob = lax.dot_general(
            v_ref[:span, :], grads, (((1,), (1,)), ((), ())), preferred_element_type=f32
        )
        center = jnp.sum(probs * grad_prob, axis=0, keepdims=True)
        grad_score = (probs * (grad_prob - center)).astype(bf16)
        dv_sum[:span, :] += jnp.dot(probs.astype(bf16), grads, preferred_element_type=f32)
        dk_sum[:span, :] += jnp.dot(grad_score, queries, preferred_element_type=f32)
        wide = jnp.dot(k2t[:, :span], grad_score, preferred_element_type=f32)
        grad_query = join_heads(wide) * HEAD_DIM ** (-0.5)
        dq_ref[here, :] = turn(grad_query, cosine[here, :], -sine[here, :]).astype(bf16)

    @pl.when(pair == pl.num_programs(0) - 1)
    def _():
        keys = dk_sum[...] + pltpu.roll(dk_sum[...], HEAD_DIM, 1)
        dk_ref[...] = turn(keys, cosine, -sine).astype(bf16)
        dv_ref[...] = (dv_sum[...] + pltpu.roll(dv_sum[...], HEAD_DIM, 1)).astype(bf16)


def attend_forward(raw, heads_width, group, bias, cosine, sine):
    rows = raw.shape[0]
    pairs = heads_width // LANES
    own = pairs // 2
    whole = lambda shape: pl.BlockSpec(shape, lambda i: (0, 0))
    column = pl.BlockSpec((rows, LANES), lambda i: (0, i))
    wide = jax.ShapeDtypeStruct((rows, own * LANES), bf16)
    narrow = jax.ShapeDtypeStruct((rows, LANES), bf16)
    return pl.pallas_call(
        functools.partial(forward_kernel, group == 1),
        grid=(own,),
        in_specs=[
            pl.BlockSpec((rows, LANES), lambda i: (0, group * own + i)),
            pl.BlockSpec((rows, LANES), lambda i: (0, pairs)),
            pl.BlockSpec((rows, LANES), lambda i: (0, pairs + 1)),
            whole((rows, rows)),
            whole((rows, LANES)),
            whole((rows, LANES)),
        ],
        out_specs=[
            column,
            column,
            whole((rows, LANES)),
            whole((rows, LANES)),
            pl.BlockSpec((None, 1, 2 * rows), lambda i: (i, 0, 0)),
        ],
        out_shape=[wide, wide, narrow, narrow, jax.ShapeDtypeStruct((own, 1, 2 * rows), f32)],
        scratch_shapes=[pltpu.VMEM((LANES, rows), bf16)],
        compiler_params=pltpu.CompilerParams(vmem_limit_bytes=40 * 1024 * 1024),
        cost_estimate=no_cost(),
        name="attend_forward",
    )(raw, raw, raw, bias, cosine, sine)


def attend_backward(queries, keys, values, grads, bias, cosine, sine, totals):
    rows, width = queries.shape
    whole = lambda shape: pl.BlockSpec(shape, lambda i: (0, 0))
    column = pl.BlockSpec((rows, LANES), lambda i: (0, i))
    narrow = jax.ShapeDtypeStruct((rows, LANES), bf16)
    return pl.pallas_call(
        backward_kernel,
        grid=(width // LANES,),
        in_specs=[
            column,
            whole((rows, LANES)),
            whole((rows, LANES)),
            column,
            whole((rows, rows)),
            whole((rows, LANES)),
            whole((rows, LANES)),
            pl.BlockSpec((None, 1, 2 * rows), lambda i: (i, 0, 0)),
        ],
        out_specs=[column, whole((rows, LANES)), whole((rows, LANES))],
        out_shape=[jax.ShapeDtypeStruct((rows, width), bf16), narrow, narrow],
        scratch_shapes=[
            pltpu.VMEM((LANES, rows), bf16),
            pltpu.VMEM((rows, LANES), f32),
            pltpu.VMEM((rows, LANES), f32),
        ],
        compiler_params=pltpu.CompilerParams(vmem_limit_bytes=40 * 1024 * 1024),
        cost_estimate=no_cost(),
        name="attend_backward",
    )(queries, keys, values, grads, bias, cosine, sine, totals)


def no_cost():
    return pl.CostEstimate(flops=1000000, bytes_accessed=1000000, transcendentals=0)


def whole_block(shape):
    return pl.BlockSpec(shape, lambda i: (0,) * len(shape))


def stack_kernel(*refs):
    out, turned = refs[-2:]
    for index, ref in enumerate(refs[:-2]):

        @pl.when(pl.program_id(0) == index)
        def _():
            value = ref[...]
            out[...] = value
            turned[...] = value.T


def stack_rows(*pieces):
    rows, width = pieces[0].shape
    count = len(pieces)
    kind = pieces[0].dtype
    return pl.pallas_call(
        stack_kernel,
        grid=(count,),
        in_specs=[whole_block((rows, width))] * count,
        out_specs=[
            pl.BlockSpec((rows, width), lambda i: (i, 0)),
            pl.BlockSpec((width, rows), lambda i: (0, i)),
        ],
        out_shape=[
            jax.ShapeDtypeStruct((count * rows, width), kind),
            jax.ShapeDtypeStruct((width, count * rows), kind),
        ],
        compiler_params=pltpu.CompilerParams(vmem_limit_bytes=40 * 1024 * 1024),
        cost_estimate=no_cost(),
        name="stack_rows",
    )(*pieces)


def hidden_kernel(
    rows_ref, grads_ref, gate_ref, up_ref, down_a, down_b, hidden_out, gate_out, up_out
):
    rows, grads = rows_ref[...], grads_ref[...]
    at = down_a.shape[1]
    for down, where in ((down_a, slice(0, at)), (down_b, slice(at, at + down_b.shape[1]))):
        gate = jnp.dot(rows, gate_ref[:, where], preferred_element_type=f32)
        up = jnp.dot(rows, up_ref[:, where], preferred_element_type=f32)
        grad = jnp.dot(grads, down[...], preferred_element_type=f32)
        sigmoid = 1.0 / (1.0 + jnp.exp(-gate))
        silu = gate * sigmoid
        hidden_out[:, where] = (silu * up).astype(bf16)
        gate_out[:, where] = (grad * up * sigmoid * (1.0 + gate * (1.0 - sigmoid))).astype(bf16)
        up_out[:, where] = (grad * silu).astype(bf16)


def hidden_rows(rows, grads, gate, up, down_a, down_b, height):
    total, depth = rows.shape
    width = gate.shape[1]
    tall = pl.BlockSpec((height, depth), lambda i: (i, 0))
    tile = pl.BlockSpec((height, width), lambda i: (i, 0))
    return pl.pallas_call(
        hidden_kernel,
        grid=(total // height,),
        in_specs=[tall, tall] + [whole_block(v.shape) for v in (gate, up, down_a, down_b)],
        out_specs=[tile] * 3,
        out_shape=[jax.ShapeDtypeStruct((total, width), bf16)] * 3,
        compiler_params=pltpu.CompilerParams(vmem_limit_bytes=48 * 1024 * 1024),
        cost_estimate=no_cost(),
        name="hidden_rows",
    )(rows, grads, gate, up, down_a, down_b)


def weight_grad_kernel(
    inner, turned_near, turned_far, near_ref, far_ref,
    grads_near, grads_far, hidden_near, hidden_far, kept, sent,
):
    def product(*pairs):
        return sum(jnp.dot(l[...], r[...], preferred_element_type=f32) for l, r in pairs)

    both = jnp.concatenate(
        [
            product((turned_near, near_ref), (turned_far, far_ref)),
            product((grads_near, hidden_near), (grads_far, hidden_far)),
        ],
        axis=1,
    ).astype(bf16)
    block = kept.shape[-2] * (1 if inner else 2)
    both = both.reshape(-1, 2, block, both.shape[-1])
    kept[...] = both[:, 0].reshape(kept.shape)
    sent[...] = both[:, 1].reshape(sent.shape)


def weight_grads(turned, lefts, grads_turned, hiddens, inner):
    depth, total = turned[0].shape
    block = depth // lax.axis_size("dp")
    high = 512
    count = high // (2 * block)
    width = lefts[0].shape[1] + hiddens[0].shape[1]
    out = pl.BlockSpec((count, block, width), lambda i: (i, 0, 0))
    shape = jax.ShapeDtypeStruct((depth // (2 * block), block, width), bf16)
    tall = pl.BlockSpec((high, total), lambda i: (i, 0))
    kept, sent = pl.pallas_call(
        functools.partial(weight_grad_kernel, inner),
        grid=(depth // high,),
        in_specs=[tall, tall]
        + [whole_block(v.shape) for v in lefts]
        + [tall, tall]
        + [whole_block(v.shape) for v in hiddens],
        out_specs=[out, out],
        out_shape=[shape, shape],
        compiler_params=pltpu.CompilerParams(vmem_limit_bytes=48 * 1024 * 1024),
        cost_estimate=no_cost(),
        name="weight_grads",
    )(*turned, *lefts, *grads_turned, *hiddens)
    dims = [2] * nbits()
    dims[block_axes().index(X if inner else Y)] = 1
    return kept.reshape(*dims, block, width), sent.reshape(*dims, block, width)


def back_kernel(cuts, *refs):
    count = len(cuts)
    weights, (own, other) = refs[len(refs) - 2 - count : len(refs) - 2], refs[-2:]
    lefts = refs[: len(refs) - 2 - count]
    total = 0.0
    for (index, low, high), weight in zip(cuts, weights):
        total += lax.dot_general(
            lefts[index][:, low:high],
            weight[...],
            (((1,), (1,)), ((), ())),
            preferred_element_type=f32,
        )
    half = own.shape[0]
    own[...] = total[:half]
    other[...] = total[half:].astype(bf16)


def back_rows(lefts, weights, cuts):
    rows = lefts[0].shape[0]
    depth = weights[0].shape[0]
    high = 512
    return pl.pallas_call(
        functools.partial(back_kernel, cuts),
        grid=(depth // high,),
        in_specs=[whole_block(v.shape) for v in lefts]
        + [pl.BlockSpec((high, v.shape[1]), lambda i: (i, 0)) for v in weights],
        out_specs=[pl.BlockSpec((rows // 2, high), lambda i: (0, i))] * 2,
        out_shape=[
            jax.ShapeDtypeStruct((rows // 2, depth), f32),
            jax.ShapeDtypeStruct((rows // 2, depth), bf16),
        ],
        compiler_params=pltpu.CompilerParams(vmem_limit_bytes=48 * 1024 * 1024),
        cost_estimate=no_cost(),
        name="back_rows",
    )(*lefts, *weights)


def my_half():
    return (lax.axis_index("dp") >> T) & 1


class Chunks:
    def __init__(self, quarter):
        self.quarter = quarter
        middle = -(-quarter // (2 * LANES)) * LANES
        self.spans = ((0, middle), (middle, quarter))
        self.cuts = [low + (high - low) // (2 * LANES) * LANES for low, high in self.spans]

    def layout(self, index):
        (low, high), at = self.spans[index], self.cuts[index]
        width = high - low
        return (
            (0, low, high, 0),
            (2, low, at, width),
            (1, low, high, width + at - low),
            (2, at, high, 2 * width + at - low),
        )

    def width(self, index):
        low, high = self.spans[index]
        return 3 * (high - low)

    def turn(self, index):
        (low, high), at = self.spans[index], self.cuts[index]
        return high - low + at - low


def pack_kernel(chunks, t_ref, gate_ref, up_ref, down_ref, *outs):
    for side in (0, 1):
        start = jnp.where(side == 0, t_ref[0], 1 - t_ref[0]) * chunks.quarter
        for index in (0, 1):
            out = outs[2 * side + index]
            for matrix, low, high, place in chunks.layout(index):
                where = pl.ds(pl.multiple_of(start + low, LANES), high - low)
                if matrix == 2:
                    value = down_ref[where, :].astype(f32).T.astype(bf16)
                else:
                    value = (gate_ref, up_ref)[matrix][:, where]
                out[:, place : place + high - low] = value


def pack_columns(chunks, gate, up, down):
    rows = gate.shape[0]
    if rows % LANES:
        sides = []
        for side in (0, 1):
            start = jnp.where(side == 0, my_half(), 1 - my_half()) * chunks.quarter
            halves = [
                lax.dynamic_slice_in_dim(v, start, chunks.quarter, 1) for v in (gate, up, down.T)
            ]
            for index in (0, 1):
                parts = sorted(chunks.layout(index), key=lambda entry: entry[3])
                sides.append(jnp.concatenate([halves[m][:, l:h] for m, l, h, _ in parts], axis=1))
        return sides
    whole = pl.BlockSpec(memory_space=pltpu.VMEM)
    shapes = [jax.ShapeDtypeStruct((rows, chunks.width(i)), bf16) for i in (0, 1)]
    return pl.pallas_call(
        functools.partial(pack_kernel, chunks),
        in_specs=[pl.BlockSpec(memory_space=pltpu.SMEM), whole, whole, whole],
        out_specs=[whole] * 4,
        out_shape=shapes + shapes,
        compiler_params=pltpu.CompilerParams(vmem_limit_bytes=40 * 1024 * 1024),
        cost_estimate=no_cost(),
        name="pack_columns",
    )(my_half().reshape(1).astype(jnp.int32), gate, up, down)


def unpack_kernel(chunks, t_ref, *refs):
    outs = refs[4:]
    for side in (0, 1):
        start = jnp.where(side == 0, t_ref[0], 1 - t_ref[0]) * chunks.quarter
        for index in (0, 1):
            for matrix, low, high, place in chunks.layout(index):
                where = pl.ds(pl.multiple_of(start + low, LANES), high - low)
                value = refs[2 * side + index][:, place : place + high - low].astype(f32)
                if matrix == 2:
                    outs[2][where, :] = value.T
                else:
                    outs[matrix][:, where] = value


def unpack_columns(chunks, *bundles):
    rows = bundles[0].shape[0]
    if rows % LANES:
        halves = []
        for side in (0, 1):
            found = [[], [], []]
            for index in (0, 1):
                for matrix, low, high, place in chunks.layout(index):
                    value = bundles[2 * side + index][:, place : place + high - low].astype(f32)
                    found[matrix].append((low, value))
            halves.append(
                [jnp.concatenate([v for _, v in sorted(f, key=lambda e: e[0])], axis=1) for f in found]
            )
        gate, up, down = [
            pick_first(my_half() == 0, own, came, 1) for own, came in zip(*halves)
        ]
        return gate, up, down.T
    whole = pl.BlockSpec(memory_space=pltpu.VMEM)
    flat_shape = jax.ShapeDtypeStruct((rows, 2 * chunks.quarter), f32)
    return pl.pallas_call(
        functools.partial(unpack_kernel, chunks),
        in_specs=[pl.BlockSpec(memory_space=pltpu.SMEM)] + [whole] * 4,
        out_specs=[whole] * 3,
        out_shape=[flat_shape, flat_shape, jax.ShapeDtypeStruct((2 * chunks.quarter, rows), f32)],
        compiler_params=pltpu.CompilerParams(vmem_limit_bytes=40 * 1024 * 1024),
        cost_estimate=no_cost(),
        name="unpack_columns",
    )(my_half().reshape(1).astype(jnp.int32), *bundles)


def body(
    inputs, cotangent, seq_lengths, attn_gain, w_query, w_key, w_value, w_out,
    mlp_gain, w_gate, w_up, w_down,
):
    own_rows = inputs.shape[0]
    chip_rows = 2 * own_rows
    core = lax.axis_index("tensor")
    rest = rest_bits()
    heads_width = w_query.shape[1]
    kv_width = w_key.shape[1]
    cut = (heads_width + 2 * kv_width) // 2
    cut_out = heads_width // 2

    last = []

    def held(values, *others):
        values = after(values, *last, *others)
        last[:] = [values]
        return values

    def did(values):
        last[:] = [values]
        return values

    def send(values, bit, *others):
        return exchange(held(values, *others), bit)

    def swap(values, *others):
        return core_exchange(held(values, *others))

    def gather(values, bit, *others):
        came = send(values, bit, *others)
        return lambda: join(values, held(came), bit)

    def fold(values, bit, kind=bf16):
        came = send(row_major(part(values, bit, 1).astype(bf16)), bit)
        return lambda: add(part(values, bit, 0), held(came), kind)

    gains = as_block(jnp.stack([attn_gain, mlp_gain]))
    gains = gather(gains, rest[0])
    qkv = jnp.concatenate([w_query, w_key, w_value], axis=1)
    q = gather(as_block(qkv), rest[0])
    for bit in rest[1:] + [T]:
        gains = gather(gains(), bit)
    inputs_rel, cotangent_rel = to_relative(held(inputs), cotangent)
    did(inputs_rel)
    gains = gather(gains(), X)
    out_t = did(held(w_out.T))
    gains = gather(gains(), Y)
    o = gather(as_block(out_t), rest[0])
    for bit in rest[1:] + [T]:
        q = gather(q(), bit)
    chunks = Chunks(w_gate.shape[1] // 2)
    own_0, own_1, other_0, other_1 = pack_columns(chunks, held(w_gate), w_up, w_down)
    did(own_0)
    gains = flat(gains()).reshape(-1, 2, attn_gain.shape[0]).transpose(1, 0, 2)
    gains = gains.reshape(2, -1).astype(f32)
    gain_one, gain_two = gains[0], gains[1]
    inputs_wide = inputs_rel.astype(f32)
    scale_one = rms_scale(inputs_wide)
    unit_one = inputs_wide * scale_one
    normed_own = (unit_one * gain_one).astype(bf16)
    normed_other = swap(normed_own)
    for bit in rest[1:] + [T]:
        o = gather(o(), bit)
    position, is_valid, bias = build_layout(seq_lengths[0], chip_rows)
    cosine, sine = rotation_tables(position)
    own_valid = lax.dynamic_slice_in_dim(is_valid, core * own_rows, own_rows, 0)[:, None]
    grad_branch_own = jnp.where(own_valid, cotangent_rel, jnp.zeros_like(cotangent_rel))
    q = q()
    qa = gather(columns(q, 0, cut), X)
    qb = gather(columns(q, cut, 2 * cut), Y)
    w0_t = send(as_block(other_0), T)
    bias = did(held(bias))
    grad_branch_other = swap(grad_branch_own)
    qa = gather(qa(), Y)
    qb = gather(qb(), X)
    w0 = join(as_block(own_0), held(w0_t), T)
    w0 = gather(w0, rest[0])
    grad_far_own = send(swap_halves(grad_branch_own), T)
    qa, qb = qa(), qb()
    o = o()
    oa = gather(columns(o, 0, cut_out), X)
    ob = gather(columns(o, cut_out, heads_width), Y)
    query_w = jnp.concatenate([flat(qa), flat(qb)], axis=1)

    normed = pick_first(core == 0, normed_own, normed_other, 0)
    raw = did(matmul(held(normed), query_w))
    tables = (bias, cosine, sine)
    mixed_a, queries_a, keys_a, values_a, totals_a = attend_forward(raw, heads_width, 0, *tables)
    did(mixed_a)
    oa = gather(oa(), Y)
    ob = gather(ob(), X)
    mixed_b, queries_b, keys_b, values_b, totals_b = attend_forward(
        held(raw), heads_width, 1, *tables
    )
    did(mixed_b)
    for bit in rest[1:]:
        w0 = gather(w0(), bit)
    w0 = w0()
    grad_far_other = swap(grad_far_own)
    w1_t = send(as_block(other_1), T)
    oa, ob = flat(oa()), flat(ob())
    w0b = gather(columns(w0, chunks.turn(0), w0.shape[-1]), Y)
    w0a = gather(columns(w0, 0, chunks.turn(0)), X)

    def rows_of(values, which):
        return lax.dynamic_slice_in_dim(values, which * own_rows, own_rows, 0)

    def project(which, mixed_a):
        return contract_cols(rows_of(mixed_a, which), oa) + contract_cols(
            rows_of(mixed_b, which), ob
        )

    came = swap(project(1 - core, held(mixed_a)).astype(bf16))
    residual = did(inputs_wide + (project(core, held(mixed_a)) + held(came).astype(f32)))

    scale_two = rms_scale(residual)
    unit_two = residual * scale_two
    normed_mlp_own = (unit_two * gain_two).astype(bf16)
    far_own = send(swap_halves(normed_mlp_own), T)
    near_other = held(swap(normed_mlp_own))
    near, near_turned = stack_rows(normed_mlp_own, near_other)
    did(near)
    grad_near, grad_near_turned = stack_rows(held(grad_branch_own), grad_branch_other)
    did(grad_near)
    w1 = join(as_block(own_1), held(w1_t), T)
    w1 = gather(w1, rest[0])
    grad_far, grad_far_turned = stack_rows(grad_far_own, held(grad_far_other))
    did(grad_far)
    w0b, w0a = w0b(), w0a()
    w0b_x = send(w0b, X)
    w0a_y = send(w0a, Y)
    for bit in rest[1:]:
        w1 = gather(w1(), bit)
    w1 = w1()

    def weights_of(first_a, came_a, first_b, came_b, index):
        whole_a = lambda low, high: flat(
            join(columns(first_a, low, high), columns(came_a, low, high), Y)
        )
        whole_b = lambda low, high: flat(
            join(columns(first_b, low, high), columns(came_b, low, high), X)
        )
        width, at = chunks.width(index) // 3, chunks.turn(index)
        return (
            whole_a(0, width), whole_b(0, width),
            whole_a(width, at), whole_b(width, chunks.width(index) - at),
        )

    def hidden_layer(rows, grads, weights):
        hidden, grad_gate, grad_up = hidden_rows(held(rows), grads, *weights, own_rows)
        return did(hidden), grad_gate, grad_up

    def weight_grad(left, right):
        return did(as_blocks(contract_rows(left, held(right)).astype(bf16)))

    def bundle_grads(grads, hiddens, index, inner):
        width = chunks.width(index) // 3
        at = chunks.turn(index) - width
        low, high = (at, width) if inner else (0, at)
        kept, sent = weight_grads(
            (near_turned, far_turned), (held(grads[0]), grads[1]),
            (grad_near_turned, grad_far_turned), [v[:, low:high] for v in hiddens], inner,
        )
        did(sent)
        return kept, sent

    weights_0 = weights_of(w0a, held(w0a_y), w0b, held(w0b_x), 0)
    w1a = gather(columns(w1, 0, chunks.turn(1)), X)
    w1b = gather(columns(w1, chunks.turn(1), w1.shape[-1]), Y)
    far_other = swap(far_own)
    near_0 = hidden_layer(near, grad_near, weights_0)
    far, far_turned = stack_rows(far_own, held(far_other))
    did(far)
    w1a, w1b = w1a(), w1b()
    w1a_y = send(w1a, Y)
    w1b_x = send(w1b, X)
    far_0 = hidden_layer(far, grad_far, weights_0)
    both = lambda index: (near_0[index], far_0[index])
    r0a, r0a_sent = bundle_grads(both(1), both(0), 0, False)
    r0a_y = send(r0a_sent, Y)
    r0b, r0b_sent = bundle_grads(both(2), both(0), 0, True)
    r0b_x = send(r0b_sent, X)
    weights_1 = weights_of(w1a, held(w1a_y), w1b, held(w1b_x), 1)
    weights_hidden = [*weights_0[:2], *weights_1[:2]]
    weights_down = [*weights_0[2:], *weights_1[2:]]
    cuts_hidden = tuple((i, 0, v.shape[1]) for i, v in enumerate(weights_hidden))
    cuts_down = tuple(
        (i, low, high)
        for i in (0, 1)
        for low, high in (
            (0, weights_down[2 * i].shape[1]),
            (weights_down[2 * i].shape[1], weights_hidden[2 * i].shape[1]),
        )
    )

    def hidden_back(first, second):
        lefts = [held(first[1]), first[2], second[1], second[2]]
        own, other = back_rows(lefts, weights_hidden, cuts_hidden)
        return did(own), other

    def branch_back(first, second):
        own, other = back_rows([held(first[0]), second[0]], weights_down, cuts_down)
        return did(own), other

    far_1 = hidden_layer(far, grad_far, weights_1)
    far_part, far_sent = hidden_back(far_0, far_1)
    far_came = swap(far_sent)
    near_1 = hidden_layer(near, grad_near, weights_1)
    both_1 = lambda index: (near_1[index], far_1[index])
    r0a = add(r0a, held(r0a_y))
    r0b = add(r0b, held(r0b_x))
    r0a_x = send(row_major(part(r0a, X, 1)), X)
    r0b_y = send(row_major(part(r0b, Y, 1)), Y)
    far_sum = far_part + held(far_came).astype(f32)
    grad_z = send(swap_halves(far_sum.astype(bf16)), T)
    r1a, r1a_sent = bundle_grads(both_1(1), both_1(0), 1, False)
    r1a_y = send(r1a_sent, Y)
    r1b, r1b_sent = bundle_grads(both_1(2), both_1(0), 1, True)
    r1b_x = send(r1b_sent, X)
    near_part, near_sent = hidden_back(near_0, near_1)
    near_came = swap(near_sent)

    def joined(a, a_came, b, b_came):
        return jnp.concatenate(
            [add(part(a, X, 0), held(a_came)), add(part(b, Y, 0), held(b_came))], axis=-1
        )

    r0 = joined(r0a, r0a_x, r0b, r0b_y)
    for bit in rest[:0:-1]:
        r0 = fold(r0, bit)()
    r0 = fold(r0, rest[0], f32)

    grad_normed_mlp = near_part + held(near_came).astype(f32) + held(grad_z).astype(f32)
    grad_gain_two, grad_norm_two = norm_back(grad_normed_mlp, unit_two, scale_two, gain_two)
    grad_residual = grad_branch_own.astype(f32) + grad_norm_two
    grad_att_own = grad_residual.astype(bf16)
    grad_att_other = swap(grad_att_own)
    far_branch, far_branch_sent = branch_back(far_0, far_1)
    far_branch_came = swap(far_branch_sent)
    r1a = add(r1a, held(r1a_y))
    r1b = add(r1b, held(r1b_x))
    r1a_x = send(row_major(part(r1a, X, 1)), X)
    r1b_y = send(row_major(part(r1b, Y, 1)), Y)
    grad_attended = pick_first(core == 0, grad_att_own, held(grad_att_other), 0)
    grad_out_a = weight_grad(grad_attended, mixed_a)
    roa_y = send(row_major(part(grad_out_a, Y, 1)), Y)
    grad_out_b = weight_grad(grad_attended, mixed_b)
    rob_x = send(row_major(part(grad_out_b, X, 1)), X)
    branch_sum = far_branch + held(far_branch_came).astype(f32)
    branch_z = send(swap_halves(branch_sum.astype(bf16)), T)
    d_query_a, d_key_a, d_value_a = attend_backward(
        queries_a, keys_a, values_a, matmul(held(grad_attended), oa).astype(bf16), *tables, totals_a
    )
    did(d_query_a)
    r0 = r0()
    r0_t = send(row_major(part(r0, T, 1).astype(bf16)), T)
    r1 = joined(r1a, r1a_x, r1b, r1b_y)
    for bit in rest[:0:-1]:
        r1 = fold(r1, bit)()
    r1 = fold(r1, rest[0], f32)
    d_query_b, d_key_b, d_value_b = attend_backward(
        queries_b, keys_b, values_b, matmul(held(grad_attended), ob).astype(bf16), *tables, totals_b
    )
    did(d_query_b)
    out_a = add(part(grad_out_a, Y, 0), held(roa_y))
    out_b = add(part(grad_out_b, X, 0), held(rob_x))
    roa_x = send(row_major(part(out_a, X, 1)), X)
    rob_y = send(row_major(part(out_b, Y, 1)), Y)
    low = jnp.arange(kv_width) < HEAD_DIM
    d_qkv = jnp.concatenate(
        [
            d_query_a, d_query_b,
            jnp.where(low, d_key_a, d_key_b), jnp.where(low, d_value_a, d_value_b),
        ],
        axis=1,
    )
    grad_qkv = weight_grad(normed, d_qkv)
    qkv_a, qkv_b = columns(grad_qkv, 0, cut), columns(grad_qkv, cut, 2 * cut)
    rqa_y = send(row_major(part(qkv_a, Y, 1)), Y)
    rqb_x = send(row_major(part(qkv_b, X, 1)), X)
    r0_t = held(r0_t)
    d_came = swap(contract_cols(rows_of(held(d_qkv), 1 - core), query_w).astype(bf16))
    near_branch, near_branch_sent = branch_back(near_0, near_1)
    near_branch_came = swap(near_branch_sent)
    out = fold(joined(out_a, roa_x, out_b, rob_y), T)
    r1 = r1()
    r1_t = send(row_major(part(r1, T, 1).astype(bf16)), T)
    qkv_a = add(part(qkv_a, Y, 0), held(rqa_y))
    qkv_b = add(part(qkv_b, X, 0), held(rqb_x))
    rqa_x = send(row_major(part(qkv_a, X, 1)), X)
    rqb_y = send(row_major(part(qkv_b, Y, 1)), Y)
    grad_normed = contract_cols(rows_of(held(d_qkv), core), query_w) + held(d_came).astype(f32)
    grad_gain_one, grad_norm_one = norm_back(grad_normed, unit_one, scale_one, gain_one)
    grad_rows = did(grad_residual + grad_norm_one)
    grad_gains = jnp.stack([grad_gain_one, grad_gain_two])
    gains_came = swap(grad_gains)
    out = out()
    for bit in rest[:0:-1]:
        out = fold(out, bit)()
    out = fold(out, rest[0], f32)
    grad_gains = grad_gains + held(gains_came)
    gain_blocks = grad_gains.reshape(2, lax.axis_size("dp"), -1).transpose(1, 0, 2)
    gain_blocks = gain_blocks.reshape((2,) * nbits() + gain_blocks.shape[1:])

    def fold_gains(blocks, bit):
        came = send(part(blocks, bit, 1), bit)
        return lambda: part(blocks, bit, 0) + held(came)

    gain_blocks = fold_gains(gain_blocks, Y)
    grad_rows = did(from_relative(held(grad_rows))[0])
    sum_qkv = fold(joined(qkv_a, rqa_x, qkv_b, rqb_y), T)
    gain_blocks = fold_gains(gain_blocks(), X)
    branch = near_branch + held(near_branch_came).astype(f32) + held(branch_z).astype(f32)
    output = jnp.where(own_valid, residual + branch, 0.0).astype(bf16)
    output = did(from_relative(output)[0])
    sum_gate, sum_up, sum_down = unpack_columns(
        chunks, flat(part(r0, T, 0)), flat(part(r1, T, 0)), flat(r0_t), held(flat(r1_t))
    )
    did(sum_gate)
    gain_blocks = fold_gains(gain_blocks(), T)
    for bit in rest[:0:-1]:
        sum_qkv = fold(sum_qkv(), bit)
        gain_blocks = fold_gains(gain_blocks(), bit)
    sum_qkv = fold(sum_qkv(), rest[0], f32)
    gain_blocks = fold_gains(gain_blocks(), rest[0])
    out = out()
    sum_qkv = flat(sum_qkv())
    gain_sums = gain_blocks().reshape(2, -1)
    return (
        output,
        grad_rows,
        gain_sums[0],
        sum_qkv[:, :heads_width],
        sum_qkv[:, heads_width : heads_width + kv_width],
        sum_qkv[:, heads_width + kv_width :],
        flat(out).T,
        gain_sums[1],
        sum_gate,
        sum_up,
        sum_down,
    )


def solution(mesh):
    placed = (
        P(("dp", "tensor"), None),
        P(("dp", "tensor"), None),
        P("dp", None),
        P("dp"),
        P("dp", "tensor"),
        P("dp", "tensor"),
        P("dp", "tensor"),
        P("tensor", "dp"),
        P("dp"),
        P("dp", "tensor"),
        P("dp", "tensor"),
        P("tensor", "dp"),
    )
    return jax.shard_map(
        body,
        mesh=mesh,
        in_specs=placed,
        out_specs=(
            P(("dp", "tensor"), None),
            P(("dp", "tensor"), None),
            P("dp"),
            P("dp", "tensor"),
            P("dp", "tensor"),
            P("dp", "tensor"),
            P("tensor", "dp"),
            P("dp"),
            P("dp", "tensor"),
            P("dp", "tensor"),
            P("tensor", "dp"),
        ),
        check_vma=False,
    )
```

```python
import functools

import jax
import jax.numpy as jnp
from jax import lax
from jax.experimental import pallas as pl
from jax.experimental.layout import Layout, with_layout_constraint
from jax.experimental.pallas import tpu as pltpu
from jax.sharding import PartitionSpec as P

HEAD_DIM = 64
BLOCK = 128
LANES = 128

norm_epsilon = 1e-05
rope_base = 10000.0
masked_score = -1e30

bf16 = jnp.bfloat16
f32 = jnp.float32

X, Y, T, Z = 0, 1, 2, 3


def nbits():
    return lax.axis_size("dp").bit_length() - 1


def block_axes():
    return [T] + list(range(nbits() - 1, Z - 1, -1)) + [Y, X]


def rest_bits():
    return list(range(Z, nbits()))


def exchange(values, bit):
    size = lax.axis_size("dp")
    return lax.ppermute(values, "dp", [(i, i ^ (1 << bit)) for i in range(size)])


def core_exchange(values):
    return lax.ppermute(values, "tensor", [(0, 1), (1, 0)])


def as_block(values):
    return values.reshape((1,) * nbits() + values.shape)


def after(values, *others):
    return lax.optimization_barrier((values,) + others)[0] if others else values


def row_major(values):
    return with_layout_constraint(values, Layout(major_to_minor=tuple(range(values.ndim))))


def join(values, came, bit):
    return jnp.concatenate([values, came], axis=block_axes().index(bit))


def part(values, bit, index):
    return lax.slice_in_dim(values, index, index + 1, axis=block_axes().index(bit))


def columns(values, low, high):
    return lax.slice_in_dim(values, low, high, axis=values.ndim - 1)


def add(kept, came, kind=bf16):
    return row_major((kept.astype(f32) + came.astype(f32)).astype(kind))


def flat(blocks):
    return blocks.reshape(-1, blocks.shape[-1])


def as_blocks(rows):
    return rows.reshape((2,) * nbits() + (rows.shape[0] // lax.axis_size("dp"), rows.shape[1]))


def block_mask(place):
    axes = block_axes()
    mask = 0
    for level, bit in enumerate(axes):
        mask |= ((place >> (len(axes) - 1 - level)) & 1) << bit
    return mask


def block_place(mask):
    axes = block_axes()
    place = 0
    for level, bit in enumerate(axes):
        place = place + (((mask >> bit) & 1) << (len(axes) - 1 - level))
    return place


def reorder_kernel(count, offsets, *refs):
    half = len(refs) // 2
    for source, target in zip(refs[:half], refs[half:]):
        for place in range(count):
            start = pl.multiple_of(offsets[place], LANES)
            target[:, place * LANES : (place + 1) * LANES] = source[:, pl.ds(start, LANES)]


def reorder(arrays, places):
    count = len(places)
    rows, columns = arrays[0].shape
    width = columns // count
    if width % LANES:
        return [
            jnp.concatenate(
                [lax.dynamic_slice_in_dim(v, p * width, width, 1) for p in places], axis=1
            )
            for v in arrays
        ]
    spec = pl.BlockSpec((BLOCK, columns), lambda i, offsets: (i, 0))
    return pl.pallas_call(
        functools.partial(reorder_kernel, count),
        grid_spec=pltpu.PrefetchScalarGridSpec(
            num_scalar_prefetch=1,
            grid=(rows // BLOCK,),
            in_specs=[spec] * len(arrays),
            out_specs=[spec] * len(arrays),
        ),
        out_shape=[jax.ShapeDtypeStruct(v.shape, v.dtype) for v in arrays],
        compiler_params=pltpu.CompilerParams(vmem_limit_bytes=32 * 1024 * 1024),
        cost_estimate=no_cost(),
        name="reorder",
    )(jnp.stack(places).astype(jnp.int32) * width, *arrays)


def to_relative(*arrays):
    me = lax.axis_index("dp")
    return reorder(arrays, [me ^ block_mask(place) for place in range(lax.axis_size("dp"))])


def from_relative(*arrays):
    me = lax.axis_index("dp")
    return reorder(arrays, [block_place(me ^ index) for index in range(lax.axis_size("dp"))])


def swap_halves(values):
    half = values.shape[1] // 2
    return jnp.concatenate([values[:, half:], values[:, :half]], axis=1)


def pick_first(flag, first, second, axis):
    return jnp.concatenate(
        [jnp.where(flag, first, second), jnp.where(flag, second, first)], axis=axis
    )


def build_layout(lengths, total_rows):
    block_counts = (lengths + BLOCK - 1) // BLOCK
    seq_ends = jnp.cumsum(block_counts, dtype=jnp.int32) * BLOCK
    seq_starts = seq_ends - block_counts * BLOCK
    row_ids = jnp.arange(total_rows, dtype=jnp.int32)
    membership = (
        (row_ids[:, None] >= seq_starts[None, :]) & (row_ids[:, None] < seq_ends[None, :])
    ).astype(jnp.int32)
    slot_ids = jnp.arange(lengths.shape[0], dtype=jnp.int32)
    segment = jnp.sum(membership * (slot_ids[None, :] + 1), axis=1, dtype=jnp.int32) - 1
    first_row = jnp.sum(membership * seq_starts[None, :], axis=1, dtype=jnp.int32)
    seq_limit = jnp.sum(membership * lengths[None, :], axis=1, dtype=jnp.int32)
    position = row_ids - first_row
    is_valid = (segment >= 0) & (position < seq_limit)
    allowed = (
        (segment[:, None] == segment[None, :])
        & (segment[:, None] >= 0)
        & (position[:, None] <= position[None, :])
        & is_valid[:, None]
    )
    allowed = allowed | (row_ids[:, None] == row_ids[None, :])
    bias = jnp.where(allowed, 0.0, masked_score).astype(f32)
    return position, is_valid, bias


def rotation_tables(position):
    half_dim = HEAD_DIM // 2
    lane = jnp.arange(LANES, dtype=jnp.int32)
    frequency = rope_base ** (-2.0 * (lane % half_dim).astype(f32) / HEAD_DIM)
    angles = position.astype(f32)[:, None] * frequency[None, :]
    sign = jnp.where(lane % HEAD_DIM < half_dim, -1.0, 1.0).astype(f32)
    return jnp.cos(angles), jnp.sin(angles) * sign[None, :]


def matmul(left, right):
    return jnp.dot(left, right, preferred_element_type=f32)


def contract_rows(left, right):
    return lax.dot_general(left, right, (((0,), (0,)), ((), ())), preferred_element_type=f32)


def contract_cols(left, right):
    return lax.dot_general(left, right, (((1,), (1,)), ((), ())), preferred_element_type=f32)


def rms_scale(values):
    return lax.rsqrt(jnp.mean(values * values, axis=-1, keepdims=True) + norm_epsilon)


def norm_back(grad_normed, unit_rows, row_scale, gain):
    scaled = grad_normed * gain
    grad_gain = jnp.sum(grad_normed * unit_rows, axis=0)
    grad_rows = row_scale * (
        scaled - unit_rows * jnp.mean(scaled * unit_rows, axis=-1, keepdims=True)
    )
    return grad_gain, grad_rows


def turn(values, cosine, sine):
    lane = lax.broadcasted_iota(jnp.int32, values.shape, 1)
    half_dim = HEAD_DIM // 2
    partner = jnp.where(
        lane % HEAD_DIM < half_dim,
        pltpu.roll(values, LANES - half_dim, 1),
        pltpu.roll(values, half_dim, 1),
    )
    return values * cosine + partner * sine


def doubled(values, second):
    lane = lax.broadcasted_iota(jnp.int32, values.shape, 1)
    rolled = pltpu.roll(values, HEAD_DIM, 1)
    low = lane < HEAD_DIM
    return jnp.where(second, jnp.where(low, rolled, values), jnp.where(low, values, rolled))


def split_heads(pair):
    lane = lax.broadcasted_iota(jnp.int32, pair.shape, 1)
    zero = jnp.zeros_like(pair)
    return jnp.concatenate(
        [jnp.where(lane < HEAD_DIM, pair, zero), jnp.where(lane < HEAD_DIM, zero, pair)], axis=0
    )


def join_heads(wide):
    row = lax.broadcasted_iota(jnp.int32, (LANES, BLOCK), 0)
    return jnp.where(row < HEAD_DIM, wide[:, :BLOCK], wide[:, BLOCK:]).T


def forward_kernel(
    second, q_ref, k_ref, v_ref, bias_ref, cos_ref, sin_ref,
    out_ref, turned_ref, keys_ref, values_ref, total_ref, v2t,
):
    rows = q_ref.shape[0]
    cosine, sine = cos_ref[...], sin_ref[...]

    @pl.when(pl.program_id(0) == 0)
    def _():
        keys = turn(k_ref[...], cosine, sine).astype(bf16).astype(f32)
        keys_ref[...] = doubled(keys, second).astype(bf16)
        values = doubled(v_ref[...], second)
        values_ref[...] = values.astype(bf16)
        v2t[...] = values.T.astype(bf16)

    turned_ref[...] = (turn(q_ref[...], cosine, sine) * HEAD_DIM ** (-0.5)).astype(bf16)
    for index in range(rows // BLOCK):
        span = (index + 1) * BLOCK
        here = slice(index * BLOCK, span)
        queries = split_heads(turned_ref[here, :])
        scores = lax.dot_general(
            keys_ref[:span, :], queries, (((1,), (1,)), ((), ())), preferred_element_type=f32
        )
        bias = bias_ref[:span, here]
        scores = scores + jnp.concatenate([bias, bias], axis=1)
        top = jnp.max(scores, axis=0, keepdims=True)
        weights = jnp.exp(scores - top)
        total = jnp.sum(weights, axis=0, keepdims=True)
        weights = (weights * (1.0 / total)).astype(bf16)
        mixed = jnp.dot(v2t[:, :span], weights, preferred_element_type=f32)
        out_ref[here, :] = join_heads(mixed).astype(bf16)
        total_ref[:, 2 * index * BLOCK : 2 * span] = top + jnp.log(total)


def backward_kernel(
    q_ref, k_ref, v_ref, grad_ref, bias_ref, cos_ref, sin_ref, total_ref,
    dq_ref, dk_ref, dv_ref, k2t, dk_sum, dv_sum,
):
    pair = pl.program_id(0)
    rows = q_ref.shape[0]
    cosine, sine = cos_ref[...], sin_ref[...]

    @pl.when(pair == 0)
    def _():
        k2t[...] = k_ref[...].astype(f32).T.astype(bf16)
        dk_sum[...] = jnp.zeros_like(dk_sum)
        dv_sum[...] = jnp.zeros_like(dv_sum)

    for index in range(rows // BLOCK):
        span = (index + 1) * BLOCK
        here = slice(index * BLOCK, span)
        queries = split_heads(q_ref[here, :])
        grads = split_heads(grad_ref[here, :])
        scores = lax.dot_general(
            k_ref[:span, :], queries, (((1,), (1,)), ((), ())), preferred_element_type=f32
        )
        bias = bias_ref[:span, here]
        scores = scores + jnp.concatenate([bias, bias], axis=1)
        probs = jnp.exp(scores - total_ref[:, 2 * index * BLOCK : 2 * span])
        grad_prob = lax.dot_general(
            v_ref[:span, :], grads, (((1,), (1,)), ((), ())), preferred_element_type=f32
        )
        center = jnp.sum(probs * grad_prob, axis=0, keepdims=True)
        grad_score = (probs * (grad_prob - center)).astype(bf16)
        dv_sum[:span, :] += jnp.dot(probs.astype(bf16), grads, preferred_element_type=f32)
        dk_sum[:span, :] += jnp.dot(grad_score, queries, preferred_element_type=f32)
        wide = jnp.dot(k2t[:, :span], grad_score, preferred_element_type=f32)
        grad_query = join_heads(wide) * HEAD_DIM ** (-0.5)
        dq_ref[here, :] = turn(grad_query, cosine[here, :], -sine[here, :]).astype(bf16)

    @pl.when(pair == pl.num_programs(0) - 1)
    def _():
        keys = dk_sum[...] + pltpu.roll(dk_sum[...], HEAD_DIM, 1)
        dk_ref[...] = turn(keys, cosine, -sine).astype(bf16)
        dv_ref[...] = (dv_sum[...] + pltpu.roll(dv_sum[...], HEAD_DIM, 1)).astype(bf16)


def attend_forward(raw, heads_width, group, bias, cosine, sine):
    rows = raw.shape[0]
    pairs = heads_width // LANES
    own = pairs // 2
    whole = lambda shape: pl.BlockSpec(shape, lambda i: (0, 0))
    column = pl.BlockSpec((rows, LANES), lambda i: (0, i))
    wide = jax.ShapeDtypeStruct((rows, own * LANES), bf16)
    narrow = jax.ShapeDtypeStruct((rows, LANES), bf16)
    return pl.pallas_call(
        functools.partial(forward_kernel, group == 1),
        grid=(own,),
        in_specs=[
            pl.BlockSpec((rows, LANES), lambda i: (0, group * own + i)),
            pl.BlockSpec((rows, LANES), lambda i: (0, pairs)),
            pl.BlockSpec((rows, LANES), lambda i: (0, pairs + 1)),
            whole((rows, rows)),
            whole((rows, LANES)),
            whole((rows, LANES)),
        ],
        out_specs=[
            column,
            column,
            whole((rows, LANES)),
            whole((rows, LANES)),
            pl.BlockSpec((None, 1, 2 * rows), lambda i: (i, 0, 0)),
        ],
        out_shape=[wide, wide, narrow, narrow, jax.ShapeDtypeStruct((own, 1, 2 * rows), f32)],
        scratch_shapes=[pltpu.VMEM((LANES, rows), bf16)],
        compiler_params=pltpu.CompilerParams(vmem_limit_bytes=40 * 1024 * 1024),
        cost_estimate=no_cost(),
        name="attend_forward",
    )(raw, raw, raw, bias, cosine, sine)


def attend_backward(queries, keys, values, grads, bias, cosine, sine, totals):
    rows, width = queries.shape
    whole = lambda shape: pl.BlockSpec(shape, lambda i: (0, 0))
    column = pl.BlockSpec((rows, LANES), lambda i: (0, i))
    narrow = jax.ShapeDtypeStruct((rows, LANES), bf16)
    return pl.pallas_call(
        backward_kernel,
        grid=(width // LANES,),
        in_specs=[
            column,
            whole((rows, LANES)),
            whole((rows, LANES)),
            column,
            whole((rows, rows)),
            whole((rows, LANES)),
            whole((rows, LANES)),
            pl.BlockSpec((None, 1, 2 * rows), lambda i: (i, 0, 0)),
        ],
        out_specs=[column, whole((rows, LANES)), whole((rows, LANES))],
        out_shape=[jax.ShapeDtypeStruct((rows, width), bf16), narrow, narrow],
        scratch_shapes=[
            pltpu.VMEM((LANES, rows), bf16),
            pltpu.VMEM((rows, LANES), f32),
            pltpu.VMEM((rows, LANES), f32),
        ],
        compiler_params=pltpu.CompilerParams(vmem_limit_bytes=40 * 1024 * 1024),
        cost_estimate=no_cost(),
        name="attend_backward",
    )(queries, keys, values, grads, bias, cosine, sine, totals)


def no_cost():
    return pl.CostEstimate(flops=1000000, bytes_accessed=1000000, transcendentals=0)


def whole_block(shape):
    return pl.BlockSpec(shape, lambda i: (0,) * len(shape))


def stack_kernel(*refs):
    out, turned = refs[-2:]
    for index, ref in enumerate(refs[:-2]):

        @pl.when(pl.program_id(0) == index)
        def _():
            value = ref[...]
            out[...] = value
            turned[...] = value.T


def stack_rows(*pieces):
    rows, width = pieces[0].shape
    count = len(pieces)
    kind = pieces[0].dtype
    return pl.pallas_call(
        stack_kernel,
        grid=(count,),
        in_specs=[whole_block((rows, width))] * count,
        out_specs=[
            pl.BlockSpec((rows, width), lambda i: (i, 0)),
            pl.BlockSpec((width, rows), lambda i: (0, i)),
        ],
        out_shape=[
            jax.ShapeDtypeStruct((count * rows, width), kind),
            jax.ShapeDtypeStruct((width, count * rows), kind),
        ],
        compiler_params=pltpu.CompilerParams(vmem_limit_bytes=40 * 1024 * 1024),
        cost_estimate=no_cost(),
        name="stack_rows",
    )(*pieces)


def hidden_kernel(
    rows_ref, grads_ref, gate_ref, up_ref, down_a, down_b, hidden_out, gate_out, up_out
):
    rows, grads = rows_ref[...], grads_ref[...]
    at = down_a.shape[1]
    for down, where in ((down_a, slice(0, at)), (down_b, slice(at, at + down_b.shape[1]))):
        gate = jnp.dot(rows, gate_ref[:, where], preferred_element_type=f32)
        up = jnp.dot(rows, up_ref[:, where], preferred_element_type=f32)
        grad = jnp.dot(grads, down[...], preferred_element_type=f32)
        sigmoid = 1.0 / (1.0 + jnp.exp(-gate))
        silu = gate * sigmoid
        hidden_out[:, where] = (silu * up).astype(bf16)
        gate_out[:, where] = (grad * up * sigmoid * (1.0 + gate * (1.0 - sigmoid))).astype(bf16)
        up_out[:, where] = (grad * silu).astype(bf16)


def hidden_rows(rows, grads, gate, up, down_a, down_b, height):
    total, depth = rows.shape
    width = gate.shape[1]
    tall = pl.BlockSpec((height, depth), lambda i: (i, 0))
    tile = pl.BlockSpec((height, width), lambda i: (i, 0))
    return pl.pallas_call(
        hidden_kernel,
        grid=(total // height,),
        in_specs=[tall, tall] + [whole_block(v.shape) for v in (gate, up, down_a, down_b)],
        out_specs=[tile] * 3,
        out_shape=[jax.ShapeDtypeStruct((total, width), bf16)] * 3,
        compiler_params=pltpu.CompilerParams(vmem_limit_bytes=48 * 1024 * 1024),
        cost_estimate=no_cost(),
        name="hidden_rows",
    )(rows, grads, gate, up, down_a, down_b)


def weight_grad_kernel(
    inner, turned_near, turned_far, near_ref, far_ref,
    grads_near, grads_far, hidden_near, hidden_far, kept, sent,
):
    def product(*pairs):
        return sum(jnp.dot(l[...], r[...], preferred_element_type=f32) for l, r in pairs)

    both = jnp.concatenate(
        [
            product((turned_near, near_ref), (turned_far, far_ref)),
            product((grads_near, hidden_near), (grads_far, hidden_far)),
        ],
        axis=1,
    ).astype(bf16)
    block = kept.shape[-2] * (1 if inner else 2)
    both = both.reshape(-1, 2, block, both.shape[-1])
    kept[...] = both[:, 0].reshape(kept.shape)
    sent[...] = both[:, 1].reshape(sent.shape)


def weight_grads(turned, lefts, grads_turned, hiddens, inner):
    depth, total = turned[0].shape
    block = depth // lax.axis_size("dp")
    high = 512
    count = high // (2 * block)
    width = lefts[0].shape[1] + hiddens[0].shape[1]
    out = pl.BlockSpec((count, block, width), lambda i: (i, 0, 0))
    shape = jax.ShapeDtypeStruct((depth // (2 * block), block, width), bf16)
    tall = pl.BlockSpec((high, total), lambda i: (i, 0))
    kept, sent = pl.pallas_call(
        functools.partial(weight_grad_kernel, inner),
        grid=(depth // high,),
        in_specs=[tall, tall]
        + [whole_block(v.shape) for v in lefts]
        + [tall, tall]
        + [whole_block(v.shape) for v in hiddens],
        out_specs=[out, out],
        out_shape=[shape, shape],
        compiler_params=pltpu.CompilerParams(vmem_limit_bytes=48 * 1024 * 1024),
        cost_estimate=no_cost(),
        name="weight_grads",
    )(*turned, *lefts, *grads_turned, *hiddens)
    dims = [2] * nbits()
    dims[block_axes().index(X if inner else Y)] = 1
    return kept.reshape(*dims, block, width), sent.reshape(*dims, block, width)


def back_kernel(cuts, *refs):
    count = len(cuts)
    weights, (own, other) = refs[len(refs) - 2 - count : len(refs) - 2], refs[-2:]
    lefts = refs[: len(refs) - 2 - count]
    total = 0.0
    for (index, low, high), weight in zip(cuts, weights):
        total += lax.dot_general(
            lefts[index][:, low:high],
            weight[...],
            (((1,), (1,)), ((), ())),
            preferred_element_type=f32,
        )
    half = own.shape[0]
    own[...] = total[:half]
    other[...] = total[half:].astype(bf16)


def back_rows(lefts, weights, cuts):
    rows = lefts[0].shape[0]
    depth = weights[0].shape[0]
    high = 512
    return pl.pallas_call(
        functools.partial(back_kernel, cuts),
        grid=(depth // high,),
        in_specs=[whole_block(v.shape) for v in lefts]
        + [pl.BlockSpec((high, v.shape[1]), lambda i: (i, 0)) for v in weights],
        out_specs=[pl.BlockSpec((rows // 2, high), lambda i: (0, i))] * 2,
        out_shape=[
            jax.ShapeDtypeStruct((rows // 2, depth), f32),
            jax.ShapeDtypeStruct((rows // 2, depth), bf16),
        ],
        compiler_params=pltpu.CompilerParams(vmem_limit_bytes=48 * 1024 * 1024),
        cost_estimate=no_cost(),
        name="back_rows",
    )(*lefts, *weights)


def my_half():
    return (lax.axis_index("dp") >> T) & 1


class Chunks:
    def __init__(self, quarter):
        self.quarter = quarter
        middle = -(-quarter // (2 * LANES)) * LANES
        self.spans = ((0, middle), (middle, quarter))
        self.cuts = [low + (high - low) // (2 * LANES) * LANES for low, high in self.spans]

    def layout(self, index):
        (low, high), at = self.spans[index], self.cuts[index]
        width = high - low
        return (
            (0, low, high, 0),
            (2, low, at, width),
            (1, low, high, width + at - low),
            (2, at, high, 2 * width + at - low),
        )

    def width(self, index):
        low, high = self.spans[index]
        return 3 * (high - low)

    def turn(self, index):
        (low, high), at = self.spans[index], self.cuts[index]
        return high - low + at - low


def pack_kernel(chunks, t_ref, gate_ref, up_ref, down_ref, *outs):
    for side in (0, 1):
        start = jnp.where(side == 0, t_ref[0], 1 - t_ref[0]) * chunks.quarter
        for index in (0, 1):
            out = outs[2 * side + index]
            for matrix, low, high, place in chunks.layout(index):
                where = pl.ds(pl.multiple_of(start + low, LANES), high - low)
                if matrix == 2:
                    value = down_ref[where, :].astype(f32).T.astype(bf16)
                else:
                    value = (gate_ref, up_ref)[matrix][:, where]
                out[:, place : place + high - low] = value


def pack_columns(chunks, gate, up, down):
    rows = gate.shape[0]
    if rows % LANES:
        sides = []
        for side in (0, 1):
            start = jnp.where(side == 0, my_half(), 1 - my_half()) * chunks.quarter
            halves = [
                lax.dynamic_slice_in_dim(v, start, chunks.quarter, 1) for v in (gate, up, down.T)
            ]
            for index in (0, 1):
                parts = sorted(chunks.layout(index), key=lambda entry: entry[3])
                sides.append(jnp.concatenate([halves[m][:, l:h] for m, l, h, _ in parts], axis=1))
        return sides
    whole = pl.BlockSpec(memory_space=pltpu.VMEM)
    shapes = [jax.ShapeDtypeStruct((rows, chunks.width(i)), bf16) for i in (0, 1)]
    return pl.pallas_call(
        functools.partial(pack_kernel, chunks),
        in_specs=[pl.BlockSpec(memory_space=pltpu.SMEM), whole, whole, whole],
        out_specs=[whole] * 4,
        out_shape=shapes + shapes,
        compiler_params=pltpu.CompilerParams(vmem_limit_bytes=40 * 1024 * 1024),
        cost_estimate=no_cost(),
        name="pack_columns",
    )(my_half().reshape(1).astype(jnp.int32), gate, up, down)


def unpack_kernel(chunks, t_ref, *refs):
    outs = refs[4:]
    for side in (0, 1):
        start = jnp.where(side == 0, t_ref[0], 1 - t_ref[0]) * chunks.quarter
        for index in (0, 1):
            for matrix, low, high, place in chunks.layout(index):
                where = pl.ds(pl.multiple_of(start + low, LANES), high - low)
                value = refs[2 * side + index][:, place : place + high - low].astype(f32)
                if matrix == 2:
                    outs[2][where, :] = value.T
                else:
                    outs[matrix][:, where] = value


def unpack_columns(chunks, *bundles):
    rows = bundles[0].shape[0]
    if rows % LANES:
        halves = []
        for side in (0, 1):
            found = [[], [], []]
            for index in (0, 1):
                for matrix, low, high, place in chunks.layout(index):
                    value = bundles[2 * side + index][:, place : place + high - low].astype(f32)
                    found[matrix].append((low, value))
            halves.append(
                [jnp.concatenate([v for _, v in sorted(f, key=lambda e: e[0])], axis=1) for f in found]
            )
        gate, up, down = [
            pick_first(my_half() == 0, own, came, 1) for own, came in zip(*halves)
        ]
        return gate, up, down.T
    whole = pl.BlockSpec(memory_space=pltpu.VMEM)
    flat_shape = jax.ShapeDtypeStruct((rows, 2 * chunks.quarter), f32)
    return pl.pallas_call(
        functools.partial(unpack_kernel, chunks),
        in_specs=[pl.BlockSpec(memory_space=pltpu.SMEM)] + [whole] * 4,
        out_specs=[whole] * 3,
        out_shape=[flat_shape, flat_shape, jax.ShapeDtypeStruct((2 * chunks.quarter, rows), f32)],
        compiler_params=pltpu.CompilerParams(vmem_limit_bytes=40 * 1024 * 1024),
        cost_estimate=no_cost(),
        name="unpack_columns",
    )(my_half().reshape(1).astype(jnp.int32), *bundles)


def body(
    inputs, cotangent, seq_lengths, attn_gain, w_query, w_key, w_value, w_out,
    mlp_gain, w_gate, w_up, w_down,
):
    own_rows = inputs.shape[0]
    chip_rows = 2 * own_rows
    core = lax.axis_index("tensor")
    rest = rest_bits()
    heads_width = w_query.shape[1]
    kv_width = w_key.shape[1]
    cut = (heads_width + 2 * kv_width) // 2
    cut_out = heads_width // 2

    last = []

    def held(values, *others):
        values = after(values, *last, *others)
        last[:] = [values]
        return values

    def did(values):
        last[:] = [values]
        return values

    def send(values, bit, *others):
        return exchange(held(values, *others), bit)

    def swap(values, *others):
        return core_exchange(held(values, *others))

    def gather(values, bit, *others):
        came = send(values, bit, *others)
        return lambda: join(values, held(came), bit)

    def fold(values, bit, kind=bf16):
        came = send(row_major(part(values, bit, 1).astype(bf16)), bit)
        return lambda: add(part(values, bit, 0), held(came), kind)

    gains = as_block(jnp.stack([attn_gain, mlp_gain]))
    gains = gather(gains, rest[0])
    qkv = jnp.concatenate([w_query, w_key, w_value], axis=1)
    q = gather(as_block(qkv), rest[0])
    for bit in rest[1:] + [T]:
        gains = gather(gains(), bit)
    inputs_rel, cotangent_rel = to_relative(held(inputs), cotangent)
    did(inputs_rel)
    gains = gather(gains(), X)
    out_t = did(held(w_out.T))
    gains = gather(gains(), Y)
    o = gather(as_block(out_t), rest[0])
    for bit in rest[1:] + [T]:
        q = gather(q(), bit)
    chunks = Chunks(w_gate.shape[1] // 2)
    own_0, own_1, other_0, other_1 = pack_columns(chunks, held(w_gate), w_up, w_down)
    did(own_0)
    gains = flat(gains()).reshape(-1, 2, attn_gain.shape[0]).transpose(1, 0, 2)
    gains = gains.reshape(2, -1).astype(f32)
    gain_one, gain_two = gains[0], gains[1]
    inputs_wide = inputs_rel.astype(f32)
    scale_one = rms_scale(inputs_wide)
    unit_one = inputs_wide * scale_one
    normed_own = (unit_one * gain_one).astype(bf16)
    normed_other = swap(normed_own)
    for bit in rest[1:] + [T]:
        o = gather(o(), bit)
    position, is_valid, bias = build_layout(seq_lengths[0], chip_rows)
    cosine, sine = rotation_tables(position)
    own_valid = lax.dynamic_slice_in_dim(is_valid, core * own_rows, own_rows, 0)[:, None]
    grad_branch_own = jnp.where(own_valid, cotangent_rel, jnp.zeros_like(cotangent_rel))
    q = q()
    qa = gather(columns(q, 0, cut), X)
    qb = gather(columns(q, cut, 2 * cut), Y)
    w0_t = send(as_block(other_0), T)
    bias = did(held(bias))
    grad_branch_other = swap(grad_branch_own)
    qa = gather(qa(), Y)
    qb = gather(qb(), X)
    w0 = join(as_block(own_0), held(w0_t), T)
    w0 = gather(w0, rest[0])
    for bit in rest[1:]:
        w0 = gather(w0(), bit)
    grad_far_own = send(swap_halves(grad_branch_own), T)
    qa, qb = qa(), qb()
    o = o()
    oa = gather(columns(o, 0, cut_out), X)
    ob = gather(columns(o, cut_out, heads_width), Y)
    query_w = jnp.concatenate([flat(qa), flat(qb)], axis=1)

    normed = pick_first(core == 0, normed_own, normed_other, 0)
    raw = did(matmul(held(normed), query_w))
    tables = (bias, cosine, sine)
    mixed_a, queries_a, keys_a, values_a, totals_a = attend_forward(raw, heads_width, 0, *tables)
    did(mixed_a)
    oa = gather(oa(), Y)
    ob = gather(ob(), X)
    w0 = w0()
    w1_t = send(as_block(other_1), T)
    mixed_b, queries_b, keys_b, values_b, totals_b = attend_forward(
        held(raw), heads_width, 1, *tables
    )
    did(mixed_b)
    grad_far_other = swap(grad_far_own)
    oa, ob = flat(oa()), flat(ob())
    w0b = gather(columns(w0, chunks.turn(0), w0.shape[-1]), Y)
    w0a = gather(columns(w0, 0, chunks.turn(0)), X)
    w1 = join(as_block(own_1), held(w1_t), T)
    w1 = gather(w1, rest[0])

    def rows_of(values, which):
        return lax.dynamic_slice_in_dim(values, which * own_rows, own_rows, 0)

    def project(which, mixed_a):
        return contract_cols(rows_of(mixed_a, which), oa) + contract_cols(
            rows_of(mixed_b, which), ob
        )

    came = swap(project(1 - core, held(mixed_a)).astype(bf16))
    projected = did(project(core, held(mixed_a)))
    w0b, w0a = w0b(), w0a()
    w0b_x = send(w0b, X)
    w0a_y = send(w0a, Y)
    residual = did(inputs_wide + (projected + held(came).astype(f32)))

    scale_two = rms_scale(residual)
    unit_two = residual * scale_two
    normed_mlp_own = (unit_two * gain_two).astype(bf16)
    far_own = send(swap_halves(normed_mlp_own), T)
    near_other = swap(normed_mlp_own)
    grad_near, grad_near_turned = stack_rows(held(grad_branch_own), grad_branch_other)
    did(grad_near)
    grad_far, grad_far_turned = stack_rows(grad_far_own, held(grad_far_other))
    did(grad_far)
    for bit in rest[1:]:
        w1 = gather(w1(), bit)
    w1 = w1()

    def weights_of(first_a, came_a, first_b, came_b, index):
        whole_a = lambda low, high: flat(
            join(columns(first_a, low, high), columns(came_a, low, high), Y)
        )
        whole_b = lambda low, high: flat(
            join(columns(first_b, low, high), columns(came_b, low, high), X)
        )
        width, at = chunks.width(index) // 3, chunks.turn(index)
        return (
            whole_a(0, width), whole_b(0, width),
            whole_a(width, at), whole_b(width, chunks.width(index) - at),
        )

    def hidden_layer(rows, grads, weights):
        hidden, grad_gate, grad_up = hidden_rows(held(rows), grads, *weights, own_rows)
        return did(hidden), grad_gate, grad_up

    def weight_grad(left, right):
        return did(as_blocks(contract_rows(left, held(right)).astype(bf16)))

    def bundle_grads(grads, hiddens, index, inner):
        width = chunks.width(index) // 3
        at = chunks.turn(index) - width
        low, high = (at, width) if inner else (0, at)
        kept, sent = weight_grads(
            (near_turned, far_turned), (held(grads[0]), grads[1]),
            (grad_near_turned, grad_far_turned), [v[:, low:high] for v in hiddens], inner,
        )
        did(sent)
        return kept, sent

    weights_0 = weights_of(w0a, held(w0a_y), w0b, held(w0b_x), 0)
    w1a = gather(columns(w1, 0, chunks.turn(1)), X)
    w1b = gather(columns(w1, chunks.turn(1), w1.shape[-1]), Y)
    far_other = swap(far_own)
    near, near_turned = stack_rows(normed_mlp_own, held(near_other))
    did(near)
    near_0 = hidden_layer(near, grad_near, weights_0)
    far, far_turned = stack_rows(far_own, held(far_other))
    did(far)
    w1a, w1b = w1a(), w1b()
    w1a_y = send(w1a, Y)
    w1b_x = send(w1b, X)
    far_0 = hidden_layer(far, grad_far, weights_0)
    both = lambda index: (near_0[index], far_0[index])
    r0a, r0a_sent = bundle_grads(both(1), both(0), 0, False)
    r0a_y = send(r0a_sent, Y)
    r0b, r0b_sent = bundle_grads(both(2), both(0), 0, True)
    r0b_x = send(r0b_sent, X)
    weights_1 = weights_of(w1a, held(w1a_y), w1b, held(w1b_x), 1)
    weights_hidden = [*weights_0[:2], *weights_1[:2]]
    weights_down = [*weights_0[2:], *weights_1[2:]]
    cuts_hidden = tuple((i, 0, v.shape[1]) for i, v in enumerate(weights_hidden))
    cuts_down = tuple(
        (i, low, high)
        for i in (0, 1)
        for low, high in (
            (0, weights_down[2 * i].shape[1]),
            (weights_down[2 * i].shape[1], weights_hidden[2 * i].shape[1]),
        )
    )

    def hidden_back(first, second):
        lefts = [held(first[1]), first[2], second[1], second[2]]
        own, other = back_rows(lefts, weights_hidden, cuts_hidden)
        return did(own), other

    def branch_back(first, second):
        own, other = back_rows([held(first[0]), second[0]], weights_down, cuts_down)
        return did(own), other

    def pass_on(kept, came, bit):
        came = held(came)
        sent = add(part(kept, bit, 1), part(came, bit, 1))
        return send(sent, bit), (part(kept, bit, 0), part(came, bit, 0))

    def joined(a, a_came, b, b_came):
        totals = [
            sum(v.astype(f32) for v in (*terms, held(came))).astype(bf16)
            for terms, came in ((a, a_came), (b, b_came))
        ]
        return row_major(jnp.concatenate(totals, axis=-1))

    far_1 = hidden_layer(far, grad_far, weights_1)
    far_part, far_sent = hidden_back(far_0, far_1)
    far_came = swap(far_sent)
    near_1 = hidden_layer(near, grad_near, weights_1)
    both_1 = lambda index: (near_1[index], far_1[index])
    r0a_x, r0a = pass_on(r0a, r0a_y, X)
    r0b_y, r0b = pass_on(r0b, r0b_x, Y)
    far_sum = far_part + held(far_came).astype(f32)
    grad_z = send(swap_halves(far_sum.astype(bf16)), T)
    r1a, r1a_sent = bundle_grads(both_1(1), both_1(0), 1, False)
    r1a_y = send(r1a_sent, Y)
    r1b, r1b_sent = bundle_grads(both_1(2), both_1(0), 1, True)
    r1b_x = send(r1b_sent, X)
    near_part, near_sent = hidden_back(near_0, near_1)
    near_came = swap(near_sent)

    r0 = joined(r0a, r0a_x, r0b, r0b_y)
    for bit in rest[:0:-1]:
        r0 = fold(r0, bit)()
    r0 = fold(r0, rest[0], f32)

    grad_normed_mlp = near_part + held(near_came).astype(f32) + held(grad_z).astype(f32)
    grad_gain_two, grad_norm_two = norm_back(grad_normed_mlp, unit_two, scale_two, gain_two)
    grad_residual = grad_branch_own.astype(f32) + grad_norm_two
    grad_att_own = grad_residual.astype(bf16)
    grad_att_other = swap(grad_att_own)
    far_branch, far_branch_sent = branch_back(far_0, far_1)
    far_branch_came = swap(far_branch_sent)
    r1a_x, r1a = pass_on(r1a, r1a_y, X)
    r1b_y, r1b = pass_on(r1b, r1b_x, Y)
    grad_attended = pick_first(core == 0, grad_att_own, held(grad_att_other), 0)
    grad_out_a = weight_grad(grad_attended, mixed_a)
    roa_y = send(row_major(part(grad_out_a, Y, 1)), Y)
    grad_out_b = weight_grad(grad_attended, mixed_b)
    rob_x = send(row_major(part(grad_out_b, X, 1)), X)
    branch_sum = far_branch + held(far_branch_came).astype(f32)
    branch_z = send(swap_halves(branch_sum.astype(bf16)), T)
    d_query_a, d_key_a, d_value_a = attend_backward(
        queries_a, keys_a, values_a, matmul(held(grad_attended), oa).astype(bf16), *tables, totals_a
    )
    did(d_query_a)
    r0 = r0()
    r0_t = send(row_major(part(r0, T, 1).astype(bf16)), T)
    r1 = joined(r1a, r1a_x, r1b, r1b_y)
    for bit in rest[:0:-1]:
        r1 = fold(r1, bit)()
    r1 = fold(r1, rest[0], f32)
    out_a, out_b = part(grad_out_a, Y, 0), part(grad_out_b, X, 0)
    roa_x, out_a = pass_on(out_a, roa_y, X)
    rob_y, out_b = pass_on(out_b, rob_x, Y)
    d_query_b, d_key_b, d_value_b = attend_backward(
        queries_b, keys_b, values_b, matmul(held(grad_attended), ob).astype(bf16), *tables, totals_b
    )
    did(d_query_b)
    low = jnp.arange(kv_width) < HEAD_DIM
    d_qkv = jnp.concatenate(
        [
            d_query_a, d_query_b,
            jnp.where(low, d_key_a, d_key_b), jnp.where(low, d_value_a, d_value_b),
        ],
        axis=1,
    )
    grad_qkv = weight_grad(normed, d_qkv)
    qkv_a, qkv_b = columns(grad_qkv, 0, cut), columns(grad_qkv, cut, 2 * cut)
    rqa_y = send(row_major(part(qkv_a, Y, 1)), Y)
    rqb_x = send(row_major(part(qkv_b, X, 1)), X)
    out = fold(joined(out_a, roa_x, out_b, rob_y), T)
    d_came = swap(contract_cols(rows_of(held(d_qkv), 1 - core), query_w).astype(bf16))
    r1 = r1()
    r1_t = send(row_major(part(r1, T, 1).astype(bf16)), T)
    rqa_x, qkv_a = pass_on(part(qkv_a, Y, 0), rqa_y, X)
    rqb_y, qkv_b = pass_on(part(qkv_b, X, 0), rqb_x, Y)
    grad_normed = contract_cols(rows_of(held(d_qkv), core), query_w) + held(d_came).astype(f32)
    grad_gain_one, grad_norm_one = norm_back(grad_normed, unit_one, scale_one, gain_one)
    grad_rows = did(grad_residual + grad_norm_one)
    grad_gains = jnp.stack([grad_gain_one, grad_gain_two])
    gains_came = swap(grad_gains)
    out = out()
    for bit in rest[:0:-1]:
        out = fold(out, bit)()
    out = fold(out, rest[0], f32)
    near_branch, near_branch_sent = branch_back(near_0, near_1)
    near_branch_came = swap(near_branch_sent)
    r1_t = held(r1_t)
    grad_gains = grad_gains + held(gains_came)
    gain_blocks = grad_gains.reshape(2, lax.axis_size("dp"), -1).transpose(1, 0, 2)
    gain_blocks = gain_blocks.reshape((2,) * nbits() + gain_blocks.shape[1:])

    def fold_gains(blocks, bit):
        came = send(part(blocks, bit, 1), bit)
        return lambda: part(blocks, bit, 0) + held(came)

    gain_blocks = fold_gains(gain_blocks, Y)
    grad_rows = did(from_relative(held(grad_rows))[0])
    sum_qkv = fold(joined(qkv_a, rqa_x, qkv_b, rqb_y), T)
    gain_blocks = fold_gains(gain_blocks(), X)
    branch = near_branch + held(near_branch_came).astype(f32) + held(branch_z).astype(f32)
    output = jnp.where(own_valid, residual + branch, 0.0).astype(bf16)
    output = did(from_relative(output)[0])
    sum_gate, sum_up, sum_down = unpack_columns(
        chunks, flat(part(r0, T, 0)), flat(part(r1, T, 0)), flat(r0_t), held(flat(r1_t))
    )
    did(sum_gate)
    gain_blocks = fold_gains(gain_blocks(), T)
    for bit in rest[:0:-1]:
        sum_qkv = fold(sum_qkv(), bit)
        gain_blocks = fold_gains(gain_blocks(), bit)
    sum_qkv = fold(sum_qkv(), rest[0], f32)
    gain_blocks = fold_gains(gain_blocks(), rest[0])
    out = out()
    sum_qkv = flat(sum_qkv())
    gain_sums = gain_blocks().reshape(2, -1)
    return (
        output,
        grad_rows,
        gain_sums[0],
        sum_qkv[:, :heads_width],
        sum_qkv[:, heads_width : heads_width + kv_width],
        sum_qkv[:, heads_width + kv_width :],
        flat(out).T,
        gain_sums[1],
        sum_gate,
        sum_up,
        sum_down,
    )


def solution(mesh):
    placed = (
        P(("dp", "tensor"), None),
        P(("dp", "tensor"), None),
        P("dp", None),
        P("dp"),
        P("dp", "tensor"),
        P("dp", "tensor"),
        P("dp", "tensor"),
        P("tensor", "dp"),
        P("dp"),
        P("dp", "tensor"),
        P("dp", "tensor"),
        P("tensor", "dp"),
    )
    return jax.shard_map(
        body,
        mesh=mesh,
        in_specs=placed,
        out_specs=(
            P(("dp", "tensor"), None),
            P(("dp", "tensor"), None),
            P("dp"),
            P("dp", "tensor"),
            P("dp", "tensor"),
            P("dp", "tensor"),
            P("tensor", "dp"),
            P("dp"),
            P("dp", "tensor"),
            P("dp", "tensor"),
            P("tensor", "dp"),
        ),
        check_vma=False,
    )
```

```python
import functools

import jax
import jax.numpy as jnp
from jax import lax
from jax.experimental import pallas as pl
from jax.experimental.layout import Layout, with_layout_constraint
from jax.experimental.pallas import tpu as pltpu
from jax.sharding import PartitionSpec as P

HEAD_DIM = 64
BLOCK = 128
LANES = 128

norm_epsilon = 1e-05
rope_base = 10000.0
masked_score = -1e30

bf16 = jnp.bfloat16
f32 = jnp.float32

X, Y, T, Z = 0, 1, 2, 3


def nbits():
    return lax.axis_size("dp").bit_length() - 1


def block_axes():
    return [T] + list(range(nbits() - 1, Z - 1, -1)) + [Y, X]


def rest_bits():
    return list(range(Z, nbits()))


def exchange(values, bit):
    size = lax.axis_size("dp")
    return lax.ppermute(values, "dp", [(i, i ^ (1 << bit)) for i in range(size)])


def core_exchange(values):
    return lax.ppermute(values, "tensor", [(0, 1), (1, 0)])


def as_block(values):
    return values.reshape((1,) * nbits() + values.shape)


def after(values, *others):
    return lax.optimization_barrier((values,) + others)[0] if others else values


def row_major(values):
    return with_layout_constraint(values, Layout(major_to_minor=tuple(range(values.ndim))))


def join(values, came, bit):
    return jnp.concatenate([values, came], axis=block_axes().index(bit))


def part(values, bit, index):
    return lax.slice_in_dim(values, index, index + 1, axis=block_axes().index(bit))


def columns(values, low, high):
    return lax.slice_in_dim(values, low, high, axis=values.ndim - 1)


def add(kept, came, kind=bf16):
    return row_major((kept.astype(f32) + came.astype(f32)).astype(kind))


def flat(blocks):
    return blocks.reshape(-1, blocks.shape[-1])


def as_blocks(rows):
    return rows.reshape((2,) * nbits() + (rows.shape[0] // lax.axis_size("dp"), rows.shape[1]))


def block_mask(place):
    axes = block_axes()
    mask = 0
    for level, bit in enumerate(axes):
        mask |= ((place >> (len(axes) - 1 - level)) & 1) << bit
    return mask


def block_place(mask):
    axes = block_axes()
    place = 0
    for level, bit in enumerate(axes):
        place = place + (((mask >> bit) & 1) << (len(axes) - 1 - level))
    return place


def reorder_kernel(count, offsets, *refs):
    half = len(refs) // 2
    for source, target in zip(refs[:half], refs[half:]):
        for place in range(count):
            start = pl.multiple_of(offsets[place], LANES)
            target[:, place * LANES : (place + 1) * LANES] = source[:, pl.ds(start, LANES)]


def reorder(arrays, places):
    count = len(places)
    rows, columns = arrays[0].shape
    width = columns // count
    if width % LANES:
        return [
            jnp.concatenate(
                [lax.dynamic_slice_in_dim(v, p * width, width, 1) for p in places], axis=1
            )
            for v in arrays
        ]
    spec = pl.BlockSpec((BLOCK, columns), lambda i, offsets: (i, 0))
    return pl.pallas_call(
        functools.partial(reorder_kernel, count),
        grid_spec=pltpu.PrefetchScalarGridSpec(
            num_scalar_prefetch=1,
            grid=(rows // BLOCK,),
            in_specs=[spec] * len(arrays),
            out_specs=[spec] * len(arrays),
        ),
        out_shape=[jax.ShapeDtypeStruct(v.shape, v.dtype) for v in arrays],
        compiler_params=pltpu.CompilerParams(vmem_limit_bytes=32 * 1024 * 1024),
        cost_estimate=no_cost(),
        name="reorder",
    )(jnp.stack(places).astype(jnp.int32) * width, *arrays)


def to_relative(*arrays):
    me = lax.axis_index("dp")
    return reorder(arrays, [me ^ block_mask(place) for place in range(lax.axis_size("dp"))])


def from_relative(*arrays):
    me = lax.axis_index("dp")
    return reorder(arrays, [block_place(me ^ index) for index in range(lax.axis_size("dp"))])


def swap_halves(values):
    half = values.shape[1] // 2
    return jnp.concatenate([values[:, half:], values[:, :half]], axis=1)


def pick_first(flag, first, second, axis):
    return jnp.concatenate(
        [jnp.where(flag, first, second), jnp.where(flag, second, first)], axis=axis
    )


def build_layout(lengths, total_rows):
    block_counts = (lengths + BLOCK - 1) // BLOCK
    seq_ends = jnp.cumsum(block_counts, dtype=jnp.int32) * BLOCK
    seq_starts = seq_ends - block_counts * BLOCK
    row_ids = jnp.arange(total_rows, dtype=jnp.int32)
    membership = (
        (row_ids[:, None] >= seq_starts[None, :]) & (row_ids[:, None] < seq_ends[None, :])
    ).astype(jnp.int32)
    slot_ids = jnp.arange(lengths.shape[0], dtype=jnp.int32)
    segment = jnp.sum(membership * (slot_ids[None, :] + 1), axis=1, dtype=jnp.int32) - 1
    first_row = jnp.sum(membership * seq_starts[None, :], axis=1, dtype=jnp.int32)
    seq_limit = jnp.sum(membership * lengths[None, :], axis=1, dtype=jnp.int32)
    position = row_ids - first_row
    is_valid = (segment >= 0) & (position < seq_limit)
    allowed = (
        (segment[:, None] == segment[None, :])
        & (segment[:, None] >= 0)
        & (position[:, None] <= position[None, :])
        & is_valid[:, None]
    )
    allowed = allowed | (row_ids[:, None] == row_ids[None, :])
    bias = jnp.where(allowed, 0.0, masked_score).astype(f32)
    return position, is_valid, bias


def rotation_tables(position):
    half_dim = HEAD_DIM // 2
    lane = jnp.arange(LANES, dtype=jnp.int32)
    frequency = rope_base ** (-2.0 * (lane % half_dim).astype(f32) / HEAD_DIM)
    angles = position.astype(f32)[:, None] * frequency[None, :]
    sign = jnp.where(lane % HEAD_DIM < half_dim, -1.0, 1.0).astype(f32)
    return jnp.cos(angles), jnp.sin(angles) * sign[None, :]


def matmul(left, right):
    return jnp.dot(left, right, preferred_element_type=f32)


def contract_rows(left, right):
    return lax.dot_general(left, right, (((0,), (0,)), ((), ())), preferred_element_type=f32)


def contract_cols(left, right):
    return lax.dot_general(left, right, (((1,), (1,)), ((), ())), preferred_element_type=f32)


def rms_scale(values):
    return lax.rsqrt(jnp.mean(values * values, axis=-1, keepdims=True) + norm_epsilon)


def norm_back(grad_normed, unit_rows, row_scale, gain):
    scaled = grad_normed * gain
    grad_gain = jnp.sum(grad_normed * unit_rows, axis=0)
    grad_rows = row_scale * (
        scaled - unit_rows * jnp.mean(scaled * unit_rows, axis=-1, keepdims=True)
    )
    return grad_gain, grad_rows


def turn(values, cosine, sine):
    lane = lax.broadcasted_iota(jnp.int32, values.shape, 1)
    half_dim = HEAD_DIM // 2
    partner = jnp.where(
        lane % HEAD_DIM < half_dim,
        pltpu.roll(values, LANES - half_dim, 1),
        pltpu.roll(values, half_dim, 1),
    )
    return values * cosine + partner * sine


def doubled(values, second):
    lane = lax.broadcasted_iota(jnp.int32, values.shape, 1)
    rolled = pltpu.roll(values, HEAD_DIM, 1)
    low = lane < HEAD_DIM
    return jnp.where(second, jnp.where(low, rolled, values), jnp.where(low, values, rolled))


def split_heads(pair):
    lane = lax.broadcasted_iota(jnp.int32, pair.shape, 1)
    zero = jnp.zeros_like(pair)
    return jnp.concatenate(
        [jnp.where(lane < HEAD_DIM, pair, zero), jnp.where(lane < HEAD_DIM, zero, pair)], axis=0
    )


def join_heads(wide):
    row = lax.broadcasted_iota(jnp.int32, (LANES, BLOCK), 0)
    return jnp.where(row < HEAD_DIM, wide[:, :BLOCK], wide[:, BLOCK:]).T


def forward_kernel(
    second, q_ref, k_ref, v_ref, bias_ref, cos_ref, sin_ref,
    out_ref, turned_ref, keys_ref, values_ref, total_ref, v2t,
):
    rows = q_ref.shape[0]
    cosine, sine = cos_ref[...], sin_ref[...]

    @pl.when(pl.program_id(0) == 0)
    def _():
        keys = turn(k_ref[...], cosine, sine).astype(bf16).astype(f32)
        keys_ref[...] = doubled(keys, second).astype(bf16)
        values = doubled(v_ref[...], second)
        values_ref[...] = values.astype(bf16)
        v2t[...] = values.T.astype(bf16)

    turned_ref[...] = (turn(q_ref[...], cosine, sine) * HEAD_DIM ** (-0.5)).astype(bf16)
    for index in range(rows // BLOCK):
        span = (index + 1) * BLOCK
        here = slice(index * BLOCK, span)
        queries = split_heads(turned_ref[here, :])
        scores = lax.dot_general(
            keys_ref[:span, :], queries, (((1,), (1,)), ((), ())), preferred_element_type=f32
        )
        bias = bias_ref[:span, here]
        scores = scores + jnp.concatenate([bias, bias], axis=1)
        top = jnp.max(scores, axis=0, keepdims=True)
        weights = jnp.exp(scores - top)
        total = jnp.sum(weights, axis=0, keepdims=True)
        weights = (weights * (1.0 / total)).astype(bf16)
        mixed = jnp.dot(v2t[:, :span], weights, preferred_element_type=f32)
        out_ref[here, :] = join_heads(mixed).astype(bf16)
        total_ref[:, 2 * index * BLOCK : 2 * span] = top + jnp.log(total)


def backward_kernel(
    q_ref, k_ref, v_ref, grad_ref, bias_ref, cos_ref, sin_ref, total_ref,
    dq_ref, dk_ref, dv_ref, k2t, dk_sum, dv_sum,
):
    pair = pl.program_id(0)
    rows = q_ref.shape[0]
    cosine, sine = cos_ref[...], sin_ref[...]

    @pl.when(pair == 0)
    def _():
        k2t[...] = k_ref[...].astype(f32).T.astype(bf16)
        dk_sum[...] = jnp.zeros_like(dk_sum)
        dv_sum[...] = jnp.zeros_like(dv_sum)

    for index in range(rows // BLOCK):
        span = (index + 1) * BLOCK
        here = slice(index * BLOCK, span)
        queries = split_heads(q_ref[here, :])
        grads = split_heads(grad_ref[here, :])
        scores = lax.dot_general(
            k_ref[:span, :], queries, (((1,), (1,)), ((), ())), preferred_element_type=f32
        )
        bias = bias_ref[:span, here]
        scores = scores + jnp.concatenate([bias, bias], axis=1)
        probs = jnp.exp(scores - total_ref[:, 2 * index * BLOCK : 2 * span])
        grad_prob = lax.dot_general(
            v_ref[:span, :], grads, (((1,), (1,)), ((), ())), preferred_element_type=f32
        )
        center = jnp.sum(probs * grad_prob, axis=0, keepdims=True)
        grad_score = (probs * (grad_prob - center)).astype(bf16)
        dv_sum[:span, :] += jnp.dot(probs.astype(bf16), grads, preferred_element_type=f32)
        dk_sum[:span, :] += jnp.dot(grad_score, queries, preferred_element_type=f32)
        wide = jnp.dot(k2t[:, :span], grad_score, preferred_element_type=f32)
        grad_query = join_heads(wide) * HEAD_DIM ** (-0.5)
        dq_ref[here, :] = turn(grad_query, cosine[here, :], -sine[here, :]).astype(bf16)

    @pl.when(pair == pl.num_programs(0) - 1)
    def _():
        keys = dk_sum[...] + pltpu.roll(dk_sum[...], HEAD_DIM, 1)
        dk_ref[...] = turn(keys, cosine, -sine).astype(bf16)
        dv_ref[...] = (dv_sum[...] + pltpu.roll(dv_sum[...], HEAD_DIM, 1)).astype(bf16)


def attend_forward(raw, heads_width, group, bias, cosine, sine):
    rows = raw.shape[0]
    pairs = heads_width // LANES
    own = pairs // 2
    whole = lambda shape: pl.BlockSpec(shape, lambda i: (0, 0))
    column = pl.BlockSpec((rows, LANES), lambda i: (0, i))
    wide = jax.ShapeDtypeStruct((rows, own * LANES), bf16)
    narrow = jax.ShapeDtypeStruct((rows, LANES), bf16)
    return pl.pallas_call(
        functools.partial(forward_kernel, group == 1),
        grid=(own,),
        in_specs=[
            pl.BlockSpec((rows, LANES), lambda i: (0, group * own + i)),
            pl.BlockSpec((rows, LANES), lambda i: (0, pairs)),
            pl.BlockSpec((rows, LANES), lambda i: (0, pairs + 1)),
            whole((rows, rows)),
            whole((rows, LANES)),
            whole((rows, LANES)),
        ],
        out_specs=[
            column,
            column,
            whole((rows, LANES)),
            whole((rows, LANES)),
            pl.BlockSpec((None, 1, 2 * rows), lambda i: (i, 0, 0)),
        ],
        out_shape=[wide, wide, narrow, narrow, jax.ShapeDtypeStruct((own, 1, 2 * rows), f32)],
        scratch_shapes=[pltpu.VMEM((LANES, rows), bf16)],
        compiler_params=pltpu.CompilerParams(vmem_limit_bytes=40 * 1024 * 1024),
        cost_estimate=no_cost(),
        name="attend_forward",
    )(raw, raw, raw, bias, cosine, sine)


def attend_backward(queries, keys, values, grads, bias, cosine, sine, totals):
    rows, width = queries.shape
    whole = lambda shape: pl.BlockSpec(shape, lambda i: (0, 0))
    column = pl.BlockSpec((rows, LANES), lambda i: (0, i))
    narrow = jax.ShapeDtypeStruct((rows, LANES), bf16)
    return pl.pallas_call(
        backward_kernel,
        grid=(width // LANES,),
        in_specs=[
            column,
            whole((rows, LANES)),
            whole((rows, LANES)),
            column,
            whole((rows, rows)),
            whole((rows, LANES)),
            whole((rows, LANES)),
            pl.BlockSpec((None, 1, 2 * rows), lambda i: (i, 0, 0)),
        ],
        out_specs=[column, whole((rows, LANES)), whole((rows, LANES))],
        out_shape=[jax.ShapeDtypeStruct((rows, width), bf16), narrow, narrow],
        scratch_shapes=[
            pltpu.VMEM((LANES, rows), bf16),
            pltpu.VMEM((rows, LANES), f32),
            pltpu.VMEM((rows, LANES), f32),
        ],
        compiler_params=pltpu.CompilerParams(vmem_limit_bytes=40 * 1024 * 1024),
        cost_estimate=no_cost(),
        name="attend_backward",
    )(queries, keys, values, grads, bias, cosine, sine, totals)


def no_cost(hint=1):
    return pl.CostEstimate(flops=hint * 1000000, bytes_accessed=1000000, transcendentals=0)


def whole_block(shape):
    return pl.BlockSpec(shape, lambda i: (0,) * len(shape))


def stack_kernel(*refs):
    out, turned = refs[-2:]
    for index, ref in enumerate(refs[:-2]):

        @pl.when(pl.program_id(0) == index)
        def _():
            value = ref[...]
            out[...] = value
            turned[...] = value.T


def stack_rows(*pieces):
    rows, width = pieces[0].shape
    count = len(pieces)
    kind = pieces[0].dtype
    return pl.pallas_call(
        stack_kernel,
        grid=(count,),
        in_specs=[whole_block((rows, width))] * count,
        out_specs=[
            pl.BlockSpec((rows, width), lambda i: (i, 0)),
            pl.BlockSpec((width, rows), lambda i: (0, i)),
        ],
        out_shape=[
            jax.ShapeDtypeStruct((count * rows, width), kind),
            jax.ShapeDtypeStruct((width, count * rows), kind),
        ],
        compiler_params=pltpu.CompilerParams(vmem_limit_bytes=40 * 1024 * 1024),
        cost_estimate=no_cost(),
        name="stack_rows",
    )(*pieces)


def join_kernel(block, first_a, came_a, first_b, came_b, gate, up, down_a, down_b):
    def whole(first, came, size):
        shape = (-1, size, first.shape[1])
        both = jnp.concatenate([first[...].reshape(shape), came[...].reshape(shape)], axis=1)
        return both.reshape(-1, first.shape[1])

    width = gate.shape[1]
    both_a = whole(first_a, came_a, 2 * block)
    gate[...] = both_a[:, :width]
    down_a[...] = both_a[:, width:]
    both_b = whole(first_b, came_b, block)
    up[...] = both_b[:, :width]
    down_b[...] = both_b[:, width:]


def join_weights(first_a, came_a, first_b, came_b, width):
    high = 512
    arrays = [flat(v) for v in (first_a, came_a, first_b, came_b)]
    depth = 2 * arrays[0].shape[0]
    widths = (width, width, arrays[0].shape[1] - width, arrays[2].shape[1] - width)
    return pl.pallas_call(
        functools.partial(join_kernel, depth // lax.axis_size("dp")),
        grid=(depth // high,),
        in_specs=[pl.BlockSpec((high // 2, v.shape[1]), lambda i: (i, 0)) for v in arrays],
        out_specs=[pl.BlockSpec((high, w), lambda i: (i, 0)) for w in widths],
        out_shape=[jax.ShapeDtypeStruct((depth, w), bf16) for w in widths],
        compiler_params=pltpu.CompilerParams(vmem_limit_bytes=40 * 1024 * 1024),
        cost_estimate=no_cost(20000),
        name="join_weights",
    )(*arrays)


def hidden_kernel(
    rows_ref, grads_ref, gate_ref, up_ref, down_a, down_b, hidden_out, gate_out, up_out
):
    rows, grads = rows_ref[...], grads_ref[...]
    at = down_a.shape[1]
    for down, where in ((down_a, slice(0, at)), (down_b, slice(at, at + down_b.shape[1]))):
        gate = jnp.dot(rows, gate_ref[:, where], preferred_element_type=f32)
        up = jnp.dot(rows, up_ref[:, where], preferred_element_type=f32)
        grad = jnp.dot(grads, down[...], preferred_element_type=f32)
        sigmoid = 1.0 / (1.0 + jnp.exp(-gate))
        silu = gate * sigmoid
        hidden_out[:, where] = (silu * up).astype(bf16)
        gate_out[:, where] = (grad * up * sigmoid * (1.0 + gate * (1.0 - sigmoid))).astype(bf16)
        up_out[:, where] = (grad * silu).astype(bf16)


def hidden_rows(rows, grads, gate, up, down_a, down_b, height):
    total, depth = rows.shape
    width = gate.shape[1]
    tall = pl.BlockSpec((height, depth), lambda i: (i, 0))
    tile = pl.BlockSpec((height, width), lambda i: (i, 0))
    return pl.pallas_call(
        hidden_kernel,
        grid=(total // height,),
        in_specs=[tall, tall] + [whole_block(v.shape) for v in (gate, up, down_a, down_b)],
        out_specs=[tile] * 3,
        out_shape=[jax.ShapeDtypeStruct((total, width), bf16)] * 3,
        compiler_params=pltpu.CompilerParams(vmem_limit_bytes=48 * 1024 * 1024),
        cost_estimate=no_cost(),
        name="hidden_rows",
    )(rows, grads, gate, up, down_a, down_b)


def weight_grad_kernel(
    inner, turned_near, turned_far, near_ref, far_ref,
    grads_near, grads_far, hidden_near, hidden_far, kept, sent,
):
    def product(*pairs):
        return sum(jnp.dot(l[...], r[...], preferred_element_type=f32) for l, r in pairs)

    both = jnp.concatenate(
        [
            product((turned_near, near_ref), (turned_far, far_ref)),
            product((grads_near, hidden_near), (grads_far, hidden_far)),
        ],
        axis=1,
    ).astype(bf16)
    block = kept.shape[-2] * (1 if inner else 2)
    both = both.reshape(-1, 2, block, both.shape[-1])
    kept[...] = both[:, 0].reshape(kept.shape)
    sent[...] = both[:, 1].reshape(sent.shape)


def weight_grads(turned, lefts, grads_turned, hiddens, inner):
    depth, total = turned[0].shape
    block = depth // lax.axis_size("dp")
    high = 512
    count = high // (2 * block)
    width = lefts[0].shape[1] + hiddens[0].shape[1]
    out = pl.BlockSpec((count, block, width), lambda i: (i, 0, 0))
    shape = jax.ShapeDtypeStruct((depth // (2 * block), block, width), bf16)
    tall = pl.BlockSpec((high, total), lambda i: (i, 0))
    kept, sent = pl.pallas_call(
        functools.partial(weight_grad_kernel, inner),
        grid=(depth // high,),
        in_specs=[tall, tall]
        + [whole_block(v.shape) for v in lefts]
        + [tall, tall]
        + [whole_block(v.shape) for v in hiddens],
        out_specs=[out, out],
        out_shape=[shape, shape],
        compiler_params=pltpu.CompilerParams(vmem_limit_bytes=48 * 1024 * 1024),
        cost_estimate=no_cost(),
        name="weight_grads",
    )(*turned, *lefts, *grads_turned, *hiddens)
    dims = [2] * nbits()
    dims[block_axes().index(X if inner else Y)] = 1
    return kept.reshape(*dims, block, width), sent.reshape(*dims, block, width)


def back_kernel(cuts, *refs):
    count = len(cuts)
    weights, (own, other) = refs[len(refs) - 2 - count : len(refs) - 2], refs[-2:]
    lefts = refs[: len(refs) - 2 - count]
    total = 0.0
    for (index, low, high), weight in zip(cuts, weights):
        total += lax.dot_general(
            lefts[index][:, low:high],
            weight[...],
            (((1,), (1,)), ((), ())),
            preferred_element_type=f32,
        )
    half = own.shape[0]
    own[...] = total[:half]
    other[...] = total[half:].astype(bf16)


def back_rows(lefts, weights, cuts):
    rows = lefts[0].shape[0]
    depth = weights[0].shape[0]
    high = 512
    return pl.pallas_call(
        functools.partial(back_kernel, cuts),
        grid=(depth // high,),
        in_specs=[whole_block(v.shape) for v in lefts]
        + [pl.BlockSpec((high, v.shape[1]), lambda i: (i, 0)) for v in weights],
        out_specs=[pl.BlockSpec((rows // 2, high), lambda i: (0, i))] * 2,
        out_shape=[
            jax.ShapeDtypeStruct((rows // 2, depth), f32),
            jax.ShapeDtypeStruct((rows // 2, depth), bf16),
        ],
        compiler_params=pltpu.CompilerParams(vmem_limit_bytes=48 * 1024 * 1024),
        cost_estimate=no_cost(),
        name="back_rows",
    )(*lefts, *weights)


def my_half():
    return (lax.axis_index("dp") >> T) & 1


class Chunks:
    def __init__(self, quarter):
        self.quarter = quarter
        middle = -(-quarter // (2 * LANES)) * LANES
        self.spans = ((0, middle), (middle, quarter))
        self.cuts = [low + (high - low) // (2 * LANES) * LANES for low, high in self.spans]

    def layout(self, index):
        (low, high), at = self.spans[index], self.cuts[index]
        width = high - low
        return (
            (0, low, high, 0),
            (2, low, at, width),
            (1, low, high, width + at - low),
            (2, at, high, 2 * width + at - low),
        )

    def width(self, index):
        low, high = self.spans[index]
        return 3 * (high - low)

    def turn(self, index):
        (low, high), at = self.spans[index], self.cuts[index]
        return high - low + at - low


def pack_kernel(chunks, t_ref, gate_ref, up_ref, down_ref, *outs):
    for side in (0, 1):
        start = jnp.where(side == 0, t_ref[0], 1 - t_ref[0]) * chunks.quarter
        for index in (0, 1):
            out = outs[2 * side + index]
            for matrix, low, high, place in chunks.layout(index):
                where = pl.ds(pl.multiple_of(start + low, LANES), high - low)
                if matrix == 2:
                    value = down_ref[where, :].astype(f32).T.astype(bf16)
                else:
                    value = (gate_ref, up_ref)[matrix][:, where]
                out[:, place : place + high - low] = value


def pack_columns(chunks, gate, up, down):
    rows = gate.shape[0]
    if rows % LANES:
        sides = []
        for side in (0, 1):
            start = jnp.where(side == 0, my_half(), 1 - my_half()) * chunks.quarter
            halves = [
                lax.dynamic_slice_in_dim(v, start, chunks.quarter, 1) for v in (gate, up, down.T)
            ]
            for index in (0, 1):
                parts = sorted(chunks.layout(index), key=lambda entry: entry[3])
                sides.append(jnp.concatenate([halves[m][:, l:h] for m, l, h, _ in parts], axis=1))
        return sides
    whole = pl.BlockSpec(memory_space=pltpu.VMEM)
    shapes = [jax.ShapeDtypeStruct((rows, chunks.width(i)), bf16) for i in (0, 1)]
    return pl.pallas_call(
        functools.partial(pack_kernel, chunks),
        in_specs=[pl.BlockSpec(memory_space=pltpu.SMEM), whole, whole, whole],
        out_specs=[whole] * 4,
        out_shape=shapes + shapes,
        compiler_params=pltpu.CompilerParams(vmem_limit_bytes=40 * 1024 * 1024),
        cost_estimate=no_cost(),
        name="pack_columns",
    )(my_half().reshape(1).astype(jnp.int32), gate, up, down)


def unpack_kernel(chunks, t_ref, *refs):
    outs = refs[4:]
    for side in (0, 1):
        start = jnp.where(side == 0, t_ref[0], 1 - t_ref[0]) * chunks.quarter
        for index in (0, 1):
            for matrix, low, high, place in chunks.layout(index):
                where = pl.ds(pl.multiple_of(start + low, LANES), high - low)
                value = refs[2 * side + index][:, place : place + high - low].astype(f32)
                if matrix == 2:
                    outs[2][where, :] = value.T
                else:
                    outs[matrix][:, where] = value


def unpack_columns(chunks, *bundles):
    rows = bundles[0].shape[0]
    if rows % LANES:
        halves = []
        for side in (0, 1):
            found = [[], [], []]
            for index in (0, 1):
                for matrix, low, high, place in chunks.layout(index):
                    value = bundles[2 * side + index][:, place : place + high - low].astype(f32)
                    found[matrix].append((low, value))
            halves.append(
                [jnp.concatenate([v for _, v in sorted(f, key=lambda e: e[0])], axis=1) for f in found]
            )
        gate, up, down = [
            pick_first(my_half() == 0, own, came, 1) for own, came in zip(*halves)
        ]
        return gate, up, down.T
    whole = pl.BlockSpec(memory_space=pltpu.VMEM)
    flat_shape = jax.ShapeDtypeStruct((rows, 2 * chunks.quarter), f32)
    return pl.pallas_call(
        functools.partial(unpack_kernel, chunks),
        in_specs=[pl.BlockSpec(memory_space=pltpu.SMEM)] + [whole] * 4,
        out_specs=[whole] * 3,
        out_shape=[flat_shape, flat_shape, jax.ShapeDtypeStruct((2 * chunks.quarter, rows), f32)],
        compiler_params=pltpu.CompilerParams(vmem_limit_bytes=40 * 1024 * 1024),
        cost_estimate=no_cost(),
        name="unpack_columns",
    )(my_half().reshape(1).astype(jnp.int32), *bundles)


def body(
    inputs, cotangent, seq_lengths, attn_gain, w_query, w_key, w_value, w_out,
    mlp_gain, w_gate, w_up, w_down,
):
    own_rows = inputs.shape[0]
    chip_rows = 2 * own_rows
    core = lax.axis_index("tensor")
    rest = rest_bits()
    heads_width = w_query.shape[1]
    kv_width = w_key.shape[1]
    cut = (heads_width + 2 * kv_width) // 2
    cut_out = heads_width // 2

    last = []

    def held(values, *others):
        values = after(values, *last, *others)
        last[:] = [values]
        return values

    def did(values):
        last[:] = [values]
        return values

    def send(values, bit, *others):
        return exchange(held(values, *others), bit)

    def swap(values, *others):
        return core_exchange(held(values, *others))

    def gather(values, bit, *others):
        came = send(values, bit, *others)
        return lambda: join(values, held(came), bit)

    def fold(values, bit, kind=bf16):
        came = send(row_major(part(values, bit, 1).astype(bf16)), bit)
        return lambda: add(part(values, bit, 0), held(came), kind)

    gains = as_block(jnp.stack([attn_gain, mlp_gain]))
    gains = gather(gains, rest[0])
    qkv = jnp.concatenate([w_query, w_key, w_value], axis=1)
    q = gather(as_block(qkv), rest[0])
    for bit in rest[1:] + [T]:
        gains = gather(gains(), bit)
    inputs_rel, cotangent_rel = to_relative(held(inputs), cotangent)
    did(inputs_rel)
    gains = gather(gains(), X)
    out_t = did(held(w_out.T))
    gains = gather(gains(), Y)
    o = gather(as_block(out_t), rest[0])
    for bit in rest[1:] + [T]:
        q = gather(q(), bit)
    chunks = Chunks(w_gate.shape[1] // 2)
    own_0, own_1, other_0, other_1 = pack_columns(chunks, held(w_gate), w_up, w_down)
    did(own_0)
    gains = flat(gains()).reshape(-1, 2, attn_gain.shape[0]).transpose(1, 0, 2)
    gains = gains.reshape(2, -1).astype(f32)
    gain_one, gain_two = gains[0], gains[1]
    inputs_wide = inputs_rel.astype(f32)
    scale_one = rms_scale(inputs_wide)
    unit_one = inputs_wide * scale_one
    normed_own = (unit_one * gain_one).astype(bf16)
    normed_other = swap(normed_own)
    for bit in rest[1:] + [T]:
        o = gather(o(), bit)
    position, is_valid, bias = build_layout(seq_lengths[0], chip_rows)
    cosine, sine = rotation_tables(position)
    own_valid = lax.dynamic_slice_in_dim(is_valid, core * own_rows, own_rows, 0)[:, None]
    grad_branch_own = jnp.where(own_valid, cotangent_rel, jnp.zeros_like(cotangent_rel))
    q = q()
    qa = gather(columns(q, 0, cut), X)
    qb = gather(columns(q, cut, 2 * cut), Y)
    w0_t = send(as_block(other_0), T)
    bias = did(held(bias))
    grad_branch_other = swap(grad_branch_own)
    qa = gather(qa(), Y)
    qb = gather(qb(), X)
    w0 = join(as_block(own_0), held(w0_t), T)
    w0 = gather(w0, rest[0])
    for bit in rest[1:]:
        w0 = gather(w0(), bit)
    grad_far_own = send(swap_halves(grad_branch_own), T)
    qa, qb = qa(), qb()
    o = o()
    oa = gather(columns(o, 0, cut_out), X)
    ob = gather(columns(o, cut_out, heads_width), Y)
    query_w = jnp.concatenate([flat(qa), flat(qb)], axis=1)

    normed = pick_first(core == 0, normed_own, normed_other, 0)
    raw = did(matmul(held(normed), query_w))
    tables = (bias, cosine, sine)
    mixed_a, queries_a, keys_a, values_a, totals_a = attend_forward(raw, heads_width, 0, *tables)
    did(mixed_a)
    oa = gather(oa(), Y)
    ob = gather(ob(), X)
    w0 = w0()
    w1_t = send(as_block(other_1), T)
    mixed_b, queries_b, keys_b, values_b, totals_b = attend_forward(
        held(raw), heads_width, 1, *tables
    )
    did(mixed_b)
    grad_far_other = swap(grad_far_own)
    oa, ob = flat(oa()), flat(ob())
    w0b = gather(columns(w0, chunks.turn(0), w0.shape[-1]), Y)
    w0a = gather(columns(w0, 0, chunks.turn(0)), X)
    w1 = join(as_block(own_1), held(w1_t), T)
    w1 = gather(w1, rest[0])

    def rows_of(values, which):
        return lax.dynamic_slice_in_dim(values, which * own_rows, own_rows, 0)

    def project(which, mixed_a):
        return contract_cols(rows_of(mixed_a, which), oa) + contract_cols(
            rows_of(mixed_b, which), ob
        )

    came = swap(project(1 - core, held(mixed_a)).astype(bf16))
    projected = did(project(core, held(mixed_a)))
    w0b, w0a = w0b(), w0a()
    w0b_x = send(w0b, X)
    w0a_y = send(w0a, Y)
    residual = did(inputs_wide + (projected + held(came).astype(f32)))

    scale_two = rms_scale(residual)
    unit_two = residual * scale_two
    normed_mlp_own = (unit_two * gain_two).astype(bf16)
    far_own = send(swap_halves(normed_mlp_own), T)
    near_other = swap(normed_mlp_own)
    grad_near, grad_near_turned = stack_rows(held(grad_branch_own), grad_branch_other)
    did(grad_near)
    grad_far, grad_far_turned = stack_rows(grad_far_own, held(grad_far_other))
    did(grad_far)
    for bit in rest[1:]:
        w1 = gather(w1(), bit)
    w1 = w1()

    def weights_of(first_a, came_a, first_b, came_b, index):
        width = chunks.width(index) // 3
        return join_weights(first_a, came_a, first_b, held(came_b), width)

    def hidden_layer(rows, grads, weights):
        hidden, grad_gate, grad_up = hidden_rows(held(rows), grads, *weights, own_rows)
        return did(hidden), grad_gate, grad_up

    def weight_grad(left, right):
        return did(as_blocks(contract_rows(left, held(right)).astype(bf16)))

    def bundle_grads(grads, hiddens, index, inner):
        width = chunks.width(index) // 3
        at = chunks.turn(index) - width
        low, high = (at, width) if inner else (0, at)
        kept, sent = weight_grads(
            (near_turned, far_turned), (held(grads[0]), grads[1]),
            (grad_near_turned, grad_far_turned), [v[:, low:high] for v in hiddens], inner,
        )
        did(sent)
        return kept, sent

    weights_0 = weights_of(w0a, held(w0a_y), w0b, w0b_x, 0)
    w1a = gather(columns(w1, 0, chunks.turn(1)), X)
    w1b = gather(columns(w1, chunks.turn(1), w1.shape[-1]), Y)
    far_other = swap(far_own)
    near, near_turned = stack_rows(normed_mlp_own, held(near_other))
    did(near)
    near_0 = hidden_layer(near, grad_near, weights_0)
    far, far_turned = stack_rows(far_own, held(far_other))
    did(far)
    w1a, w1b = w1a(), w1b()
    w1a_y = send(w1a, Y)
    w1b_x = send(w1b, X)
    far_0 = hidden_layer(far, grad_far, weights_0)
    both = lambda index: (near_0[index], far_0[index])
    r0a, r0a_sent = bundle_grads(both(1), both(0), 0, False)
    r0a_y = send(r0a_sent, Y)
    r0b, r0b_sent = bundle_grads(both(2), both(0), 0, True)
    r0b_x = send(r0b_sent, X)
    w1a_y, w1b_x = held(w1a_y), held(w1b_x)
    weights_1 = weights_of(w1a, w1a_y, w1b, w1b_x, 1)
    weights_hidden = [*weights_0[:2], *weights_1[:2]]
    weights_down = [*weights_0[2:], *weights_1[2:]]
    cuts_hidden = tuple((i, 0, v.shape[1]) for i, v in enumerate(weights_hidden))
    cuts_down = tuple(
        (i, low, high)
        for i in (0, 1)
        for low, high in (
            (0, weights_down[2 * i].shape[1]),
            (weights_down[2 * i].shape[1], weights_hidden[2 * i].shape[1]),
        )
    )

    def hidden_back(first, second):
        lefts = [held(first[1]), first[2], second[1], second[2]]
        own, other = back_rows(lefts, weights_hidden, cuts_hidden)
        return did(own), other

    def branch_back(first, second):
        own, other = back_rows([held(first[0]), second[0]], weights_down, cuts_down)
        return did(own), other

    def pass_on(kept, came, bit):
        came = held(came)
        sent = add(part(kept, bit, 1), part(came, bit, 1))
        return send(sent, bit), (part(kept, bit, 0), part(came, bit, 0))

    def joined(a, a_came, b, b_came):
        totals = [
            sum(v.astype(f32) for v in (*terms, held(came))).astype(bf16)
            for terms, came in ((a, a_came), (b, b_came))
        ]
        return row_major(jnp.concatenate(totals, axis=-1))

    far_1 = hidden_layer(far, grad_far, weights_1)
    far_part, far_sent = hidden_back(far_0, far_1)
    far_came = swap(far_sent)
    near_1 = hidden_layer(near, grad_near, weights_1)
    both_1 = lambda index: (near_1[index], far_1[index])
    r0a_x, r0a = pass_on(r0a, r0a_y, X)
    r0b_y, r0b = pass_on(r0b, r0b_x, Y)
    far_sum = far_part + held(far_came).astype(f32)
    grad_z = send(swap_halves(far_sum.astype(bf16)), T)
    r1a, r1a_sent = bundle_grads(both_1(1), both_1(0), 1, False)
    r1a_y = send(r1a_sent, Y)
    r1b, r1b_sent = bundle_grads(both_1(2), both_1(0), 1, True)
    r1b_x = send(r1b_sent, X)
    near_part, near_sent = hidden_back(near_0, near_1)
    near_came = swap(near_sent)

    r0 = joined(r0a, r0a_x, r0b, r0b_y)
    for bit in rest[:0:-1]:
        r0 = fold(r0, bit)()
    r0 = fold(r0, rest[0], f32)

    grad_normed_mlp = near_part + held(near_came).astype(f32) + held(grad_z).astype(f32)
    grad_gain_two, grad_norm_two = norm_back(grad_normed_mlp, unit_two, scale_two, gain_two)
    grad_residual = grad_branch_own.astype(f32) + grad_norm_two
    grad_att_own = grad_residual.astype(bf16)
    grad_att_other = swap(grad_att_own)
    far_branch, far_branch_sent = branch_back(far_0, far_1)
    far_branch_came = swap(far_branch_sent)
    r1a_x, r1a = pass_on(r1a, r1a_y, X)
    r1b_y, r1b = pass_on(r1b, r1b_x, Y)
    grad_attended = pick_first(core == 0, grad_att_own, held(grad_att_other), 0)
    grad_out_a = weight_grad(grad_attended, mixed_a)
    roa_y = send(row_major(part(grad_out_a, Y, 1)), Y)
    grad_out_b = weight_grad(grad_attended, mixed_b)
    rob_x = send(row_major(part(grad_out_b, X, 1)), X)
    branch_sum = far_branch + held(far_branch_came).astype(f32)
    branch_z = send(swap_halves(branch_sum.astype(bf16)), T)
    d_query_a, d_key_a, d_value_a = attend_backward(
        queries_a, keys_a, values_a, matmul(held(grad_attended), oa).astype(bf16), *tables, totals_a
    )
    did(d_query_a)
    r0 = r0()
    r0_t = send(row_major(part(r0, T, 1).astype(bf16)), T)
    r1 = joined(r1a, r1a_x, r1b, r1b_y)
    for bit in rest[:0:-1]:
        r1 = fold(r1, bit)()
    r1 = fold(r1, rest[0], f32)
    d_query_b, d_key_b, d_value_b = attend_backward(
        queries_b, keys_b, values_b, matmul(held(grad_attended), ob).astype(bf16), *tables, totals_b
    )
    did(d_query_b)
    out_a, out_b = part(grad_out_a, Y, 0), part(grad_out_b, X, 0)
    roa_x, out_a = pass_on(out_a, roa_y, X)
    rob_y, out_b = pass_on(out_b, rob_x, Y)
    low = jnp.arange(kv_width) < HEAD_DIM
    d_qkv = jnp.concatenate(
        [
            d_query_a, d_query_b,
            jnp.where(low, d_key_a, d_key_b), jnp.where(low, d_value_a, d_value_b),
        ],
        axis=1,
    )
    grad_qkv = weight_grad(normed, d_qkv)
    qkv_a, qkv_b = columns(grad_qkv, 0, cut), columns(grad_qkv, cut, 2 * cut)
    rqa_y = send(row_major(part(qkv_a, Y, 1)), Y)
    rqb_x = send(row_major(part(qkv_b, X, 1)), X)
    out = fold(joined(out_a, roa_x, out_b, rob_y), T)
    d_came = swap(contract_cols(rows_of(held(d_qkv), 1 - core), query_w).astype(bf16))
    r1 = r1()
    r1_t = send(row_major(part(r1, T, 1).astype(bf16)), T)
    rqa_x, qkv_a = pass_on(part(qkv_a, Y, 0), rqa_y, X)
    rqb_y, qkv_b = pass_on(part(qkv_b, X, 0), rqb_x, Y)
    grad_normed = contract_cols(rows_of(held(d_qkv), core), query_w) + held(d_came).astype(f32)
    grad_gain_one, grad_norm_one = norm_back(grad_normed, unit_one, scale_one, gain_one)
    grad_rows = did(grad_residual + grad_norm_one)
    grad_gains = jnp.stack([grad_gain_one, grad_gain_two])
    gains_came = swap(grad_gains)
    out = out()
    for bit in rest[:0:-1]:
        out = fold(out, bit)()
    out = fold(out, rest[0], f32)
    near_branch, near_branch_sent = branch_back(near_0, near_1)
    near_branch_came = swap(near_branch_sent)
    r1_t = held(r1_t)
    grad_gains = grad_gains + held(gains_came)
    gain_blocks = grad_gains.reshape(2, lax.axis_size("dp"), -1).transpose(1, 0, 2)
    gain_blocks = gain_blocks.reshape((2,) * nbits() + gain_blocks.shape[1:])

    def fold_gains(blocks, bit):
        came = send(part(blocks, bit, 1), bit)
        return lambda: part(blocks, bit, 0) + held(came)

    gain_blocks = fold_gains(gain_blocks, Y)
    grad_rows = did(from_relative(held(grad_rows))[0])
    sum_qkv = fold(joined(qkv_a, rqa_x, qkv_b, rqb_y), T)
    gain_blocks = fold_gains(gain_blocks(), X)
    branch = near_branch + held(near_branch_came).astype(f32) + held(branch_z).astype(f32)
    output = jnp.where(own_valid, residual + branch, 0.0).astype(bf16)
    output = did(from_relative(output)[0])
    sum_gate, sum_up, sum_down = unpack_columns(
        chunks, flat(part(r0, T, 0)), flat(part(r1, T, 0)), flat(r0_t), held(flat(r1_t))
    )
    did(sum_gate)
    gain_blocks = fold_gains(gain_blocks(), T)
    for bit in rest[:0:-1]:
        sum_qkv = fold(sum_qkv(), bit)
        gain_blocks = fold_gains(gain_blocks(), bit)
    sum_qkv = fold(sum_qkv(), rest[0], f32)
    gain_blocks = fold_gains(gain_blocks(), rest[0])
    out = out()
    sum_qkv = flat(sum_qkv())
    gain_sums = gain_blocks().reshape(2, -1)
    return (
        output,
        grad_rows,
        gain_sums[0],
        sum_qkv[:, :heads_width],
        sum_qkv[:, heads_width : heads_width + kv_width],
        sum_qkv[:, heads_width + kv_width :],
        flat(out).T,
        gain_sums[1],
        sum_gate,
        sum_up,
        sum_down,
    )


def solution(mesh):
    placed = (
        P(("dp", "tensor"), None),
        P(("dp", "tensor"), None),
        P("dp", None),
        P("dp"),
        P("dp", "tensor"),
        P("dp", "tensor"),
        P("dp", "tensor"),
        P("tensor", "dp"),
        P("dp"),
        P("dp", "tensor"),
        P("dp", "tensor"),
        P("tensor", "dp"),
    )
    return jax.shard_map(
        body,
        mesh=mesh,
        in_specs=placed,
        out_specs=(
            P(("dp", "tensor"), None),
            P(("dp", "tensor"), None),
            P("dp"),
            P("dp", "tensor"),
            P("dp", "tensor"),
            P("dp", "tensor"),
            P("tensor", "dp"),
            P("dp"),
            P("dp", "tensor"),
            P("dp", "tensor"),
            P("tensor", "dp"),
        ),
        check_vma=False,
    )
```

```python
import functools

import jax
import jax.numpy as jnp
from jax import lax
from jax.experimental import pallas as pl
from jax.experimental.layout import Layout, with_layout_constraint
from jax.experimental.pallas import tpu as pltpu
from jax.sharding import PartitionSpec as P

HEAD_DIM = 64
BLOCK = 128
LANES = 128

norm_epsilon = 1e-05
rope_base = 10000.0
masked_score = -1e30

bf16 = jnp.bfloat16
f32 = jnp.float32

X, Y, T, Z = 0, 1, 2, 3


def nbits():
    return lax.axis_size("dp").bit_length() - 1


def block_axes():
    return [T] + list(range(nbits() - 1, Z - 1, -1)) + [Y, X]


def rest_bits():
    return list(range(Z, nbits()))


def exchange(values, bit):
    size = lax.axis_size("dp")
    return lax.ppermute(values, "dp", [(i, i ^ (1 << bit)) for i in range(size)])


def core_exchange(values):
    return lax.ppermute(values, "tensor", [(0, 1), (1, 0)])


def as_block(values):
    return values.reshape((1,) * nbits() + values.shape)


def after(values, *others):
    return lax.optimization_barrier((values,) + others)[0] if others else values


def row_major(values):
    return with_layout_constraint(values, Layout(major_to_minor=tuple(range(values.ndim))))


def join(values, came, bit):
    return jnp.concatenate([values, came], axis=block_axes().index(bit))


def part(values, bit, index):
    return lax.slice_in_dim(values, index, index + 1, axis=block_axes().index(bit))


def columns(values, low, high):
    return lax.slice_in_dim(values, low, high, axis=values.ndim - 1)


def add(kept, came, kind=bf16):
    return row_major((kept.astype(f32) + came.astype(f32)).astype(kind))


def flat(blocks):
    return blocks.reshape(-1, blocks.shape[-1])


def as_blocks(rows):
    return rows.reshape((2,) * nbits() + (rows.shape[0] // lax.axis_size("dp"), rows.shape[1]))


def block_mask(place):
    axes = block_axes()
    mask = 0
    for level, bit in enumerate(axes):
        mask |= ((place >> (len(axes) - 1 - level)) & 1) << bit
    return mask


def block_place(mask):
    axes = block_axes()
    place = 0
    for level, bit in enumerate(axes):
        place = place + (((mask >> bit) & 1) << (len(axes) - 1 - level))
    return place


def reorder_kernel(count, offsets, *refs):
    half = len(refs) // 2
    for source, target in zip(refs[:half], refs[half:]):
        for place in range(count):
            start = pl.multiple_of(offsets[place], LANES)
            target[:, place * LANES : (place + 1) * LANES] = source[:, pl.ds(start, LANES)]


def reorder(arrays, places):
    count = len(places)
    rows, columns = arrays[0].shape
    width = columns // count
    if width % LANES:
        return [
            jnp.concatenate(
                [lax.dynamic_slice_in_dim(v, p * width, width, 1) for p in places], axis=1
            )
            for v in arrays
        ]
    spec = pl.BlockSpec((BLOCK, columns), lambda i, offsets: (i, 0))
    return pl.pallas_call(
        functools.partial(reorder_kernel, count),
        grid_spec=pltpu.PrefetchScalarGridSpec(
            num_scalar_prefetch=1,
            grid=(rows // BLOCK,),
            in_specs=[spec] * len(arrays),
            out_specs=[spec] * len(arrays),
        ),
        out_shape=[jax.ShapeDtypeStruct(v.shape, v.dtype) for v in arrays],
        compiler_params=pltpu.CompilerParams(vmem_limit_bytes=32 * 1024 * 1024),
        cost_estimate=no_cost(),
        name="reorder",
    )(jnp.stack(places).astype(jnp.int32) * width, *arrays)


def to_relative(*arrays):
    me = lax.axis_index("dp")
    return reorder(arrays, [me ^ block_mask(place) for place in range(lax.axis_size("dp"))])


def from_relative(*arrays):
    me = lax.axis_index("dp")
    return reorder(arrays, [block_place(me ^ index) for index in range(lax.axis_size("dp"))])


def swap_halves(values):
    half = values.shape[1] // 2
    return jnp.concatenate([values[:, half:], values[:, :half]], axis=1)


def pick_first(flag, first, second, axis):
    return jnp.concatenate(
        [jnp.where(flag, first, second), jnp.where(flag, second, first)], axis=axis
    )


def build_layout(lengths, total_rows):
    block_counts = (lengths + BLOCK - 1) // BLOCK
    seq_ends = jnp.cumsum(block_counts, dtype=jnp.int32) * BLOCK
    seq_starts = seq_ends - block_counts * BLOCK
    row_ids = jnp.arange(total_rows, dtype=jnp.int32)
    membership = (
        (row_ids[:, None] >= seq_starts[None, :]) & (row_ids[:, None] < seq_ends[None, :])
    ).astype(jnp.int32)
    slot_ids = jnp.arange(lengths.shape[0], dtype=jnp.int32)
    segment = jnp.sum(membership * (slot_ids[None, :] + 1), axis=1, dtype=jnp.int32) - 1
    first_row = jnp.sum(membership * seq_starts[None, :], axis=1, dtype=jnp.int32)
    seq_limit = jnp.sum(membership * lengths[None, :], axis=1, dtype=jnp.int32)
    position = row_ids - first_row
    is_valid = (segment >= 0) & (position < seq_limit)
    allowed = (
        (segment[:, None] == segment[None, :])
        & (segment[:, None] >= 0)
        & (position[:, None] <= position[None, :])
        & is_valid[:, None]
    )
    allowed = allowed | (row_ids[:, None] == row_ids[None, :])
    bias = jnp.where(allowed, 0.0, masked_score).astype(f32)
    return position, is_valid, bias


def rotation_tables(position):
    half_dim = HEAD_DIM // 2
    lane = jnp.arange(LANES, dtype=jnp.int32)
    frequency = rope_base ** (-2.0 * (lane % half_dim).astype(f32) / HEAD_DIM)
    angles = position.astype(f32)[:, None] * frequency[None, :]
    sign = jnp.where(lane % HEAD_DIM < half_dim, -1.0, 1.0).astype(f32)
    return jnp.cos(angles), jnp.sin(angles) * sign[None, :]


def matmul(left, right):
    return jnp.dot(left, right, preferred_element_type=f32)


def contract_rows(left, right):
    return lax.dot_general(left, right, (((0,), (0,)), ((), ())), preferred_element_type=f32)


def contract_cols(left, right):
    return lax.dot_general(left, right, (((1,), (1,)), ((), ())), preferred_element_type=f32)


def rms_scale(values):
    return lax.rsqrt(jnp.mean(values * values, axis=-1, keepdims=True) + norm_epsilon)


def norm_back(grad_normed, unit_rows, row_scale, gain):
    scaled = grad_normed * gain
    grad_gain = jnp.sum(grad_normed * unit_rows, axis=0)
    grad_rows = row_scale * (
        scaled - unit_rows * jnp.mean(scaled * unit_rows, axis=-1, keepdims=True)
    )
    return grad_gain, grad_rows


def turn(values, cosine, sine):
    lane = lax.broadcasted_iota(jnp.int32, values.shape, 1)
    half_dim = HEAD_DIM // 2
    partner = jnp.where(
        lane % HEAD_DIM < half_dim,
        pltpu.roll(values, LANES - half_dim, 1),
        pltpu.roll(values, half_dim, 1),
    )
    return values * cosine + partner * sine


def doubled(values, second):
    lane = lax.broadcasted_iota(jnp.int32, values.shape, 1)
    rolled = pltpu.roll(values, HEAD_DIM, 1)
    low = lane < HEAD_DIM
    return jnp.where(second, jnp.where(low, rolled, values), jnp.where(low, values, rolled))


def split_heads(pair):
    lane = lax.broadcasted_iota(jnp.int32, pair.shape, 1)
    zero = jnp.zeros_like(pair)
    return jnp.concatenate(
        [jnp.where(lane < HEAD_DIM, pair, zero), jnp.where(lane < HEAD_DIM, zero, pair)], axis=0
    )


def join_heads(wide):
    row = lax.broadcasted_iota(jnp.int32, (LANES, BLOCK), 0)
    return jnp.where(row < HEAD_DIM, wide[:, :BLOCK], wide[:, BLOCK:]).T


def forward_kernel(
    second, q_ref, k_ref, v_ref, bias_ref, cos_ref, sin_ref,
    out_ref, turned_ref, keys_ref, values_ref, total_ref, v2t,
):
    rows = q_ref.shape[0]
    cosine, sine = cos_ref[...], sin_ref[...]

    @pl.when(pl.program_id(0) == 0)
    def _():
        keys = turn(k_ref[...], cosine, sine).astype(bf16).astype(f32)
        keys_ref[...] = doubled(keys, second).astype(bf16)
        values = doubled(v_ref[...], second)
        values_ref[...] = values.astype(bf16)
        v2t[...] = values.T.astype(bf16)

    turned_ref[...] = (turn(q_ref[...], cosine, sine) * HEAD_DIM ** (-0.5)).astype(bf16)
    for index in range(rows // BLOCK):
        span = (index + 1) * BLOCK
        here = slice(index * BLOCK, span)
        queries = split_heads(turned_ref[here, :])
        scores = lax.dot_general(
            keys_ref[:span, :], queries, (((1,), (1,)), ((), ())), preferred_element_type=f32
        )
        bias = bias_ref[:span, here]
        scores = scores + jnp.concatenate([bias, bias], axis=1)
        top = jnp.max(scores, axis=0, keepdims=True)
        weights = jnp.exp(scores - top)
        total = jnp.sum(weights, axis=0, keepdims=True)
        weights = (weights * (1.0 / total)).astype(bf16)
        mixed = jnp.dot(v2t[:, :span], weights, preferred_element_type=f32)
        out_ref[here, :] = join_heads(mixed).astype(bf16)
        total_ref[:, 2 * index * BLOCK : 2 * span] = top + jnp.log(total)


def backward_kernel(
    q_ref, k_ref, v_ref, grad_ref, bias_ref, cos_ref, sin_ref, total_ref,
    dq_ref, dk_ref, dv_ref, k2t, dk_sum, dv_sum,
):
    pair = pl.program_id(0)
    rows = q_ref.shape[0]
    cosine, sine = cos_ref[...], sin_ref[...]

    @pl.when(pair == 0)
    def _():
        k2t[...] = k_ref[...].astype(f32).T.astype(bf16)
        dk_sum[...] = jnp.zeros_like(dk_sum)
        dv_sum[...] = jnp.zeros_like(dv_sum)

    for index in range(rows // BLOCK):
        span = (index + 1) * BLOCK
        here = slice(index * BLOCK, span)
        queries = split_heads(q_ref[here, :])
        grads = split_heads(grad_ref[here, :])
        scores = lax.dot_general(
            k_ref[:span, :], queries, (((1,), (1,)), ((), ())), preferred_element_type=f32
        )
        bias = bias_ref[:span, here]
        scores = scores + jnp.concatenate([bias, bias], axis=1)
        probs = jnp.exp(scores - total_ref[:, 2 * index * BLOCK : 2 * span])
        grad_prob = lax.dot_general(
            v_ref[:span, :], grads, (((1,), (1,)), ((), ())), preferred_element_type=f32
        )
        center = jnp.sum(probs * grad_prob, axis=0, keepdims=True)
        grad_score = (probs * (grad_prob - center)).astype(bf16)
        dv_sum[:span, :] += jnp.dot(probs.astype(bf16), grads, preferred_element_type=f32)
        dk_sum[:span, :] += jnp.dot(grad_score, queries, preferred_element_type=f32)
        wide = jnp.dot(k2t[:, :span], grad_score, preferred_element_type=f32)
        grad_query = join_heads(wide) * HEAD_DIM ** (-0.5)
        dq_ref[here, :] = turn(grad_query, cosine[here, :], -sine[here, :]).astype(bf16)

    @pl.when(pair == pl.num_programs(0) - 1)
    def _():
        keys = dk_sum[...] + pltpu.roll(dk_sum[...], HEAD_DIM, 1)
        dk_ref[...] = turn(keys, cosine, -sine).astype(bf16)
        dv_ref[...] = (dv_sum[...] + pltpu.roll(dv_sum[...], HEAD_DIM, 1)).astype(bf16)


def attend_forward(raw, heads_width, group, bias, cosine, sine):
    rows = raw.shape[0]
    pairs = heads_width // LANES
    own = pairs // 2
    whole = lambda shape: pl.BlockSpec(shape, lambda i: (0, 0))
    column = pl.BlockSpec((rows, LANES), lambda i: (0, i))
    wide = jax.ShapeDtypeStruct((rows, own * LANES), bf16)
    narrow = jax.ShapeDtypeStruct((rows, LANES), bf16)
    return pl.pallas_call(
        functools.partial(forward_kernel, group == 1),
        grid=(own,),
        in_specs=[
            pl.BlockSpec((rows, LANES), lambda i: (0, group * own + i)),
            pl.BlockSpec((rows, LANES), lambda i: (0, pairs)),
            pl.BlockSpec((rows, LANES), lambda i: (0, pairs + 1)),
            whole((rows, rows)),
            whole((rows, LANES)),
            whole((rows, LANES)),
        ],
        out_specs=[
            column,
            column,
            whole((rows, LANES)),
            whole((rows, LANES)),
            pl.BlockSpec((None, 1, 2 * rows), lambda i: (i, 0, 0)),
        ],
        out_shape=[wide, wide, narrow, narrow, jax.ShapeDtypeStruct((own, 1, 2 * rows), f32)],
        scratch_shapes=[pltpu.VMEM((LANES, rows), bf16)],
        compiler_params=pltpu.CompilerParams(vmem_limit_bytes=40 * 1024 * 1024),
        cost_estimate=no_cost(),
        name="attend_forward",
    )(raw, raw, raw, bias, cosine, sine)


def attend_backward(queries, keys, values, grads, bias, cosine, sine, totals):
    rows, width = queries.shape
    whole = lambda shape: pl.BlockSpec(shape, lambda i: (0, 0))
    column = pl.BlockSpec((rows, LANES), lambda i: (0, i))
    narrow = jax.ShapeDtypeStruct((rows, LANES), bf16)
    return pl.pallas_call(
        backward_kernel,
        grid=(width // LANES,),
        in_specs=[
            column,
            whole((rows, LANES)),
            whole((rows, LANES)),
            column,
            whole((rows, rows)),
            whole((rows, LANES)),
            whole((rows, LANES)),
            pl.BlockSpec((None, 1, 2 * rows), lambda i: (i, 0, 0)),
        ],
        out_specs=[column, whole((rows, LANES)), whole((rows, LANES))],
        out_shape=[jax.ShapeDtypeStruct((rows, width), bf16), narrow, narrow],
        scratch_shapes=[
            pltpu.VMEM((LANES, rows), bf16),
            pltpu.VMEM((rows, LANES), f32),
            pltpu.VMEM((rows, LANES), f32),
        ],
        compiler_params=pltpu.CompilerParams(vmem_limit_bytes=40 * 1024 * 1024),
        cost_estimate=no_cost(),
        name="attend_backward",
    )(queries, keys, values, grads, bias, cosine, sine, totals)


def no_cost(hint=1):
    return pl.CostEstimate(flops=hint * 1000000, bytes_accessed=1000000, transcendentals=0)


def whole_block(shape):
    return pl.BlockSpec(shape, lambda i: (0,) * len(shape))


def stack_kernel(*refs):
    out, turned = refs[-2:]
    for index, ref in enumerate(refs[:-2]):

        @pl.when(pl.program_id(0) == index)
        def _():
            value = ref[...]
            out[...] = value
            turned[...] = value.T


def stack_rows(*pieces):
    rows, width = pieces[0].shape
    count = len(pieces)
    kind = pieces[0].dtype
    return pl.pallas_call(
        stack_kernel,
        grid=(count,),
        in_specs=[whole_block((rows, width))] * count,
        out_specs=[
            pl.BlockSpec((rows, width), lambda i: (i, 0)),
            pl.BlockSpec((width, rows), lambda i: (0, i)),
        ],
        out_shape=[
            jax.ShapeDtypeStruct((count * rows, width), kind),
            jax.ShapeDtypeStruct((width, count * rows), kind),
        ],
        compiler_params=pltpu.CompilerParams(vmem_limit_bytes=40 * 1024 * 1024),
        cost_estimate=no_cost(),
        name="stack_rows",
    )(*pieces)


def join_kernel(block, first_a, came_a, first_b, came_b, gate, up, down_a, down_b):
    def whole(first, came, size):
        shape = (-1, size, first.shape[1])
        both = jnp.concatenate([first[...].reshape(shape), came[...].reshape(shape)], axis=1)
        return both.reshape(-1, first.shape[1])

    width = gate.shape[1]
    both_a = whole(first_a, came_a, 2 * block)
    gate[...] = both_a[:, :width]
    down_a[...] = both_a[:, width:]
    both_b = whole(first_b, came_b, block)
    up[...] = both_b[:, :width]
    down_b[...] = both_b[:, width:]


def join_weights(first_a, came_a, first_b, came_b, width):
    high = 512
    arrays = [flat(v) for v in (first_a, came_a, first_b, came_b)]
    depth = 2 * arrays[0].shape[0]
    widths = (width, width, arrays[0].shape[1] - width, arrays[2].shape[1] - width)
    return pl.pallas_call(
        functools.partial(join_kernel, depth // lax.axis_size("dp")),
        grid=(depth // high,),
        in_specs=[pl.BlockSpec((high // 2, v.shape[1]), lambda i: (i, 0)) for v in arrays],
        out_specs=[pl.BlockSpec((high, w), lambda i: (i, 0)) for w in widths],
        out_shape=[jax.ShapeDtypeStruct((depth, w), bf16) for w in widths],
        compiler_params=pltpu.CompilerParams(vmem_limit_bytes=40 * 1024 * 1024),
        cost_estimate=no_cost(20000),
        name="join_weights",
    )(*arrays)


def hidden_kernel(
    rows_ref, grads_ref, gate_ref, up_ref, down_a, down_b, hidden_out, gate_out, up_out
):
    rows, grads = rows_ref[...], grads_ref[...]
    at = down_a.shape[1]
    for down, where in ((down_a, slice(0, at)), (down_b, slice(at, at + down_b.shape[1]))):
        gate = jnp.dot(rows, gate_ref[:, where], preferred_element_type=f32)
        up = jnp.dot(rows, up_ref[:, where], preferred_element_type=f32)
        grad = jnp.dot(grads, down[...], preferred_element_type=f32)
        sigmoid = 1.0 / (1.0 + jnp.exp(-gate))
        silu = gate * sigmoid
        hidden_out[:, where] = (silu * up).astype(bf16)
        gate_out[:, where] = (grad * up * sigmoid * (1.0 + gate * (1.0 - sigmoid))).astype(bf16)
        up_out[:, where] = (grad * silu).astype(bf16)


def hidden_rows(rows, grads, gate, up, down_a, down_b, height):
    total, depth = rows.shape
    width = gate.shape[1]
    tall = pl.BlockSpec((height, depth), lambda i: (i, 0))
    tile = pl.BlockSpec((height, width), lambda i: (i, 0))
    return pl.pallas_call(
        hidden_kernel,
        grid=(total // height,),
        in_specs=[tall, tall] + [whole_block(v.shape) for v in (gate, up, down_a, down_b)],
        out_specs=[tile] * 3,
        out_shape=[jax.ShapeDtypeStruct((total, width), bf16)] * 3,
        compiler_params=pltpu.CompilerParams(vmem_limit_bytes=48 * 1024 * 1024),
        cost_estimate=no_cost(),
        name="hidden_rows",
    )(rows, grads, gate, up, down_a, down_b)


def weight_grad_kernel(
    inner, turned_near, turned_far, near_ref, far_ref,
    grads_near, grads_far, hidden_near, hidden_far, kept, sent,
):
    def product(*pairs):
        return sum(jnp.dot(l[...], r[...], preferred_element_type=f32) for l, r in pairs)

    both = jnp.concatenate(
        [
            product((turned_near, near_ref), (turned_far, far_ref)),
            product((grads_near, hidden_near), (grads_far, hidden_far)),
        ],
        axis=1,
    ).astype(bf16)
    block = kept.shape[-2] * (1 if inner else 2)
    both = both.reshape(-1, 2, block, both.shape[-1])
    kept[...] = both[:, 0].reshape(kept.shape)
    sent[...] = both[:, 1].reshape(sent.shape)


def weight_grads(turned, lefts, grads_turned, hiddens, inner):
    depth, total = turned[0].shape
    block = depth // lax.axis_size("dp")
    high = 512
    count = high // (2 * block)
    width = lefts[0].shape[1] + hiddens[0].shape[1]
    out = pl.BlockSpec((count, block, width), lambda i: (i, 0, 0))
    shape = jax.ShapeDtypeStruct((depth // (2 * block), block, width), bf16)
    tall = pl.BlockSpec((high, total), lambda i: (i, 0))
    kept, sent = pl.pallas_call(
        functools.partial(weight_grad_kernel, inner),
        grid=(depth // high,),
        in_specs=[tall, tall]
        + [whole_block(v.shape) for v in lefts]
        + [tall, tall]
        + [whole_block(v.shape) for v in hiddens],
        out_specs=[out, out],
        out_shape=[shape, shape],
        compiler_params=pltpu.CompilerParams(vmem_limit_bytes=48 * 1024 * 1024),
        cost_estimate=no_cost(),
        name="weight_grads",
    )(*turned, *lefts, *grads_turned, *hiddens)
    dims = [2] * nbits()
    dims[block_axes().index(X if inner else Y)] = 1
    return kept.reshape(*dims, block, width), sent.reshape(*dims, block, width)


def back_kernel(cuts, *refs):
    count = len(cuts)
    weights, (own, other) = refs[len(refs) - 2 - count : len(refs) - 2], refs[-2:]
    lefts = refs[: len(refs) - 2 - count]
    total = 0.0
    for (index, low, high), weight in zip(cuts, weights):
        total += lax.dot_general(
            lefts[index][:, low:high],
            weight[...],
            (((1,), (1,)), ((), ())),
            preferred_element_type=f32,
        )
    half = own.shape[0]
    own[...] = total[:half]
    other[...] = total[half:].astype(bf16)


def back_rows(lefts, weights, cuts):
    rows = lefts[0].shape[0]
    depth = weights[0].shape[0]
    high = 512
    return pl.pallas_call(
        functools.partial(back_kernel, cuts),
        grid=(depth // high,),
        in_specs=[whole_block(v.shape) for v in lefts]
        + [pl.BlockSpec((high, v.shape[1]), lambda i: (i, 0)) for v in weights],
        out_specs=[pl.BlockSpec((rows // 2, high), lambda i: (0, i))] * 2,
        out_shape=[
            jax.ShapeDtypeStruct((rows // 2, depth), f32),
            jax.ShapeDtypeStruct((rows // 2, depth), bf16),
        ],
        compiler_params=pltpu.CompilerParams(vmem_limit_bytes=48 * 1024 * 1024),
        cost_estimate=no_cost(),
        name="back_rows",
    )(*lefts, *weights)


def my_half():
    return (lax.axis_index("dp") >> T) & 1


class Chunks:
    def __init__(self, quarter):
        self.quarter = quarter
        middle = -(-quarter // (2 * LANES)) * LANES
        self.spans = ((0, middle), (middle, quarter))
        self.cuts = [low + (high - low) // (2 * LANES) * LANES for low, high in self.spans]

    def layout(self, index):
        (low, high), at = self.spans[index], self.cuts[index]
        width = high - low
        return (
            (0, low, high, 0),
            (2, low, at, width),
            (1, low, high, width + at - low),
            (2, at, high, 2 * width + at - low),
        )

    def width(self, index):
        low, high = self.spans[index]
        return 3 * (high - low)

    def turn(self, index):
        (low, high), at = self.spans[index], self.cuts[index]
        return high - low + at - low


def pack_kernel(chunks, t_ref, gate_ref, up_ref, down_ref, *outs):
    for side in (0, 1):
        start = jnp.where(side == 0, t_ref[0], 1 - t_ref[0]) * chunks.quarter
        for index in (0, 1):
            out = outs[2 * side + index]
            for matrix, low, high, place in chunks.layout(index):
                where = pl.ds(pl.multiple_of(start + low, LANES), high - low)
                if matrix == 2:
                    value = down_ref[where, :].astype(f32).T.astype(bf16)
                else:
                    value = (gate_ref, up_ref)[matrix][:, where]
                out[:, place : place + high - low] = value


def pack_columns(chunks, gate, up, down):
    rows = gate.shape[0]
    if rows % LANES:
        sides = []
        for side in (0, 1):
            start = jnp.where(side == 0, my_half(), 1 - my_half()) * chunks.quarter
            halves = [
                lax.dynamic_slice_in_dim(v, start, chunks.quarter, 1) for v in (gate, up, down.T)
            ]
            for index in (0, 1):
                parts = sorted(chunks.layout(index), key=lambda entry: entry[3])
                sides.append(jnp.concatenate([halves[m][:, l:h] for m, l, h, _ in parts], axis=1))
        return sides
    whole = pl.BlockSpec(memory_space=pltpu.VMEM)
    shapes = [jax.ShapeDtypeStruct((rows, chunks.width(i)), bf16) for i in (0, 1)]
    return pl.pallas_call(
        functools.partial(pack_kernel, chunks),
        in_specs=[pl.BlockSpec(memory_space=pltpu.SMEM), whole, whole, whole],
        out_specs=[whole] * 4,
        out_shape=shapes + shapes,
        compiler_params=pltpu.CompilerParams(vmem_limit_bytes=40 * 1024 * 1024),
        cost_estimate=no_cost(),
        name="pack_columns",
    )(my_half().reshape(1).astype(jnp.int32), gate, up, down)


def unpack_kernel(chunks, t_ref, *refs):
    outs = refs[4:]
    for side in (0, 1):
        start = jnp.where(side == 0, t_ref[0], 1 - t_ref[0]) * chunks.quarter
        for index in (0, 1):
            for matrix, low, high, place in chunks.layout(index):
                where = pl.ds(pl.multiple_of(start + low, LANES), high - low)
                value = refs[2 * side + index][:, place : place + high - low].astype(f32)
                if matrix == 2:
                    outs[2][where, :] = value.T
                else:
                    outs[matrix][:, where] = value


def unpack_columns(chunks, *bundles):
    rows = bundles[0].shape[0]
    if rows % LANES:
        halves = []
        for side in (0, 1):
            found = [[], [], []]
            for index in (0, 1):
                for matrix, low, high, place in chunks.layout(index):
                    value = bundles[2 * side + index][:, place : place + high - low].astype(f32)
                    found[matrix].append((low, value))
            halves.append(
                [jnp.concatenate([v for _, v in sorted(f, key=lambda e: e[0])], axis=1) for f in found]
            )
        gate, up, down = [
            pick_first(my_half() == 0, own, came, 1) for own, came in zip(*halves)
        ]
        return gate, up, down.T
    whole = pl.BlockSpec(memory_space=pltpu.VMEM)
    flat_shape = jax.ShapeDtypeStruct((rows, 2 * chunks.quarter), f32)
    return pl.pallas_call(
        functools.partial(unpack_kernel, chunks),
        in_specs=[pl.BlockSpec(memory_space=pltpu.SMEM)] + [whole] * 4,
        out_specs=[whole] * 3,
        out_shape=[flat_shape, flat_shape, jax.ShapeDtypeStruct((2 * chunks.quarter, rows), f32)],
        compiler_params=pltpu.CompilerParams(vmem_limit_bytes=40 * 1024 * 1024),
        cost_estimate=no_cost(),
        name="unpack_columns",
    )(my_half().reshape(1).astype(jnp.int32), *bundles)


def body(
    inputs, cotangent, seq_lengths, attn_gain, w_query, w_key, w_value, w_out,
    mlp_gain, w_gate, w_up, w_down,
):
    own_rows = inputs.shape[0]
    chip_rows = 2 * own_rows
    core = lax.axis_index("tensor")
    rest = rest_bits()
    heads_width = w_query.shape[1]
    kv_width = w_key.shape[1]
    cut = (heads_width + 2 * kv_width) // 2
    cut_out = heads_width // 2

    last = []

    def held(values, *others):
        values = after(values, *last, *others)
        last[:] = [values]
        return values

    def did(values):
        last[:] = [values]
        return values

    def send(values, bit, *others):
        return exchange(held(values, *others), bit)

    def swap(values, *others):
        return core_exchange(held(values, *others))

    def gather(values, bit, *others):
        came = send(values, bit, *others)
        return lambda: join(values, held(came), bit)

    def fold(values, bit, kind=bf16):
        came = send(row_major(part(values, bit, 1).astype(bf16)), bit)
        return lambda: add(part(values, bit, 0), held(came), kind)

    gains = as_block(jnp.stack([attn_gain, mlp_gain]))
    gains = gather(gains, rest[0])
    qkv = jnp.concatenate([w_query, w_key, w_value], axis=1)
    q = gather(as_block(qkv), rest[0])
    for bit in rest[1:] + [T]:
        gains = gather(gains(), bit)
    inputs_rel, cotangent_rel = to_relative(held(inputs), cotangent)
    did(inputs_rel)
    gains = gather(gains(), X)
    out_t = did(held(w_out.T))
    gains = gather(gains(), Y)
    o = gather(as_block(out_t), rest[0])
    for bit in rest[1:] + [T]:
        q = gather(q(), bit)
    chunks = Chunks(w_gate.shape[1] // 2)
    own_0, own_1, other_0, other_1 = pack_columns(chunks, held(w_gate), w_up, w_down)
    did(own_0)
    gains = flat(gains()).reshape(-1, 2, attn_gain.shape[0]).transpose(1, 0, 2)
    gains = gains.reshape(2, -1).astype(f32)
    gain_one, gain_two = gains[0], gains[1]
    inputs_wide = inputs_rel.astype(f32)
    scale_one = rms_scale(inputs_wide)
    unit_one = inputs_wide * scale_one
    normed_own = (unit_one * gain_one).astype(bf16)
    normed_other = swap(normed_own)
    for bit in rest[1:] + [T]:
        o = gather(o(), bit)
    position, is_valid, bias = build_layout(seq_lengths[0], chip_rows)
    cosine, sine = rotation_tables(position)
    own_valid = lax.dynamic_slice_in_dim(is_valid, core * own_rows, own_rows, 0)[:, None]
    grad_branch_own = jnp.where(own_valid, cotangent_rel, jnp.zeros_like(cotangent_rel))
    q = q()
    qa = gather(columns(q, 0, cut), X)
    qb = gather(columns(q, cut, 2 * cut), Y)
    w0_t = send(as_block(other_0), T)
    bias = did(held(bias))
    grad_branch_other = swap(grad_branch_own)
    qa = gather(qa(), Y)
    qb = gather(qb(), X)
    w0 = join(as_block(own_0), held(w0_t), T)
    w0 = gather(w0, rest[0])
    for bit in rest[1:]:
        w0 = gather(w0(), bit)
    grad_far_own = send(swap_halves(grad_branch_own), T)
    qa, qb = qa(), qb()
    o = o()
    oa = gather(columns(o, 0, cut_out), X)
    ob = gather(columns(o, cut_out, heads_width), Y)
    query_w = jnp.concatenate([flat(qa), flat(qb)], axis=1)

    normed = pick_first(core == 0, normed_own, normed_other, 0)
    raw = did(matmul(held(normed), query_w))
    tables = (bias, cosine, sine)
    mixed_a, queries_a, keys_a, values_a, totals_a = attend_forward(raw, heads_width, 0, *tables)
    did(mixed_a)
    oa = gather(oa(), Y)
    ob = gather(ob(), X)
    w0 = w0()
    w1_t = send(as_block(other_1), T)
    mixed_b, queries_b, keys_b, values_b, totals_b = attend_forward(
        held(raw), heads_width, 1, *tables
    )
    did(mixed_b)
    grad_far_other = swap(grad_far_own)
    oa, ob = flat(oa()), flat(ob())
    w0b = gather(columns(w0, chunks.turn(0), w0.shape[-1]), Y)
    w0a = gather(columns(w0, 0, chunks.turn(0)), X)
    w1 = join(as_block(own_1), held(w1_t), T)
    w1 = gather(w1, rest[0])

    def rows_of(values, which):
        return lax.dynamic_slice_in_dim(values, which * own_rows, own_rows, 0)

    def project(which, mixed_a):
        return contract_cols(rows_of(mixed_a, which), oa) + contract_cols(
            rows_of(mixed_b, which), ob
        )

    came = swap(project(1 - core, held(mixed_a)).astype(bf16))
    projected = did(project(core, held(mixed_a)))
    w0b, w0a = w0b(), w0a()
    w0b_x = send(w0b, X)
    w0a_y = send(w0a, Y)
    residual = did(inputs_wide + (projected + held(came).astype(f32)))

    scale_two = rms_scale(residual)
    unit_two = residual * scale_two
    normed_mlp_own = (unit_two * gain_two).astype(bf16)
    far_own = send(swap_halves(normed_mlp_own), T)
    near_other = swap(normed_mlp_own)
    grad_near, grad_near_turned = stack_rows(held(grad_branch_own), grad_branch_other)
    did(grad_near)
    grad_far, grad_far_turned = stack_rows(grad_far_own, held(grad_far_other))
    did(grad_far)
    for bit in rest[1:]:
        w1 = gather(w1(), bit)
    w1 = w1()

    def weights_of(first_a, came_a, first_b, came_b, index):
        width = chunks.width(index) // 3
        return join_weights(first_a, came_a, first_b, held(came_b), width)

    def hidden_layer(rows, grads, weights):
        hidden, grad_gate, grad_up = hidden_rows(held(rows), grads, *weights, own_rows)
        return did(hidden), grad_gate, grad_up

    def weight_grad(left, right):
        return did(as_blocks(contract_rows(left, held(right)).astype(bf16)))

    def bundle_grads(grads, hiddens, index, inner):
        width = chunks.width(index) // 3
        at = chunks.turn(index) - width
        low, high = (at, width) if inner else (0, at)
        kept, sent = weight_grads(
            (near_turned, far_turned), (held(grads[0]), grads[1]),
            (grad_near_turned, grad_far_turned), [v[:, low:high] for v in hiddens], inner,
        )
        did(sent)
        return kept, sent

    weights_0 = weights_of(w0a, held(w0a_y), w0b, w0b_x, 0)
    w1a = gather(columns(w1, 0, chunks.turn(1)), X)
    w1b = gather(columns(w1, chunks.turn(1), w1.shape[-1]), Y)
    far_other = swap(far_own)
    near, near_turned = stack_rows(normed_mlp_own, held(near_other))
    did(near)
    near_0 = hidden_layer(near, grad_near, weights_0)
    far, far_turned = stack_rows(far_own, held(far_other))
    did(far)
    w1a, w1b = w1a(), w1b()
    w1a_y = send(w1a, Y)
    w1b_x = send(w1b, X)
    far_0 = hidden_layer(far, grad_far, weights_0)
    both = lambda index: (near_0[index], far_0[index])
    r0a, r0a_sent = bundle_grads(both(1), both(0), 0, False)
    r0a_y = send(r0a_sent, Y)
    r0b, r0b_sent = bundle_grads(both(2), both(0), 0, True)
    r0b_x = send(r0b_sent, X)
    w1a_y, w1b_x = held(w1a_y), held(w1b_x)
    weights_1 = weights_of(w1a, w1a_y, w1b, w1b_x, 1)
    weights_hidden = [*weights_0[:2], *weights_1[:2]]
    weights_down = [*weights_0[2:], *weights_1[2:]]
    cuts_hidden = tuple((i, 0, v.shape[1]) for i, v in enumerate(weights_hidden))
    cuts_down = tuple(
        (i, low, high)
        for i in (0, 1)
        for low, high in (
            (0, weights_down[2 * i].shape[1]),
            (weights_down[2 * i].shape[1], weights_hidden[2 * i].shape[1]),
        )
    )

    def hidden_back(first, second):
        lefts = [held(first[1]), first[2], second[1], second[2]]
        own, other = back_rows(lefts, weights_hidden, cuts_hidden)
        return did(own), other

    def branch_back(first, second):
        own, other = back_rows([held(first[0]), second[0]], weights_down, cuts_down)
        return did(own), other

    def pass_on(kept, came, bit):
        came = held(came)
        sent = add(part(kept, bit, 1), part(came, bit, 1))
        return send(sent, bit), (part(kept, bit, 0), part(came, bit, 0))

    def joined(a, a_came, b, b_came):
        totals = [
            sum(v.astype(f32) for v in (*terms, held(came))).astype(bf16)
            for terms, came in ((a, a_came), (b, b_came))
        ]
        return row_major(jnp.concatenate(totals, axis=-1))

    far_1 = hidden_layer(far, grad_far, weights_1)
    far_part, far_sent = hidden_back(far_0, far_1)
    far_came = swap(far_sent)
    near_1 = hidden_layer(near, grad_near, weights_1)
    both_1 = lambda index: (near_1[index], far_1[index])
    r0a_x, r0a = pass_on(r0a, r0a_y, X)
    r0b_y, r0b = pass_on(r0b, r0b_x, Y)
    far_sum = far_part + held(far_came).astype(f32)
    grad_z = send(swap_halves(far_sum.astype(bf16)), T)
    r1a, r1a_sent = bundle_grads(both_1(1), both_1(0), 1, False)
    r1a_y = send(r1a_sent, Y)
    r1b, r1b_sent = bundle_grads(both_1(2), both_1(0), 1, True)
    r1b_x = send(r1b_sent, X)
    near_part, near_sent = hidden_back(near_0, near_1)
    near_came = swap(near_sent)

    r0 = joined(r0a, r0a_x, r0b, r0b_y)
    for bit in rest[:0:-1]:
        r0 = fold(r0, bit)()
    r0 = fold(r0, rest[0], f32)

    grad_normed_mlp = near_part + held(near_came).astype(f32) + held(grad_z).astype(f32)
    grad_gain_two, grad_norm_two = norm_back(grad_normed_mlp, unit_two, scale_two, gain_two)
    grad_residual = grad_branch_own.astype(f32) + grad_norm_two
    grad_att_own = grad_residual.astype(bf16)
    grad_att_other = swap(grad_att_own)
    far_branch, far_branch_sent = branch_back(far_0, far_1)
    far_branch_came = swap(far_branch_sent)
    r1a_x, r1a = pass_on(r1a, r1a_y, X)
    r1b_y, r1b = pass_on(r1b, r1b_x, Y)
    grad_attended = pick_first(core == 0, grad_att_own, held(grad_att_other), 0)
    grad_out_a = weight_grad(grad_attended, mixed_a)
    roa_y = send(row_major(part(grad_out_a, Y, 1)), Y)
    grad_out_b = weight_grad(grad_attended, mixed_b)
    rob_x = send(row_major(part(grad_out_b, X, 1)), X)
    branch_sum = far_branch + held(far_branch_came).astype(f32)
    branch_z = send(swap_halves(branch_sum.astype(bf16)), T)
    d_query_a, d_key_a, d_value_a = attend_backward(
        queries_a, keys_a, values_a, matmul(held(grad_attended), oa).astype(bf16), *tables, totals_a
    )
    did(d_query_a)
    r1 = joined(r1a, r1a_x, r1b, r1b_y)
    for bit in rest[:0:-1]:
        r1 = fold(r1, bit)()
    r1 = fold(r1, rest[0], f32)
    d_query_b, d_key_b, d_value_b = attend_backward(
        queries_b, keys_b, values_b, matmul(held(grad_attended), ob).astype(bf16), *tables, totals_b
    )
    did(d_query_b)
    out_a, out_b = part(grad_out_a, Y, 0), part(grad_out_b, X, 0)
    roa_x, out_a = pass_on(out_a, roa_y, X)
    rob_y, out_b = pass_on(out_b, rob_x, Y)
    low = jnp.arange(kv_width) < HEAD_DIM
    d_qkv = jnp.concatenate(
        [
            d_query_a, d_query_b,
            jnp.where(low, d_key_a, d_key_b), jnp.where(low, d_value_a, d_value_b),
        ],
        axis=1,
    )
    grad_qkv = weight_grad(normed, d_qkv)
    qkv_a, qkv_b = columns(grad_qkv, 0, cut), columns(grad_qkv, cut, 2 * cut)
    rqa_y = send(row_major(part(qkv_a, Y, 1)), Y)
    rqb_x = send(row_major(part(qkv_b, X, 1)), X)
    r0 = r0()
    r0_t = send(row_major(part(r0, T, 1).astype(bf16)), T)
    out = fold(joined(out_a, roa_x, out_b, rob_y), T)
    d_came = swap(contract_cols(rows_of(held(d_qkv), 1 - core), query_w).astype(bf16))
    r1 = r1()
    r1_t = send(row_major(part(r1, T, 1).astype(bf16)), T)
    rqa_x, qkv_a = pass_on(part(qkv_a, Y, 0), rqa_y, X)
    rqb_y, qkv_b = pass_on(part(qkv_b, X, 0), rqb_x, Y)
    grad_normed = contract_cols(rows_of(held(d_qkv), core), query_w) + held(d_came).astype(f32)
    grad_gain_one, grad_norm_one = norm_back(grad_normed, unit_one, scale_one, gain_one)
    grad_rows = did(grad_residual + grad_norm_one)
    grad_gains = jnp.stack([grad_gain_one, grad_gain_two])
    gains_came = swap(grad_gains)
    out = out()
    for bit in rest[:0:-1]:
        out = fold(out, bit)()
    out = fold(out, rest[0], f32)
    near_branch, near_branch_sent = branch_back(near_0, near_1)
    near_branch_came = swap(near_branch_sent)
    r1_t = held(r1_t)
    grad_gains = grad_gains + held(gains_came)
    gain_blocks = grad_gains.reshape(2, lax.axis_size("dp"), -1).transpose(1, 0, 2)
    gain_blocks = gain_blocks.reshape((2,) * nbits() + gain_blocks.shape[1:])

    def fold_gains(blocks, bit):
        came = send(part(blocks, bit, 1), bit)
        return lambda: part(blocks, bit, 0) + held(came)

    gain_blocks = fold_gains(gain_blocks, Y)
    grad_rows = did(from_relative(held(grad_rows))[0])
    sum_qkv = fold(joined(qkv_a, rqa_x, qkv_b, rqb_y), T)
    gain_blocks = fold_gains(gain_blocks(), X)
    branch = near_branch + held(near_branch_came).astype(f32) + held(branch_z).astype(f32)
    output = jnp.where(own_valid, residual + branch, 0.0).astype(bf16)
    output = did(from_relative(output)[0])
    sum_gate, sum_up, sum_down = unpack_columns(
        chunks, flat(part(r0, T, 0)), flat(part(r1, T, 0)), flat(r0_t), held(flat(r1_t))
    )
    did(sum_gate)
    gain_blocks = fold_gains(gain_blocks(), T)
    for bit in rest[:0:-1]:
        sum_qkv = fold(sum_qkv(), bit)
        gain_blocks = fold_gains(gain_blocks(), bit)
    sum_qkv = fold(sum_qkv(), rest[0], f32)
    gain_blocks = fold_gains(gain_blocks(), rest[0])
    out = out()
    sum_qkv = flat(sum_qkv())
    gain_sums = gain_blocks().reshape(2, -1)
    return (
        output,
        grad_rows,
        gain_sums[0],
        sum_qkv[:, :heads_width],
        sum_qkv[:, heads_width : heads_width + kv_width],
        sum_qkv[:, heads_width + kv_width :],
        flat(out).T,
        gain_sums[1],
        sum_gate,
        sum_up,
        sum_down,
    )


def solution(mesh):
    placed = (
        P(("dp", "tensor"), None),
        P(("dp", "tensor"), None),
        P("dp", None),
        P("dp"),
        P("dp", "tensor"),
        P("dp", "tensor"),
        P("dp", "tensor"),
        P("tensor", "dp"),
        P("dp"),
        P("dp", "tensor"),
        P("dp", "tensor"),
        P("tensor", "dp"),
    )
    return jax.shard_map(
        body,
        mesh=mesh,
        in_specs=placed,
        out_specs=(
            P(("dp", "tensor"), None),
            P(("dp", "tensor"), None),
            P("dp"),
            P("dp", "tensor"),
            P("dp", "tensor"),
            P("dp", "tensor"),
            P("tensor", "dp"),
            P("dp"),
            P("dp", "tensor"),
            P("dp", "tensor"),
            P("tensor", "dp"),
        ),
        check_vma=False,
    )
```
